32 devices in a mesh: dp: 8 (over z, x), fsdp: 4 (over y, core).
Axes of the slice: x: 2, y: 2, z: 4, core: 2. Of those that a mesh axis runs over, the one named last changes fastest.
Arguments:
- features: bfloat16 [64, 625, 2048], P(('dp', 'fsdp')), may hold values from -6 to 6
- matches: int32 [64, 100], P(('dp', 'fsdp')), may hold values from -1 to 31, as said below
- target_labels: int32 [64, 32], P(('dp', 'fsdp')), may hold values from 0 to 90
- target_boxes: float32 [64, 32, 4], P(('dp', 'fsdp')), may hold values from 0.15 to 0.6
- square_weight: float32 [14, 256, 256], P(None, ('dp', 'fsdp'))
- square_momentum: float32 [14, 256, 256], P(None, ('dp', 'fsdp')), may hold values from -6.1035156e-05 to 6.1035156e-05
- expand_weight: float32 [2, 256, 2048], P(None, None, ('dp', 'fsdp')), may hold values from -0.375 to 0.375
- expand_momentum: float32 [2, 256, 2048], P(None, None, ('dp', 'fsdp')), may hold values from -6.1035156e-05 to 6.1035156e-05
- reduce_weight: float32 [2, 2048, 256], P(None, ('dp', 'fsdp')), may hold values from -0.125 to 0.125
- reduce_momentum: float32 [2, 2048, 256], P(None, ('dp', 'fsdp')), may hold values from -6.1035156e-05 to 6.1035156e-05
- input_weight: float32 [2048, 256], P(('dp', 'fsdp')), may hold values from -0.125 to 0.125
- input_momentum: float32 [2048, 256], P(('dp', 'fsdp')), may hold values from -6.67572e-06 to 6.67572e-06
- input_second: float32 [2048, 256], P(('dp', 'fsdp')), may hold values from 1.10564674e-13 to 4.422587e-13
- head_weight: float32 [256, 96], P(('dp', 'fsdp')), may hold values from -0.375 to 0.375
- head_momentum: float32 [256, 96], P(('dp', 'fsdp')), may hold values from -6.67572e-06 to 6.67572e-06
- head_second: float32 [256, 96], P(('dp', 'fsdp')), may hold values from 1.10564674e-13 to 4.422587e-13
- query_weight: float32 [2, 100, 256], P(None, None, ('dp', 'fsdp')), may hold values from -6 to 6
- query_momentum: float32 [2, 100, 256], P(None, None, ('dp', 'fsdp')), may hold values from -1.1920929e-07 to 1.1920929e-07
- query_second: float32 [2, 100, 256], P(None, None, ('dp', 'fsdp')), may hold values from 1.3820584e-16 to 5.5282336e-16
- norm_weight: float32 [12, 256], P(None, ('dp', 'fsdp'))
- norm_momentum: float32 [12, 256], P(None, ('dp', 'fsdp')), may hold values from -3.0517578e-05 to 3.0517578e-05
- norm_second: float32 [12, 256], P(None, ('dp', 'fsdp')), may hold values from 1.7690348e-12 to 7.076139e-12
Outputs:
- square_next: float32 [14, 256, 256], P(None, ('dp', 'fsdp'))
- square_momentum_next: float32 [14, 256, 256], P(None, ('dp', 'fsdp'))
- square_copy: bfloat16 [14, 256, 256], P(None, ('dp', 'fsdp'))
- expand_next: float32 [2, 256, 2048], P(None, None, ('dp', 'fsdp'))
- expand_momentum_next: float32 [2, 256, 2048], P(None, None, ('dp', 'fsdp'))
- expand_copy: bfloat16 [2, 256, 2048], P(None, None, ('dp', 'fsdp'))
- reduce_next: float32 [2, 2048, 256], P(None, ('dp', 'fsdp'))
- reduce_momentum_next: float32 [2, 2048, 256], P(None, ('dp', 'fsdp'))
- reduce_copy: bfloat16 [2, 2048, 256], P(None, ('dp', 'fsdp'))
- input_next: float32 [2048, 256], P(('dp', 'fsdp'))
- input_momentum_next: float32 [2048, 256], P(('dp', 'fsdp'))
- input_second_next: float32 [2048, 256], P(('dp', 'fsdp'))
- input_copy: bfloat16 [2048, 256], P(('dp', 'fsdp'))
- head_next: float32 [256, 96], P(('dp', 'fsdp'))
- head_momentum_next: float32 [256, 96], P(('dp', 'fsdp'))
- head_second_next: float32 [256, 96], P(('dp', 'fsdp'))
- head_copy: bfloat16 [256, 96], P(('dp', 'fsdp'))
- query_next: float32 [2, 100, 256], P(None, None, ('dp', 'fsdp'))
- query_momentum_next: float32 [2, 100, 256], P(None, None, ('dp', 'fsdp'))
- query_second_next: float32 [2, 100, 256], P(None, None, ('dp', 'fsdp'))
- query_copy: bfloat16 [2, 100, 256], P(None, None, ('dp', 'fsdp'))
- norm_next: float32 [12, 256], P(None, ('dp', 'fsdp'))
- norm_momentum_next: float32 [12, 256], P(None, ('dp', 'fsdp'))
- norm_second_next: float32 [12, 256], P(None, ('dp', 'fsdp'))
- norm_copy: bfloat16 [12, 256], P(None, ('dp', 'fsdp'))
- loss_value: float32 [], replicated
- box_total: float32 [], replicated
- gradient_norm: float32 [], replicated
The draws below stay inside these ranges and needn't reach their ends.
Inputs may be any that keep to these rules, and one draw needn't show every extreme that they name: `matches`: in each image the matched queries name targets 0 to k - 1, each exactly once, for some k of 1 to 32; the other queries hold -1. The last image has k = 32.
All inputs are finite; a program needn't handle non-finite values.
Results may differ from the reference program's by a relative error of at most 0.017.
Values may be sent and summed in bfloat16 or wider, within the bound.
No kernel may reach another device: no remote copies, remote signals or barrier semaphores. Data moves between devices by JAX's collectives and lax.ppermute only.
A program may use at most 256 MiB of HBM per device.

```python
import math
import jax
import jax.numpy as jnp
from jax import lax

D = 256
HEADS = 8
FF = 2048
C_IN = 2048
Q = 100
NCLS = 92
SIDE = 25
NT = 32
STEP = 10
HW = 625
IMAGES = 64
HEADW = 96
PARAMS = 3617792


def draw_matches(key, part):
    key = jax.random.fold_in(key, 11)
    first_key, second_key = jax.random.split(key, 2)
    images = jnp.arange(IMAGES)
    ceiling = jnp.maximum(1, NT * (IMAGES + 2 * images) // (3 * IMAGES))
    jitter = jax.random.randint(first_key, (IMAGES,), 0, 1 + ceiling // 4)
    targets = jnp.maximum(1, ceiling - jitter)
    targets = jnp.where(images == IMAGES - 1, NT, targets)
    orders = jax.vmap(lambda single: jax.random.permutation(single, Q))(jax.random.split(second_key, IMAGES))
    slots = jnp.arange(Q)[None, :]
    values = jnp.where(slots < targets[:, None], slots, -1).astype(jnp.int32)
    rows = jnp.arange(IMAGES)[:, None]
    return jnp.zeros((IMAGES, Q), jnp.int32).at[rows, orders].set(values)


def draw_square_weight(key, part):
    key = jax.random.fold_in(key, 3)
    base = jax.random.normal(key, (14, D, D), jnp.float32)
    index = jnp.arange(14)
    output_rows = (index % 4 == 3) & (index < 12)
    scale = jnp.where(output_rows, 6.0, 1.0) / math.sqrt(D)
    return base * scale[:, None, None]


def draw_norm_weight(key, part):
    key = jax.random.fold_in(key, 5)
    first_key, second_key = jax.random.split(key, 2)
    columns = jnp.arange(D).astype(jnp.float32) / D
    rising = 0.6 + 1.2 * columns
    gains = rising[None, :] * jax.random.uniform(first_key, (6, D), jnp.float32, 0.8, 1.25)
    shifts = 0.3 * jax.random.normal(second_key, (6, D), jnp.float32)
    return jnp.concatenate([gains, shifts], axis=0)


def set_ends(drawn, key, least, top_value):
    longest = drawn.shape.index(max(drawn.shape))
    spots = []
    for shift in (0, 1):
        where = [jax.random.randint(jax.random.fold_in(key, axis), (), 0, length) for axis, length in enumerate(drawn.shape)]
        where[longest] = (where[longest] + shift) % drawn.shape[longest]
        spots.append(tuple(where))
    return drawn.at[spots[0]].set(least).at[spots[1]].set(top_value)


def block_scale(own_key, extent, shards, least, high):
    def one(axis_at, shards_of):
        draws = jax.random.uniform(jax.random.fold_in(jax.random.fold_in(own_key, 6), axis_at), (shards_of,), jnp.float32, least / len(shards), high / len(shards))
        return jnp.repeat(jnp.exp(draws), extent[axis_at] // shards_of).reshape((-1,) + (1,) * (len(extent) - axis_at - 1))

    level = one(*shards[0])
    for cut in shards[1:]:
        level = level * one(*cut)
    return level


def gaussian(stream_key, shape, deviation, most, pieces=(), kind=jnp.bfloat16):
    drawn = jax.random.normal(stream_key, shape, jnp.float32) * deviation
    if len(pieces) > 0:
        drawn = block_scale(stream_key, shape, pieces, -0.22, 0.18) * drawn
    return jnp.clip(drawn, min=-most, max=most).astype(kind)


def setup_inputs(seed: int = 0) -> dict:
    seeds = jax.random.split(jax.random.key(seed), 23)
    return {
        "features": gaussian(seeds[0], (IMAGES, HW, C_IN), 1.0, 6.0, ((0, 32),)),
        "matches": draw_matches(jax.random.fold_in(seeds[22], 71), 0),
        "target_labels": set_ends(jax.random.randint(seeds[2], (IMAGES, NT), 0, NCLS - 1), jax.random.fold_in(seeds[2], 1), 0, (NCLS - 1) - 1).astype(jnp.int32),
        "target_boxes": jnp.clip(0.15 + 0.45000002 * jax.random.uniform(seeds[3], (IMAGES, NT, 4), jnp.float32) ** block_scale(seeds[3], (IMAGES, NT, 4), ((0, 32),), -0.2, 0.2), 0.15, 0.6),
        "square_weight": draw_square_weight(jax.random.fold_in(seeds[22], 71), 0),
        "square_momentum": gaussian(seeds[5], (14, D, D), (0.02 / PARAMS ** 0.5), 6.103515625e-05, ((1, 32),), jnp.float32),
        "expand_weight": gaussian(seeds[6], (2, D, FF), D ** -0.5, 0.375, ((2, 32),), jnp.float32),
        "expand_momentum": gaussian(seeds[7], (2, D, FF), (0.02 / PARAMS ** 0.5), 6.103515625e-05, ((2, 32),), jnp.float32),
        "reduce_weight": gaussian(seeds[8], (2, FF, D), FF ** -0.5, 0.125, ((1, 32),), jnp.float32),
        "reduce_momentum": gaussian(seeds[9], (2, FF, D), (0.02 / PARAMS ** 0.5), 6.103515625e-05, ((1, 32),), jnp.float32),
        "input_weight": gaussian(seeds[10], (C_IN, D), C_IN ** -0.5, 0.125, ((0, 32),), jnp.float32),
        "input_momentum": gaussian(seeds[11], (C_IN, D), (0.0022 / PARAMS ** 0.5), 6.67572021484375e-06, ((0, 32),), jnp.float32),
        "input_second": jnp.clip(jnp.exp(math.log(4.422586971121467e-13) - 1.3862944 * jax.random.uniform(seeds[12], (C_IN, D), jnp.float32) ** block_scale(seeds[12], (C_IN, D), ((0, 32),), -0.2, 0.2)), 1.1056467427803668e-13, 4.422586971121467e-13),
        "head_weight": gaussian(seeds[13], (D, HEADW), D ** -0.5, 0.375, ((0, 32),), jnp.float32),
        "head_momentum": gaussian(seeds[14], (D, HEADW), (0.0022 / PARAMS ** 0.5), 6.67572021484375e-06, ((0, 32),), jnp.float32),
        "head_second": jnp.clip(jnp.exp(math.log(4.422586971121467e-13) - 1.3862944 * jax.random.uniform(seeds[15], (D, HEADW), jnp.float32) ** block_scale(seeds[15], (D, HEADW), ((0, 32),), -0.2, 0.2)), 1.1056467427803668e-13, 4.422586971121467e-13),
        "query_weight": gaussian(seeds[16], (2, Q, D), 1.0, 6.0, ((2, 32),), jnp.float32),
        "query_momentum": gaussian(seeds[17], (2, Q, D), (0.00004 / PARAMS ** 0.5), 1.1920928955078125e-07, ((2, 32),), jnp.float32),
        "query_second": jnp.clip(jnp.exp(math.log(5.528233586846892e-16) - 1.3862944 * jax.random.uniform(seeds[18], (2, Q, D), jnp.float32) ** block_scale(seeds[18], (2, Q, D), ((2, 32),), -0.2, 0.2)), 1.382058396711723e-16, 5.528233586846892e-16),
        "norm_weight": draw_norm_weight(jax.random.fold_in(seeds[22], 71), 0),
        "norm_momentum": gaussian(seeds[20], (12, D), (0.009 / PARAMS ** 0.5), 3.0517578125e-05, ((1, 32),), jnp.float32),
        "norm_second": jnp.clip(jnp.exp(math.log(7.0761391537943474e-12) - 1.3862944 * jax.random.uniform(seeds[21], (12, D), jnp.float32) ** block_scale(seeds[21], (12, D), ((1, 32),), -0.2, 0.2)), 1.7690347884485869e-12, 7.0761391537943474e-12),
    }


HIGH = lax.Precision.HIGHEST
NS_A = 3.4445
NS_B = -4.775
NS_C = 2.0315
CLIP = 0.02
BETA_M = 0.95
LR_M = 0.3
DECAY_M = 0.01
ADAM_B1 = 0.9
ADAM_B2 = 0.999
SOFT = 0.02
SOFT_L1 = 0.05
NO_OBJECT = 0.1

@jax.custom_vjp
def low(v):
    return lax.optimization_barrier(v.astype(jnp.bfloat16)).astype(jnp.float32)

@jax.custom_vjp
def low_back(v):
    return v

def low_keep(v):
    return (low(v), None)

def low_pass(kept, grad):
    return (grad,)

def back_keep(v):
    return (v, None)

def back_low(kept, grad):
    return (low(grad),)
low.defvjp(low_keep, low_pass)
low_back.defvjp(back_keep, back_low)

def rounded(value):
    return low_back(low(value))

def matmul(left, right):
    return jnp.dot(left, right, precision=HIGH)

def layer_norm(hidden, gain, shift):
    center = hidden - lax.optimization_barrier(jnp.mean(hidden, axis=-1, keepdims=True))
    spread = lax.optimization_barrier(jnp.mean(center * center, axis=-1, keepdims=True))
    return center * lax.rsqrt(spread + 1e-05) * gain + shift

def attend(source_q, source_k, source_v, weights):
    width = weights.shape[-1]
    depth = width // HEADS
    queries = rounded(matmul(source_q, weights[0])).reshape(-1, HEADS, depth)
    keys = rounded(matmul(source_k, weights[1])).reshape(-1, HEADS, depth)
    values = rounded(matmul(source_v, weights[2])).reshape(-1, HEADS, depth)
    scores = jnp.einsum('qhd,khd->hqk', queries, keys, precision=HIGH) / math.sqrt(depth)
    probs = low(jax.nn.softmax(scores, axis=-1))
    mixed = low(jnp.einsum('hqk,khd->qhd', probs, values, precision=HIGH).reshape(-1, width))
    return matmul(mixed, weights[3])

def feed_forward(hidden, first_mat, second_mat):
    return matmul(rounded(jax.nn.gelu(matmul(low(hidden), first_mat))), second_mat)

def sine_table(width):
    cells = jnp.arange(SIDE * SIDE)
    ypos = (cells // SIDE + 1).astype(jnp.float32) / (SIDE + 1e-06) * (2.0 * math.pi)
    xpos = (cells % SIDE + 1).astype(jnp.float32) / (SIDE + 1e-06) * (2.0 * math.pi)
    half = width // 2
    index = jnp.arange(half)
    freqs = 10000.0 ** ((2 * (index // 2)).astype(jnp.float32) / half)

    def embed(coord):
        angle = coord[:, None] / freqs[None, :]
        return jnp.where(index[None, :] % 2 == 0, jnp.sin(angle), jnp.cos(angle))
    return jnp.concatenate([embed(ypos), embed(xpos)], axis=1)

def soft_max(first, second):
    return SOFT * jnp.logaddexp(first / SOFT, second / SOFT)

def soft_min(first, second):
    return -soft_max(-first, -second)

def corners(boxes):
    return (boxes[:, 0] - boxes[:, 2] / 2, boxes[:, 1] - boxes[:, 3] / 2, boxes[:, 0] + boxes[:, 2] / 2, boxes[:, 1] + boxes[:, 3] / 2)

def generalized_iou(first, second):
    left_one, top_one, right_one, bottom_one = corners(first)
    left_two, top_two, right_two, bottom_two = corners(second)
    inter_w = SOFT * jax.nn.softplus((soft_min(right_one, right_two) - soft_max(left_one, left_two)) / SOFT)
    inter_h = SOFT * jax.nn.softplus((soft_min(bottom_one, bottom_two) - soft_max(top_one, top_two)) / SOFT)
    inter = inter_w * inter_h
    union = first[:, 2] * first[:, 3] + second[:, 2] * second[:, 3] - inter
    hull = (soft_max(right_one, right_two) - soft_min(left_one, left_two)) * (soft_max(bottom_one, bottom_two) - soft_min(top_one, top_two))
    return inter / union - (hull - union) / hull

def image_loss(lows, sine_rows, box_count, inverse, feats, matched_to, labels, targets):
    square, expand, shrink, project, head, query, gains = lows
    memory = matmul(feats.astype(jnp.float32), project)
    keyed = low(memory + sine_rows)
    memory = layer_norm(memory + attend(keyed, keyed, low(memory), square[0:4]), gains[0], gains[6])
    memory = layer_norm(memory + feed_forward(memory, expand[0], shrink[0]), gains[1], gains[7])
    content, place = (query[0], query[1])
    asked = low(content + place)
    content = layer_norm(content + attend(asked, asked, low(content), square[4:8]), gains[2], gains[8])
    content = layer_norm(content + attend(low(content + place), low(memory + sine_rows), low(memory), square[8:12]), gains[3], gains[9])
    content = layer_norm(content + feed_forward(content, expand[1], shrink[1]), gains[4], gains[10])
    output = low(layer_norm(content, gains[5], gains[11]))
    classes_n = head.shape[1] - 4
    logits = matmul(output, head[:, :classes_n])
    boxed = low(jax.nn.gelu(matmul(output, square[12])))
    boxed = low(jax.nn.gelu(matmul(boxed, square[13])))
    predicted = jax.nn.sigmoid(matmul(boxed, head[:, classes_n:]))
    matched = matched_to >= 0
    picker = matched_to[:, None] == jnp.arange(targets.shape[0])[None, :]
    target_label = jnp.where(matched, lax.optimization_barrier(jnp.sum(jnp.where(picker, labels[None, :], 0), axis=1)), classes_n - 1)
    wanted = jnp.where(matched[:, None], matmul(picker.astype(logits.dtype), targets.astype(logits.dtype)), 0.5)
    chosen = lax.optimization_barrier(jnp.sum(jnp.where(jnp.arange(classes_n)[None, :] == target_label[:, None], logits, 0.0), axis=1))
    cross_entropy = jax.nn.logsumexp(logits, axis=1) - chosen
    weighting = jnp.where(matched, 1.0, NO_OBJECT)
    ce_sum = jnp.sum(weighting * cross_entropy)
    matched_mask = matched.astype(logits.dtype)
    offset = (predicted - wanted) / SOFT_L1
    l1_sum = jnp.sum(matched_mask[:, None] * SOFT_L1 * (jnp.sqrt(offset * offset + 1.0) - 1.0))
    correlation = generalized_iou(predicted, wanted)
    giou_sum = jnp.sum(matched_mask * (1.0 - correlation))
    return ce_sum * inverse + (5.0 * l1_sum + 2.0 * giou_sum) / box_count

def batch_loss(masters, features, matches, labels, boxes, box_count, inverse):
    lows = tuple((low(weight) for weight in masters))
    sine_rows = sine_table(masters[0].shape[-1])
    checked = jax.checkpoint(image_loss)

    def scan_body(running, image_items):
        return (running + checked(lows, sine_rows, box_count, inverse, *image_items), None)
    running, unused = lax.scan(scan_body, jnp.zeros((), jnp.float32), (features, matches, labels, boxes))
    return running

def orthogonal(matrix):
    wide = matrix.shape[0] <= matrix.shape[1]
    current = matrix if wide else matrix.T
    current = current / (jnp.sqrt(jnp.sum(current * current)) + 1e-07)
    for sweep in range(5):
        gram = jnp.dot(current, current.T, precision=HIGH)
        poly = NS_B * gram + NS_C * jnp.dot(gram, gram, precision=HIGH)
        current = NS_A * current + jnp.dot(poly, current, precision=HIGH)
    return current if wide else current.T

def muon_apply(weight, ortho, longest):
    return weight * (1.0 - LR_M * DECAY_M) - LR_M * 0.2 * math.sqrt(longest) * ortho

def adam(weight, first, second, gradient, rate, decay):
    first = ADAM_B1 * first + (1.0 - ADAM_B1) * gradient
    second = ADAM_B2 * second + (1.0 - ADAM_B2) * gradient * gradient
    fixed_first = first / (1.0 - ADAM_B1 ** STEP)
    fixed_second = second / (1.0 - ADAM_B2 ** STEP)
    weight = weight * (1.0 - rate * decay) - rate * fixed_first / (jnp.sqrt(fixed_second) + 1e-08)
    return (weight, first, second, weight.astype(jnp.bfloat16))

def reference(features, matches, target_labels, target_boxes, square_weight, square_momentum, expand_weight, expand_momentum, reduce_weight, reduce_momentum, input_weight, input_momentum, input_second, head_weight, head_momentum, head_second, query_weight, query_momentum, query_second, norm_weight, norm_momentum, norm_second):
    masters = (square_weight, expand_weight, reduce_weight, input_weight, head_weight, query_weight, norm_weight)
    box_total = jnp.sum((matches >= 0).astype(jnp.float32))
    inverse = 1.0 / (IMAGES * Q)

    def whole_loss(values):
        return batch_loss(values, features, matches, target_labels, target_boxes, box_total, inverse)
    loss_value, pullback = jax.vjp(whole_loss, masters)
    gradients = pullback(jnp.ones((), loss_value.dtype))[0]
    squares = sum((jnp.sum(piece * piece) for piece in gradients))
    gradient_norm = jnp.sqrt(squares)
    factor = jnp.minimum(1.0, CLIP / (gradient_norm + 1e-06))
    clipped = tuple((piece * factor for piece in gradients))
    square_mom = BETA_M * square_momentum + clipped[0]
    expand_mom = BETA_M * expand_momentum + clipped[1]
    reduce_mom = BETA_M * reduce_momentum + clipped[2]
    square_next = muon_apply(square_weight, jax.vmap(orthogonal)(square_mom), D)
    expand_next = muon_apply(expand_weight, jax.vmap(orthogonal)(expand_mom), FF)
    reduce_next = muon_apply(reduce_weight, jax.vmap(orthogonal)(reduce_mom), FF)
    input_out = adam(input_weight, input_momentum, input_second, clipped[3], 0.04, 0.0001)
    head_out = adam(head_weight, head_momentum, head_second, clipped[4], 0.1, 0.0001)
    query_out = adam(query_weight, query_momentum, query_second, clipped[5], 0.5, 0.0)
    norm_out = adam(norm_weight, norm_momentum, norm_second, clipped[6], 0.5, 0.0)
    return (square_next, square_mom, square_next.astype(jnp.bfloat16), expand_next, expand_mom, expand_next.astype(jnp.bfloat16), reduce_next, reduce_mom, reduce_next.astype(jnp.bfloat16), input_out[0], input_out[1], input_out[2], input_out[3], head_out[0], head_out[1], head_out[2], head_out[3], query_out[0], query_out[1], query_out[2], query_out[3], norm_out[0], norm_out[1], norm_out[2], norm_out[3], loss_value, box_total, gradient_norm)
```

```python
import functools
import math

import jax
import jax.numpy as jnp
import numpy as np
from jax import lax
from jax.experimental import pallas as pl
from jax.experimental.pallas import tpu as pltpu
from jax.sharding import PartitionSpec as P

HEADS = 8
SIDE = 25
STEP = 10
NS_A = 3.4445
NS_B = -4.775
NS_C = 2.0315
CLIP = 0.02
BETA_M = 0.95
LR_M = 0.3
DECAY_M = 0.01
ADAM_B1 = 0.9
ADAM_B2 = 0.999
SOFT = 0.02
SOFT_L1 = 0.05
NO_OBJECT = 0.1
EPS = 1e-05
LOG2E = math.log2(math.e)
F32 = jnp.float32
BF16 = jnp.bfloat16
VMEM_LIMIT = 56 * 1024 * 1024


def nn(left, right):
    return lax.dot_general(left, right, (((1,), (0,)), ((), ())), preferred_element_type=F32)


def nt(left, right):
    return lax.dot_general(left, right, (((1,), (1,)), ((), ())), preferred_element_type=F32)


def tn(left, right):
    return lax.dot_general(left, right, (((0,), (0,)), ((), ())), preferred_element_type=F32)


def head_mask(width, head):
    lane = lax.broadcasted_iota(jnp.int32, (1, width), 1)
    depth = width // HEADS
    return jnp.logical_and(lane >= head * depth, lane < (head + 1) * depth).astype(F32).astype(BF16)


def norm_parts(total):
    center = total - jnp.mean(total, axis=-1, keepdims=True)
    spread = jnp.mean(center * center, axis=-1, keepdims=True)
    scale = lax.rsqrt(spread + EPS)
    return center * scale, scale


def norm_back(grad, unit, scale, gain):
    inner = grad * gain
    mean_inner = jnp.mean(inner, axis=-1, keepdims=True)
    mean_cross = jnp.mean(inner * unit, axis=-1, keepdims=True)
    return scale * (inner - mean_inner - unit * mean_cross)


def column_sum(value):
    return jnp.sum(value, axis=0, keepdims=True)


GELU_C = math.sqrt(2.0 / math.pi)
GELU_K = 0.044715 * GELU_C


def gelu_parts(value):
    square = value * value
    half = 0.5 + 0.5 * jnp.tanh(value * (GELU_C + GELU_K * square))
    out = value * half
    slope = half + out * (1.0 - half) * (2.0 * GELU_C + 6.0 * GELU_K * square)
    return out, slope


def masked_softmax(scores, depth, length):
    padded = scores.shape[1]
    start = (padded - 1) // 128 * 128
    if length < padded:
        lane = lax.broadcasted_iota(jnp.int32, (1, padded - start), 1)
        tail = jnp.where(lane < length - start, scores[:, start:], -1e30)
        scores = tail if start == 0 else jnp.concatenate([scores[:, :start], tail], axis=1)
    factor = LOG2E / math.sqrt(depth)
    top = jnp.max(scores, axis=1, keepdims=True)
    powers = jnp.exp2((scores - top) * factor)
    inverse = 1.0 / jnp.sum(powers, axis=1, keepdims=True)
    return (powers * inverse).astype(BF16)


def encode_kernel(tokens, f_ref, win_ref, w_ref, sine_ref, norm_ref,
                  p_ref, keyed_ref, lowm_ref, q_ref, k_ref, v_ref, o_ref, s0_ref, x1_ref):
    head = pl.program_id(1)
    width = win_ref.shape[1]

    @pl.when(head == 0)
    def _():
        padded = s0_ref.shape[1]
        s0_ref[0, tokens // 8 * 8:padded, :] = jnp.zeros((padded - tokens // 8 * 8, width), F32)
        s0_ref[0, 0:tokens, :] = nn(f_ref[0], win_ref[...])
        memory = s0_ref[0]
        keyed = (memory + sine_ref[...]).astype(BF16)
        lowm = memory.astype(BF16)
        keyed_ref[0] = keyed
        lowm_ref[0] = lowm
        q_ref[0] = nn(keyed, w_ref[0]).astype(BF16)
        k_ref[0] = nn(keyed, w_ref[1]).astype(BF16)
        v_ref[0] = nn(lowm, w_ref[2]).astype(BF16)
        o_ref[...] = jnp.zeros_like(o_ref)

    mask = head_mask(width, head)
    scores = nt(q_ref[0] * mask, k_ref[0])
    probs = masked_softmax(scores, width // HEADS, tokens)
    p_ref[0, 0] = probs
    o_ref[0] += nn(probs, v_ref[0] * mask)

    @pl.when(head == HEADS - 1)
    def _():
        total = s0_ref[0] + nn(o_ref[0].astype(BF16), w_ref[3])
        s0_ref[0] = total
        unit, scale = norm_parts(total)
        x1_ref[0] = unit * norm_ref[0:1, :] + norm_ref[6:7, :]


def encode(features, win, square, sine, norm):
    images, tokens, depth = features.shape
    width = win.shape[1]
    padded = sine.shape[0]
    per_image = lambda kind: jax.ShapeDtypeStruct((images, padded, width), kind)
    image_block = pl.BlockSpec((1, padded, width), lambda i, h: (i, 0, 0))
    whole = lambda shape: pl.BlockSpec(shape, lambda i, h: (0,) * len(shape))
    return pl.pallas_call(
        functools.partial(encode_kernel, tokens),
        grid=(images, HEADS),
        in_specs=[
            pl.BlockSpec((1, tokens, depth), lambda i, h: (i, 0, 0)),
            whole(win.shape), whole(square.shape), whole(sine.shape), whole(norm.shape),
        ],
        out_specs=[pl.BlockSpec((1, 1, padded, padded), lambda i, h: (i, h, 0, 0))] + [image_block] * 8,
        out_shape=[jax.ShapeDtypeStruct((images, HEADS, padded, padded), BF16)]
        + [per_image(BF16)] * 5 + [per_image(F32)] * 3,
        compiler_params=pltpu.CompilerParams(vmem_limit_bytes=VMEM_LIMIT),
        name="encode",
    )(features, win, square, sine, norm)


def encode_back_kernel(tokens, dx1_ref, s0_ref, norm_ref, p_ref, keyed_ref, lowm_ref, q_ref, k_ref, v_ref, o_ref,
                       w_ref, f_ref, dsq_ref, dwin_ref, dnorm_ref,
                       ds0, dout, dout_t, q_t, cross, dq, dk_t, dv_t, dsq, dwin):
    image, head = pl.program_id(0), pl.program_id(1)
    images = pl.num_programs(0)
    width = w_ref.shape[1]
    depth = width // HEADS

    @pl.when(jnp.logical_and(image == 0, head == 0))
    def _():
        dsq[...] = jnp.zeros_like(dsq)
        dwin[...] = jnp.zeros_like(dwin)
        dnorm_ref[...] = jnp.zeros_like(dnorm_ref)

    @pl.when(head == 0)
    def _():
        unit, scale = norm_parts(s0_ref[0])
        grad = dx1_ref[0]
        dnorm_ref[0:1, :] += column_sum(grad * unit)
        dnorm_ref[1:2, :] += column_sum(grad)
        dtotal = norm_back(grad, unit, scale, norm_ref[0:1, :])
        ds0[...] = dtotal
        low = dtotal.astype(BF16)
        dsq[3] += tn(o_ref[0].astype(BF16), low)
        dmixed = nt(low, w_ref[3]).astype(BF16)
        dout[...] = dmixed
        dout_t[...] = dmixed.T
        q_t[...] = q_ref[0].T
        cross[...] = dmixed.astype(F32) * o_ref[0]
        dq[...] = jnp.zeros_like(dq)

    mask = head_mask(width, head)
    rows = pl.ds(pl.multiple_of(head * depth, depth), depth)
    weight = jnp.sum(cross[...] * mask.astype(F32), axis=1, keepdims=True)
    probs = p_ref[0, 0]
    dprobs = nt(dout[...] * mask, v_ref[0])
    dscores = (probs.astype(F32) * (dprobs - weight)).astype(BF16)
    dq[...] += nn(dscores, k_ref[0] * mask)
    dk_t[rows, :] = nn(q_t[rows, :], dscores)
    dv_t[rows, :] = nn(dout_t[rows, :], probs)

    @pl.when(head == HEADS - 1)
    def _():
        factor = 1.0 / math.sqrt(depth)
        dqb = (dq[...] * factor).astype(BF16)
        dkb = (dk_t[...] * factor).astype(BF16).T
        dvb = dv_t[...].astype(BF16).T
        dsq[0] += tn(keyed_ref[0], dqb)
        dsq[1] += tn(keyed_ref[0], dkb)
        dsq[2] += tn(lowm_ref[0], dvb)
        dm = ds0[...] + nt(dqb, w_ref[0]) + nt(dkb, w_ref[1]) + nt(dvb, w_ref[2])
        dmb = dm.astype(BF16)
        dwin[...] += tn(dmb[0:tokens], f_ref[0])

        @pl.when(image == images - 1)
        def _():
            dsq_ref[...] = dsq[...].astype(dsq_ref.dtype)
            dwin_ref[...] = dwin[...].astype(BF16).T.astype(dwin_ref.dtype)


def encode_back(dx1, s0, norm, probs, keyed, lowm, q, k, v, o, square, features):
    images, tokens, channels = features.shape
    padded, width = s0.shape[1:]
    image_block = pl.BlockSpec((1, padded, width), lambda i, h: (i, 0, 0))
    whole = lambda shape: pl.BlockSpec(shape, lambda i, h: (0,) * len(shape))
    return pl.pallas_call(
        functools.partial(encode_back_kernel, tokens),
        grid=(images, HEADS),
        in_specs=[
            image_block, image_block, whole(norm.shape),
            pl.BlockSpec((1, 1, padded, padded), lambda i, h: (i, h, 0, 0)),
        ] + [image_block] * 6 + [
            whole(square.shape), pl.BlockSpec((1, tokens, channels), lambda i, h: (i, 0, 0)),
        ],
        out_specs=[whole((4, width, width)), whole((channels, width)), whole((2, width))],
        out_shape=[
            jax.ShapeDtypeStruct((4, width, width), BF16),
            jax.ShapeDtypeStruct((channels, width), BF16),
            jax.ShapeDtypeStruct((2, width), F32),
        ],
        scratch_shapes=[
            pltpu.VMEM((padded, width), F32), pltpu.VMEM((padded, width), BF16),
            pltpu.VMEM((width, padded), BF16), pltpu.VMEM((width, padded), BF16),
            pltpu.VMEM((padded, width), F32), pltpu.VMEM((padded, width), F32),
            pltpu.VMEM((width, padded), F32), pltpu.VMEM((width, padded), F32),
            pltpu.VMEM((4, width, width), F32), pltpu.VMEM((width, channels), F32),
        ],
        compiler_params=pltpu.CompilerParams(vmem_limit_bytes=VMEM_LIMIT),
        name="encode_back",
    )(dx1, s0, norm, probs, keyed, lowm, q, k, v, o, square, features)


def stack_heads(value):
    return jnp.concatenate([value * head_mask(value.shape[1], head) for head in range(HEADS)], axis=0)


def pick_heads(stacked):
    rows, width = stacked.shape[0] // HEADS, stacked.shape[1]
    lane = lax.broadcasted_iota(jnp.int32, (1, width), 1)
    out = stacked[0:rows]
    for head in range(1, HEADS):
        out = jnp.where(lane >= head * (width // HEADS), stacked[head * rows:(head + 1) * rows], out)
    return out


def soft_gap(gap):
    return SOFT * jnp.log(1.0 + jnp.exp(-jnp.abs(gap) * (1.0 / SOFT)))


def sigmoid(value):
    return 1.0 / (1.0 + jnp.exp(-value))


def axis_terms(center, size, target_center, target_size):
    low_one, high_one = center - size / 2, center + size / 2
    low_two, high_two = target_center - target_size / 2, target_center + target_size / 2
    low_gap, high_gap = low_one - low_two, high_one - high_two
    low_soft, high_soft = soft_gap(low_gap), soft_gap(high_gap)
    inner = (jnp.minimum(high_one, high_two) - high_soft) - (jnp.maximum(low_one, low_two) + low_soft)
    overlap = jnp.maximum(inner, 0.0) + soft_gap(inner)
    hull = (jnp.maximum(high_one, high_two) + high_soft) - (jnp.minimum(low_one, low_two) - low_soft)
    return overlap, hull, sigmoid(inner / SOFT), sigmoid(low_gap / SOFT), sigmoid(high_gap / SOFT)


def box_loss(box, target, mask, box_count):
    l1_sum = 0.0
    grads = []
    for one, two in zip(box, target):
        offset = (one - two) / SOFT_L1
        root = jnp.sqrt(offset * offset + 1.0)
        l1_sum = l1_sum + mask * (SOFT_L1 * (root - 1.0))
        grads.append(5.0 * offset / root)
    ow, hw, pw, lw, uw = axis_terms(box[0], box[2], target[0], target[2])
    oh, hh, ph, lh, uh = axis_terms(box[1], box[3], target[1], target[3])
    inter = ow * oh
    union = box[2] * box[3] + target[2] * target[3] - inter
    hull = hw * hh
    by_union, by_hull = 1.0 / union, 1.0 / hull
    giou = inter * by_union - (hull - union) * by_hull
    share = inter * by_union * by_union
    g_inter = by_union + share - by_hull
    g_area = by_hull - share
    g_hull = -union * by_hull * by_hull
    for axis, (other, hull_other, slope, low_s, high_s, size_other) in enumerate(
        ((oh, hh, pw, lw, uw, box[3]), (ow, hw, ph, lh, uh, box[2]))
    ):
        flow = g_inter * other * slope
        wide = g_hull * hull_other
        g_high = flow * (1.0 - high_s) + wide * high_s
        g_low = -flow * low_s - wide * (1.0 - low_s)
        grads[axis] = grads[axis] - 2.0 * (g_low + g_high)
        grads[axis + 2] = grads[axis + 2] - 2.0 * ((g_high - g_low) / 2 + g_area * size_other)
    value = jnp.sum((5.0 * l1_sum + 2.0 * mask * (1.0 - giou)) / box_count, axis=1, keepdims=True)
    return value, [grad * mask / box_count for grad in grads]


def middle_kernel(tokens, queries, classes, scal_ref, x1_ref, sine_ref, norm_ref, w1_ref, w2_ref, w_ref, head_ref,
                  query_ref, col_ref, row_ref,
                  dx1_ref, dw1_ref, dw2_ref, dsq_ref, dhead_ref, dquery_ref, dnorm_ref, loss_ref,
                  g0, s0, total1, tall_g, tall_s, small_g, small_s, kin, vin, kk, vv, probs2, mixed2, dsum, dq2, dmix2):
    images, padded, width = x1_ref.shape
    depth = width // HEADS
    chunks = w1_ref.shape[1] // width
    many = images * padded
    qrows = query_ref.shape[1]
    factor = 1.0 / math.sqrt(depth)
    gain = lambda row: norm_ref[row:row + 1, :]
    dnorm_ref[...] = jnp.zeros_like(dnorm_ref)

    def piece(chunk):
        return pl.ds(pl.multiple_of(chunk * width, width), width)

    def feed(layer, source, g_ref, s_ref, out_ref):
        def step(chunk, carry):
            value, slope = gelu_parts(nt(source, w1_ref[layer, piece(chunk), :]))
            value = value.astype(BF16)
            g_ref[chunk] = value
            s_ref[chunk] = slope.astype(BF16)
            out_ref[...] += nn(value, w2_ref[layer, piece(chunk), :])
            return carry
        lax.fori_loop(0, chunks, step, 0)

    def feed_back(layer, source_t, grad, grad_t, g_ref, s_ref, out_ref):
        def step(chunk, carry):
            dg = nt(grad, w2_ref[layer, piece(chunk), :]).astype(BF16)
            du = (dg.astype(F32) * s_ref[chunk].astype(F32)).astype(BF16)
            dw2_ref[layer, piece(chunk), :] = nn(grad_t, g_ref[chunk]).T.astype(dw2_ref.dtype)
            dw1_ref[layer, piece(chunk), :] = nn(source_t, du).T.astype(dw1_ref.dtype)
            out_ref[...] += nn(du, w1_ref[layer, piece(chunk), :])
            return carry
        lax.fori_loop(0, chunks, step, 0)

    x1 = x1_ref[...].reshape(many, width)
    total1[...] = x1
    feed(0, x1.astype(BF16), tall_g, tall_s, total1)
    unit1, scale1 = norm_parts(total1[...])
    x2 = unit1 * gain(1) + gain(7)
    for image in range(images):
        part = x2[image * padded:(image + 1) * padded]
        keyed = (part + sine_ref[...]).astype(BF16)
        lowm = part.astype(BF16)
        kin[image] = keyed
        vin[image] = lowm
        kk[image] = nn(keyed, w_ref[5]).astype(BF16)
        vv[image] = nn(lowm, w_ref[6]).astype(BF16)

    content = query_ref[0].astype(F32)
    place = query_ref[1].astype(F32)
    asked = (content + place).astype(BF16)
    lowc = content.astype(BF16)
    q1 = nn(asked, w_ref[0]).astype(BF16)
    k1 = nn(asked, w_ref[1]).astype(BF16)
    v1 = nn(lowc, w_ref[2]).astype(BF16)
    q1s = stack_heads(q1)
    p1 = masked_softmax(nt(q1s, k1), depth, queries)
    mix1 = pick_heads(nn(p1, v1))
    mix1b = mix1.astype(BF16)
    unit2, scale2 = norm_parts(content + nn(mix1b, w_ref[3]))
    t1 = unit2 * gain(2) + gain(8)

    asked2 = (t1 + place).astype(BF16)
    q2 = nn(asked2, w_ref[4]).astype(BF16)
    q2s = stack_heads(q2)

    def cross(image, carry):
        probs = masked_softmax(nt(q2s, kk[image]), depth, tokens)
        probs2[image] = probs
        mixed2[image] = pick_heads(nn(probs, vv[image]))
        return carry
    lax.fori_loop(0, images, cross, 0)
    rows = images * qrows
    mix2 = mixed2[...].reshape(rows, width)
    mix2b = mix2.astype(BF16)
    t1s = jnp.concatenate([t1] * images, axis=0)
    unit3, scale3 = norm_parts(t1s + nn(mix2b, w_ref[7]))
    t2 = unit3 * gain(3) + gain(9)

    t2b = t2.astype(BF16)
    g0[...] = t2
    feed(1, t2b, small_g, small_s, g0)
    unit4, scale4 = norm_parts(g0[...])
    t3 = unit4 * gain(4) + gain(10)
    unit5, scale5 = norm_parts(t3)
    out = (unit5 * gain(5) + gain(11)).astype(BF16)

    inverse, box_count = scal_ref[0], scal_ref[1]
    logits = nn(out, head_ref[...])
    lane = lax.broadcasted_iota(jnp.int32, logits.shape, 1)
    weight = col_ref[:, 0:1]
    label = col_ref[:, 1:2].astype(jnp.int32)
    kept = jnp.where(lane < classes, logits, -1e30)
    top = jnp.max(kept, axis=1, keepdims=True)
    powers = jnp.exp(kept - top)
    norm_sum = jnp.sum(powers, axis=1, keepdims=True)
    chosen = lane == label
    ce = top + jnp.log(norm_sum) - jnp.sum(jnp.where(chosen, logits, 0.0), axis=1, keepdims=True)
    ce_sum = jnp.sum(weight * ce, axis=0, keepdims=True)
    dlogits = ((weight * inverse) * (powers / norm_sum - jnp.where(chosen, 1.0, 0.0))).astype(BF16)

    b1, slope_one = gelu_parts(nn(out, w_ref[8]))
    b1 = b1.astype(BF16)
    b2, slope_two = gelu_parts(nn(b1, w_ref[9]))
    b2 = b2.astype(BF16)
    raw = nn(b2, head_ref[...]).T
    box = [sigmoid(raw[classes + j:classes + j + 1, :]) for j in range(4)]
    target = [row_ref[1 + j:2 + j, :] for j in range(4)]
    box_value, dbox = box_loss(box, target, row_ref[0:1, :], box_count)
    loss_ref[...] = ce_sum * inverse + box_value
    draw = jnp.concatenate([grad * one * (1.0 - one) for grad, one in zip(dbox, box)], axis=0)
    lanes_in = head_ref.shape[1]
    spot = lax.broadcasted_iota(jnp.int32, (lanes_in, rows), 0)
    spread = jnp.zeros((lanes_in, rows), F32)
    for j in range(4):
        spread = jnp.where(spot == classes + j, draw[j:j + 1, :], spread)
    draw_rows = spread.T.astype(BF16)

    dhead_ref[...] = (tn(out, dlogits) + tn(b2, draw_rows)).astype(dhead_ref.dtype)
    du2 = (nt(draw_rows, head_ref[...]) * slope_two).astype(BF16)
    dsq_ref[9] = tn(b1, du2).astype(dsq_ref.dtype)
    du1 = (nt(du2, w_ref[9]) * slope_one).astype(BF16)
    dsq_ref[8] = tn(out, du1).astype(dsq_ref.dtype)
    dout = nt(dlogits, head_ref[...]) + nt(du1, w_ref[8])

    def through(grad, unit, scale, row):
        dnorm_ref[row:row + 1, :] = column_sum(grad * unit)
        dnorm_ref[row + 6:row + 7, :] = column_sum(grad)
        return norm_back(grad, unit, scale, gain(row))

    dt3 = through(dout, unit5, scale5, 5)
    ds3 = through(dt3, unit4, scale4, 4)
    g0[...] = ds3
    ds3b = ds3.astype(BF16)
    feed_back(1, t2b.T, ds3b, ds3b.T, small_g, small_s, g0)
    ds2 = through(g0[...], unit3, scale3, 3)
    ds2b = ds2.astype(BF16)
    dsq_ref[7] = tn(mix2b, ds2b).astype(dsq_ref.dtype)
    dmix2[...] = nt(ds2b, w_ref[7]).astype(BF16).reshape(images, qrows, width)
    dq2[...] = jnp.zeros_like(dq2)
    dsum[...] = jnp.zeros_like(dsum)

    def attention_back(dmix, mix, probs, stacked_q, keys, values):
        dms = stack_heads(dmix)
        both = dmix.astype(F32) * mix
        weight = jnp.concatenate(
            [jnp.sum(both * head_mask(width, head).astype(F32), axis=1, keepdims=True) for head in range(HEADS)],
            axis=0,
        )
        dscores = (probs.astype(F32) * (nt(dms, values) - weight)).astype(BF16)
        dq = pick_heads(nn(dscores, keys)) * factor
        dk = (tn(stacked_q, dscores) * factor).astype(BF16).T
        dv = tn(dms, probs).astype(BF16).T
        return dq, dk, dv

    def cross_back(image, carry):
        dq, dk, dv = attention_back(dmix2[image], mixed2[image], probs2[image], q2s, kk[image], vv[image])
        dq2[...] += dq
        dsum[0] += tn(kin[image], dk)
        dsum[1] += tn(vin[image], dv)
        dx1_ref[image] = nt(dk, w_ref[5]) + nt(dv, w_ref[6])
        return carry
    lax.fori_loop(0, images, cross_back, 0)
    dsq_ref[5] = dsum[0].astype(dsq_ref.dtype)
    dsq_ref[6] = dsum[1].astype(dsq_ref.dtype)
    dq2b = dq2[...].astype(BF16)
    dsq_ref[4] = tn(asked2, dq2b).astype(dsq_ref.dtype)
    dasked2 = nt(dq2b, w_ref[4])
    dt1 = dasked2
    for image in range(images):
        dt1 = dt1 + ds2[image * qrows:(image + 1) * qrows]
    ds1 = through(dt1, unit2, scale2, 2)
    ds1b = ds1.astype(BF16)
    dsq_ref[3] = tn(mix1b, ds1b).astype(dsq_ref.dtype)
    dmix1 = nt(ds1b, w_ref[3]).astype(BF16)
    dq, dk, dv = attention_back(dmix1, mix1, p1, q1s, k1, v1)
    dqb = dq.astype(BF16)
    dsq_ref[0] = tn(asked, dqb).astype(dsq_ref.dtype)
    dsq_ref[1] = tn(asked, dk).astype(dsq_ref.dtype)
    dsq_ref[2] = tn(lowc, dv).astype(dsq_ref.dtype)
    dasked = nt(dqb, w_ref[0]) + nt(dk, w_ref[1])
    dquery_ref[0] = ds1 + dasked + nt(dv, w_ref[2])
    dquery_ref[1] = dasked + dasked2

    unit, scale = norm_parts(total1[...])
    dx2 = dx1_ref[...].reshape(many, width)
    ds = through(dx2, unit, scale, 1)
    total1[...] = ds
    dsb = ds.astype(BF16)
    x1b = x1_ref[...].reshape(many, width).astype(BF16)
    feed_back(0, x1b.T, dsb, dsb.T, tall_g, tall_s, total1)
    dx1_ref[...] = total1[...].reshape(images, padded, width)


def middle(scalars, x1, sine, norm, w1, w2, square, head, query, col, row, tokens, queries, classes):
    images, padded, width = x1.shape
    qrows = query.shape[1]
    chunks = w1.shape[1] // width
    many, rows = images * padded, images * qrows
    vmem = pl.BlockSpec(memory_space=pltpu.VMEM)
    shapes = [
        ((images, padded, width), F32), (w1.shape, BF16), (w2.shape, BF16), (square.shape, BF16),
        (head.shape, BF16), (query.shape, F32), (norm.shape, F32), ((1, 1), F32),
    ]
    return pl.pallas_call(
        functools.partial(middle_kernel, tokens, queries, classes),
        in_specs=[pl.BlockSpec(memory_space=pltpu.SMEM)] + [vmem] * 10,
        out_specs=[vmem] * len(shapes),
        out_shape=[jax.ShapeDtypeStruct(shape, kind) for shape, kind in shapes],
        scratch_shapes=[
            pltpu.VMEM((rows, width), F32), pltpu.VMEM((8, 128), F32), pltpu.VMEM((many, width), F32),
            pltpu.VMEM((chunks, many, width), BF16), pltpu.VMEM((chunks, many, width), BF16),
            pltpu.VMEM((chunks, rows, width), BF16), pltpu.VMEM((chunks, rows, width), BF16),
            pltpu.VMEM((images, padded, width), BF16), pltpu.VMEM((images, padded, width), BF16),
            pltpu.VMEM((images, padded, width), BF16), pltpu.VMEM((images, padded, width), BF16),
            pltpu.VMEM((images, HEADS * qrows, padded), BF16), pltpu.VMEM((images, qrows, width), F32),
            pltpu.VMEM((2, width, width), F32), pltpu.VMEM((qrows, width), F32),
            pltpu.VMEM((images, qrows, width), BF16),
        ],
        compiler_params=pltpu.CompilerParams(vmem_limit_bytes=VMEM_LIMIT),
        name="middle",
    )(scalars, x1, sine, norm, w1, w2, square, head, query, col, row)


def sine_table(width, padded):
    cells = np.arange(SIDE * SIDE)
    half = width // 2
    index = np.arange(half)
    freqs = 10000.0 ** ((2 * (index // 2)) / half)
    parts = []
    for coord in (cells // SIDE + 1, cells % SIDE + 1):
        angle = (coord / (SIDE + 1e-06) * (2.0 * math.pi))[:, None] / freqs[None, :]
        parts.append(np.where(index[None, :] % 2 == 0, np.sin(angle), np.cos(angle)))
    table = np.concatenate(parts, axis=1).astype(np.float32)
    return np.concatenate([table, np.zeros((padded - table.shape[0], width), np.float32)], axis=0)


def round_up(value, unit):
    return -(-value // unit) * unit


def target_info(matches, labels, boxes, classes, qrows):
    images, queries = matches.shape
    pad = ((0, 0), (0, qrows - queries))
    matched = matches >= 0
    picker = matches[:, :, None] == jnp.arange(labels.shape[1])[None, None, :]
    label = jnp.where(matched, jnp.sum(jnp.where(picker, labels[:, None, :], 0), axis=2), classes - 1)
    weight = jnp.pad(jnp.where(matched, 1.0, NO_OBJECT), pad)
    label = jnp.pad(label, pad).astype(F32)
    col = jnp.stack([weight.reshape(-1), label.reshape(-1)], axis=1)
    mask = jnp.pad(matched.astype(F32), pad).reshape(1, -1)
    wanted = []
    for j in range(4):
        one = jnp.sum(jnp.where(picker, boxes[:, None, :, j], 0.0), axis=2)
        wanted.append(jnp.pad(jnp.where(matched, one, 0.5), pad, constant_values=0.5).reshape(1, -1))
    row = jnp.concatenate([mask] + wanted + [jnp.zeros((3, mask.shape[1]), F32)], axis=0)
    return col, row


AXES = ("dp", "fsdp")


def swap(value, bit, devices):
    return lax.ppermute(value, AXES, [(i, i ^ bit) for i in range(devices)])


def bits_of(devices):
    return [1 << j for j in range(devices.bit_length() - 1)]


def gather_rows(value, devices):
    me = lax.axis_index(AXES)
    held = value[None]
    for bit in reversed(bits_of(devices)):
        other = swap(held, bit, devices)
        mine = (me & bit) == 0
        held = jnp.where(mine, jnp.concatenate([held, other]), jnp.concatenate([other, held]))
    count = len(bits_of(devices))
    held = held.reshape((2,) * count + value.shape)
    return jnp.transpose(held, tuple(reversed(range(count))) + (count, count + 1)).reshape((devices,) + value.shape)


def scatter_sums(parts, devices):
    me = lax.axis_index(AXES)
    bits = bits_of(devices)
    state = []
    for part, order in parts:
        state.append((part.reshape((2,) * len(bits) + part.shape[1:]), list(reversed(bits)), order))
    for stage in range(len(bits)):
        sent = []
        for held, left, order in state:
            bit = order[stage]
            axis = left.index(bit)
            mine = (me // bit) % 2
            out = lax.dynamic_index_in_dim(held, 1 - mine, axis, keepdims=False).astype(BF16)
            sent.append((swap(out, bit, devices), lax.dynamic_index_in_dim(held, mine, axis, keepdims=False)))
        fresh = []
        for (held, left, order), (came, kept) in zip(state, sent):
            left = [bit for bit in left if bit != order[stage]]
            fresh.append((kept.astype(F32) + came.astype(F32), left, order))
        state = fresh
    return [held for held, _, _ in state]


def exact(left, right, dims=((1,), (0,))):
    return lax.dot_general(left, right, (dims, ((), ())), precision=lax.Precision.HIGHEST, preferred_element_type=F32)


def gram_kernel(mom_ref, grad_ref, x_ref, gram_ref, sums_ref):
    slot = mom_ref.shape[1]
    devices, _, width = grad_ref.shape
    sums = jnp.sum(grad_ref[:, slot:, :].astype(F32), axis=0)
    sums_ref[...] = sums
    squares = jnp.sum(sums[0:1, 0:3], axis=1, keepdims=True)
    factor = jnp.minimum(1.0, CLIP / (jnp.sqrt(squares) + 1e-06))
    x = BETA_M * mom_ref[...].astype(F32) + factor * grad_ref[:, :slot, :].astype(F32)
    x = x.reshape(devices * slot, width)
    x_ref[...] = x
    gram_ref[...] = exact(x, x, ((0,), (0,)))


def polish_kernel(x_ref, gram_ref, out_ref):
    gram = gram_ref[...]
    size = gram.shape[0]
    diagonal = lax.broadcasted_iota(jnp.int32, gram.shape, 0) == lax.broadcasted_iota(jnp.int32, gram.shape, 1)
    eye = jnp.where(diagonal, 1.0, 0.0)
    square = jnp.sum(jnp.sum(gram * eye, axis=1, keepdims=True), axis=0, keepdims=True)
    scale = 1.0 / (jnp.sqrt(square) + 1e-07)
    gram = gram * (scale * scale)
    total = None
    for sweep in range(5):
        poly = NS_A * eye + NS_B * gram + NS_C * exact(gram, gram)
        total = poly if sweep == 0 else exact(total, poly)
        if sweep < 4:
            gram = exact(exact(poly, gram), poly)
    out = exact(x_ref[...] * scale, total)
    out_ref[...] = out.reshape(out_ref.shape).astype(out_ref.dtype)


def plain_call(body, shapes, *args):
    vmem = pl.BlockSpec(memory_space=pltpu.VMEM)
    return pl.pallas_call(
        body,
        in_specs=[vmem] * len(args),
        out_specs=[vmem] * len(shapes),
        out_shape=[jax.ShapeDtypeStruct(shape, kind) for shape, kind in shapes],
        compiler_params=pltpu.CompilerParams(vmem_limit_bytes=VMEM_LIMIT),
        name=body.__name__,
    )(*args)


def split_three(value):
    high = value.astype(BF16)
    rest = value - high.astype(F32)
    middle_part = rest.astype(BF16)
    return [high, middle_part, (rest - middle_part.astype(F32)).astype(BF16)]


def to_slots(square, feeds, devices):
    count, rows, width = square.shape
    slot = feeds.shape[1] // 4
    feed_slots = feeds.reshape(feeds.shape[0] * 4, slot, width)
    square_slots = jnp.pad(square, ((0, devices - count - feed_slots.shape[0]), (0, slot - rows), (0, 0)))
    return jnp.concatenate([feed_slots, square_slots], axis=0)


def exchange(slots):
    return lax.all_to_all(slots, AXES, split_axis=0, concat_axis=0, tiled=True)


def adam(weight, first, second, gradient, rate, decay):
    first = ADAM_B1 * first + (1.0 - ADAM_B1) * gradient
    second = ADAM_B2 * second + (1.0 - ADAM_B2) * gradient * gradient
    fixed_first = first / (1.0 - ADAM_B1**STEP)
    fixed_second = second / (1.0 - ADAM_B2**STEP)
    weight = weight * (1.0 - rate * decay) - rate * fixed_first / (jnp.sqrt(fixed_second) + 1e-08)
    return weight, first, second, weight.astype(BF16)


def muon(weight, ortho, longest):
    fresh = weight * (1.0 - LR_M * DECAY_M) - LR_M * 0.2 * math.sqrt(longest) * ortho
    return fresh, fresh.astype(BF16)


def widen(value, width):
    return jnp.pad(value, ((0, 0), (0, width - value.shape[1])))


def per_device(devices, features, matches, target_labels, target_boxes,
               square_weight, square_momentum, expand_weight, expand_momentum, reduce_weight, reduce_momentum,
               input_weight, input_momentum, input_second, head_weight, head_momentum, head_second,
               query_weight, query_momentum, query_second, norm_weight, norm_momentum, norm_second):
    images, tokens, channels = features.shape
    count, rs, width = square_weight.shape
    pairs, _, rf = expand_weight.shape
    ri = input_weight.shape[0]
    rh, head_lanes = head_weight.shape
    _, queries, rq = query_weight.shape
    norms, rn = norm_weight.shape
    classes = head_lanes - 4
    padded, qrows = round_up(tokens, 128), round_up(queries, 128)
    lanes = round_up(head_lanes, 128)
    hidden = rf * devices

    low = lax.optimization_barrier(tuple(
        value.astype(BF16) for value in (
            square_weight, jnp.transpose(expand_weight, (0, 2, 1)), reduce_weight, input_weight, head_weight,
            jnp.transpose(query_weight, (0, 2, 1)), norm_weight.T)))
    wsq, wex, wre, win, whead, wquery, wnorm = low
    first = jnp.concatenate([win, wsq[:4].reshape(4 * rs, width), widen(wnorm, width)])
    found = jnp.sum((matches >= 0).astype(F32)).astype(BF16)
    second = jnp.concatenate([
        wex.reshape(pairs * rf, width), wre.reshape(pairs * rf, width), wsq[4:].reshape((count - 4) * rs, width),
        widen(whead, width), widen(wquery.reshape(2 * rq, queries), width),
        jnp.broadcast_to(found, (8, width)),
    ])
    got_one = gather_rows(first, devices)
    got_two = lax.all_gather(second, AXES, axis=0, tiled=False)

    def rows_of(got, start, parts, rows):
        piece = got[:, start:start + parts * rows].reshape(devices, parts, rows, width)
        return jnp.transpose(piece, (1, 0, 2, 3)).reshape(parts, devices * rows, width)

    win_all = rows_of(got_one, 0, 1, ri)[0]
    sq_one = rows_of(got_one, ri, 4, rs)
    norm_all = rows_of(got_one, ri + 4 * rs, 1, rn)[0, :, :norms].T.astype(F32)
    at = 0
    ex_all = rows_of(got_two, at, pairs, rf)
    at += pairs * rf
    re_all = rows_of(got_two, at, pairs, rf)
    at += pairs * rf
    sq_two = rows_of(got_two, at, count - 4, rs)
    at += (count - 4) * rs
    head_all = rows_of(got_two, at, 1, rh)[0, :, :lanes]
    at += rh
    query_all = jnp.transpose(rows_of(got_two, at, 2, rq)[:, :, :qrows], (0, 2, 1))
    at += 2 * rq
    box_total = jnp.sum(got_two[:, at, 0].astype(F32))

    sine = jnp.asarray(sine_table(width, padded))
    col, row = target_info(matches, target_labels, target_boxes, classes, qrows)
    inverse = 1.0 / (images * devices * queries)
    scalars = jnp.stack([jnp.full((), inverse, F32), box_total])
    probs, keyed, lowm, q, k, v, o, s0, x1 = encode(features, win_all, sq_one, sine, norm_all)
    dx1, dex, dre, dsq_two, dhead, dquery, dnorm, loss = middle(
        scalars, x1, sine, norm_all, ex_all, re_all, sq_two, head_all, query_all, col, row, tokens, queries, classes)
    dsq_one, dwin, dnorm_one = encode_back(dx1, s0, norm_all, probs, keyed, lowm, q, k, v, o, sq_one, features)

    def by_device(grad, rows):
        parts = grad.shape[0]
        piece = grad.astype(BF16).reshape(parts, devices, rows, width)
        return jnp.transpose(piece, (1, 0, 2, 3)).reshape(devices, parts * rows, width)

    dquery_rows = widen(jnp.transpose(dquery, (0, 2, 1)).reshape(2 * width, qrows), width).reshape(2, width, width)
    dnorm_rows = widen(dnorm.T, width)[None]
    dnorm_more = widen(dnorm_one.T, width)[None]
    bits = bits_of(devices)
    one = [bits[0], bits[1], bits[2]] + list(reversed(bits[3:]))
    two = [bits[0], bits[2], bits[1]] + list(reversed(bits[3:]))
    part_a = jnp.concatenate([by_device(dex, rf), by_device(dsq_two[:5], rs)], axis=1)
    part_b = jnp.concatenate([
        by_device(dre, rf), by_device(dsq_two[5:], rs), by_device(widen(dhead, width)[None], rh),
        by_device(dquery_rows, rq), by_device(dnorm_rows, rn)], axis=1)
    part_c = by_device(dwin[None], ri)
    part_d = jnp.concatenate([by_device(dsq_one, rs), by_device(dnorm_more, rn)], axis=1)
    sum_a, sum_b = scatter_sums([(part_a, one), (part_b, two)], devices)
    sum_c, sum_d = scatter_sums([(part_c, one), (part_d, two)], devices)
    cut = pairs * rf
    g_expand = sum_a[:cut].reshape(pairs, rf, width)
    g_reduce = sum_b[:cut].reshape(pairs, rf, width)
    half = 5 * rs
    more = count - 9
    g_square = jnp.concatenate([
        sum_d[:4 * rs].reshape(4, rs, width), sum_a[cut:cut + half].reshape(5, rs, width),
        sum_b[cut:cut + more * rs].reshape(more, rs, width)])
    at = cut + more * rs
    g_head = sum_b[at:at + rh, :head_lanes]
    at += rh
    g_query = jnp.transpose(sum_b[at:at + 2 * rq, :queries].reshape(2, rq, queries), (0, 2, 1))
    at += 2 * rq
    g_norm = sum_b[at:at + rn, :norms].T
    g_more = sum_d[4 * rs:4 * rs + rn, :2].T
    g_norm = g_norm + jnp.zeros_like(g_norm).at[0].set(g_more[0]).at[6].set(g_more[1])
    g_input = sum_c

    squares = sum(jnp.sum(g * g) for g in (g_square, g_expand, g_reduce, g_input, g_head, g_query, g_norm))
    numbers = jnp.stack(split_three(squares) + split_three(loss[0, 0]))
    pieces = jnp.zeros((8, width), BF16).at[0, 0:3].set(numbers[0:3]).at[1, 0:3].set(numbers[3:6])
    mom_slots = to_slots(
        square_momentum.astype(BF16),
        jnp.concatenate([jnp.transpose(expand_momentum, (0, 2, 1)), reduce_momentum]).astype(BF16), devices)
    grad_slots = to_slots(g_square.astype(BF16), jnp.concatenate([g_expand, g_reduce]).astype(BF16), devices)
    grad_slots = jnp.concatenate([grad_slots, jnp.broadcast_to(pieces, (devices, 8, width))], axis=1)
    slot = mom_slots.shape[1]
    mom_in = exchange(mom_slots)
    grad_in = exchange(grad_slots)
    x, gram, sums = plain_call(
        gram_kernel, [((devices * slot, width), F32), ((width, width), F32), ((8, width), F32)], mom_in, grad_in)
    feeds = 8 * pairs
    for bit in (1, 2):
        gram = gram + lax.ppermute(gram, AXES, [(i, i ^ bit) for i in range(feeds)])
    back = exchange(plain_call(polish_kernel, [((devices, slot, width), BF16)], x, gram)[0])
    o_feed = back[:feeds].reshape(2 * pairs, rf, width).astype(F32)
    o_square = back[feeds:feeds + count, :rs].astype(F32)

    gradient_norm = jnp.sqrt(jnp.sum(sums[0, 0:3]))
    loss_value = jnp.sum(sums[1, 0:3])
    factor = jnp.minimum(1.0, CLIP / (gradient_norm + 1e-06))
    square_mom = BETA_M * square_momentum + factor * g_square
    expand_mom = BETA_M * expand_momentum + factor * jnp.transpose(g_expand, (0, 2, 1))
    reduce_mom = BETA_M * reduce_momentum + factor * g_reduce
    square_next, square_copy = muon(square_weight, o_square, width)
    expand_next, expand_copy = muon(expand_weight, jnp.transpose(o_feed[:pairs], (0, 2, 1)), hidden)
    reduce_next, reduce_copy = muon(reduce_weight, o_feed[pairs:], hidden)
    return (
        (square_next, square_mom, square_copy, expand_next, expand_mom, expand_copy,
         reduce_next, reduce_mom, reduce_copy)
        + adam(input_weight, input_momentum, input_second, factor * g_input, 0.04, 0.0001)
        + adam(head_weight, head_momentum, head_second, factor * g_head, 0.1, 0.0001)
        + adam(query_weight, query_momentum, query_second, factor * g_query, 0.5, 0.0)
        + adam(norm_weight, norm_momentum, norm_second, factor * g_norm, 0.5, 0.0)
        + (loss_value, box_total, gradient_norm)
    )


def solution(mesh):
    both = ("dp", "fsdp")
    first = [P(both), P(both), P(both), P(both)]
    square, expand, reduce = P(None, both), P(None, None, both), P(None, both)
    rows, query, norm = P(both), P(None, None, both), P(None, both)
    in_specs = tuple(first + [square] * 2 + [expand] * 2 + [reduce] * 2 + [rows] * 6 + [query] * 3 + [norm] * 3)
    out_specs = tuple([square] * 3 + [expand] * 3 + [reduce] * 3 + [rows] * 8 + [query] * 4 + [norm] * 4 + [P()] * 3)
    return jax.shard_map(
        functools.partial(per_device, mesh.size), mesh=mesh, in_specs=in_specs, out_specs=out_specs, check_vma=False)
```

```python
import functools
import math

import jax
import jax.numpy as jnp
import numpy as np
from jax import lax
from jax.experimental import pallas as pl
from jax.experimental.layout import Layout, with_layout_constraint
from jax.experimental.pallas import tpu as pltpu
from jax.sharding import PartitionSpec as P

HEADS = 8
SIDE = 25
STEP = 10
NS_A = 3.4445
NS_B = -4.775
NS_C = 2.0315
CLIP = 0.02
BETA_M = 0.95
LR_M = 0.3
DECAY_M = 0.01
ADAM_B1 = 0.9
ADAM_B2 = 0.999
SOFT = 0.02
SOFT_L1 = 0.05
NO_OBJECT = 0.1
EPS = 1e-05
LOG2E = math.log2(math.e)
F32 = jnp.float32
BF16 = jnp.bfloat16
VMEM_LIMIT = 56 * 1024 * 1024
TIE = (3, 4)


def nn(left, right):
    return lax.dot_general(left, right, (((1,), (0,)), ((), ())), preferred_element_type=F32)


def nt(left, right):
    return lax.dot_general(left, right, (((1,), (1,)), ((), ())), preferred_element_type=F32)


def tn(left, right):
    return lax.dot_general(left, right, (((0,), (0,)), ((), ())), preferred_element_type=F32)


BLOCKS = 32
FIRST = (64, 8, 8, 8, 8, 8, 8)
SECOND = (64,) * 4 + (8,) * 14
PART_A = (64, 64) + (8,) * 6
PART_B = (64, 64) + (8,) * 8
PART_C = (64,) + (8,) * 6


def by_core(value):
    rows = value.shape[0] // BLOCKS
    value = value.reshape(BLOCKS // 2, 2, rows, value.shape[1])
    return value[:, 0], value[:, 1]


def pair_rows(one, two):
    width = one.shape[1]
    both = [part.reshape(BLOCKS, part.shape[0] // BLOCKS, width) for part in (one, two)]
    return jnp.concatenate(both, axis=1).reshape(2 * one.shape[0], width)


def unpair(both):
    both = both.astype(F32)
    half = both.shape[1] // 2
    return [both[:, j * half:(j + 1) * half].reshape(BLOCKS * half, both.shape[2]) for j in range(2)]


def put_blocks(refs, flip, start, value):
    rows = value.shape[0] // BLOCKS
    even, odd = by_core(value)
    refs[0][:, start:start + rows, :] = jnp.where(flip, odd, even).astype(BF16)
    refs[1][:, start:start + rows, :] = jnp.where(flip, even, odd).astype(BF16)


def head_mask(width, head):
    lane = lax.broadcasted_iota(jnp.int32, (1, width), 1)
    depth = width // HEADS
    return jnp.logical_and(lane >= head * depth, lane < (head + 1) * depth).astype(F32).astype(BF16)


def norm_parts(total):
    center = total - jnp.mean(total, axis=-1, keepdims=True)
    spread = jnp.mean(center * center, axis=-1, keepdims=True)
    scale = lax.rsqrt(spread + EPS)
    return center * scale, scale


def norm_back(grad, unit, scale, gain):
    inner = grad * gain
    mean_inner = jnp.mean(inner, axis=-1, keepdims=True)
    mean_cross = jnp.mean(inner * unit, axis=-1, keepdims=True)
    return scale * (inner - mean_inner - unit * mean_cross)


def column_sum(value):
    return jnp.sum(value, axis=0, keepdims=True)


GELU_C = math.sqrt(2.0 / math.pi)
GELU_K = 0.044715 * GELU_C


def gelu_parts(value):
    square = value * value
    half = 0.5 + 0.5 * jnp.tanh(value * (GELU_C + GELU_K * square))
    out = value * half
    slope = half + out * (1.0 - half) * (2.0 * GELU_C + 6.0 * GELU_K * square)
    return out, slope


def masked_softmax(scores, depth, length):
    padded = scores.shape[1]
    start = (padded - 1) // 128 * 128
    if length < padded:
        lane = lax.broadcasted_iota(jnp.int32, (1, padded - start), 1)
        tail = jnp.where(lane < length - start, scores[:, start:], -1e30)
        scores = tail if start == 0 else jnp.concatenate([scores[:, :start], tail], axis=1)
    factor = LOG2E / math.sqrt(depth)
    top = jnp.max(scores, axis=1, keepdims=True)
    powers = jnp.exp2((scores - top) * factor)
    inverse = 1.0 / jnp.sum(powers, axis=1, keepdims=True)
    return (powers * inverse).astype(BF16)


def encode_kernel(tokens, order, f_ref, got_ref, sine_ref,
                  p_ref, keyed_ref, lowm_ref, q_ref, k_ref, v_ref, o_ref, s0_ref, x1_ref, w_ref, norm_ref, win_ref):
    head = pl.program_id(1)
    width = got_ref.shape[2]

    @pl.when(jnp.logical_and(pl.program_id(0) == 0, head == 0))
    def _():
        rows = FIRST[0]
        for block in range(BLOCKS):
            win_ref[block * rows:(block + 1) * rows, :] = got_ref[order[block], 0:rows, :]
        for pair in range(2):
            start = rows + 16 * pair
            both = jnp.stack([got_ref[order[block], start:start + 16, :] for block in range(BLOCKS)])
            for j, one in enumerate(unpair(both)):
                w_ref[2 * pair + j] = one.astype(BF16)
        last = jnp.stack([got_ref[order[block], rows + 32:rows + 48, :] for block in range(BLOCKS)])
        norm_ref[...] = unpair(last)[0][:, 0:128].T[0:norm_ref.shape[0], :]

    @pl.when(head == 0)
    def _():
        padded = s0_ref.shape[1]
        s0_ref[0, tokens // 8 * 8:padded, :] = jnp.zeros((padded - tokens // 8 * 8, width), F32)
        s0_ref[0, 0:tokens, :] = nn(f_ref[0], win_ref[...])
        memory = s0_ref[0]
        keyed = (memory + sine_ref[...]).astype(BF16)
        lowm = memory.astype(BF16)
        keyed_ref[0] = keyed
        lowm_ref[0] = lowm
        q_ref[0] = nn(keyed, w_ref[0]).astype(BF16)
        k_ref[0] = nn(keyed, w_ref[1]).astype(BF16)
        v_ref[0] = nn(lowm, w_ref[2]).astype(BF16)
        o_ref[...] = jnp.zeros_like(o_ref)

    mask = head_mask(width, head)
    scores = nt(q_ref[0] * mask, k_ref[0])
    probs = masked_softmax(scores, width // HEADS, tokens)
    p_ref[0, 0] = probs
    o_ref[0] += nn(probs, v_ref[0] * mask)

    @pl.when(head == HEADS - 1)
    def _():
        total = s0_ref[0] + nn(o_ref[0].astype(BF16), w_ref[3])
        s0_ref[0] = total
        unit, scale = norm_parts(total)
        x1_ref[0] = unit * norm_ref[0:1, :] + norm_ref[6:7, :]


def encode(features, got, order, sine):
    images, tokens, depth = features.shape
    width = got.shape[2]
    padded = sine.shape[0]
    per_image = lambda kind: jax.ShapeDtypeStruct((images, padded, width), kind)
    image_block = pl.BlockSpec((1, padded, width), lambda i, h: (i, 0, 0))
    whole = lambda shape: pl.BlockSpec(shape, lambda i, h: (0,) * len(shape))
    return pl.pallas_call(
        functools.partial(encode_kernel, tokens, order),
        grid=(images, HEADS),
        in_specs=[pl.BlockSpec((1, tokens, depth), lambda i, h: (i, 0, 0)), whole(got.shape), whole(sine.shape)],
        out_specs=[pl.BlockSpec((1, 1, padded, padded), lambda i, h: (i, h, 0, 0))] + [image_block] * 8
        + [whole((4, width, width)), whole((16, width))],
        out_shape=[jax.ShapeDtypeStruct((images, HEADS, padded, padded), BF16)]
        + [per_image(BF16)] * 5 + [per_image(F32)] * 3
        + [jax.ShapeDtypeStruct((4, width, width), BF16), jax.ShapeDtypeStruct((16, width), F32)],
        scratch_shapes=[pltpu.VMEM((depth, width), BF16)],
        compiler_params=pltpu.CompilerParams(vmem_limit_bytes=VMEM_LIMIT),
        name="encode",
    )(features, got, sine)


def encode_back_kernel(tokens, images, first, last, *refs):
    (flip_ref, dx1_ref, s0_ref, norm_ref, p_ref, keyed_ref, lowm_ref, q_ref, k_ref, v_ref, o_ref, w_ref), refs = (
        refs[:12], refs[12:])
    if not first:
        (dsq_in, dnorm_in), refs = refs[:2], refs[2:]
    if last:
        f_refs, refs = refs[:images], refs[images:]
        dm_refs, refs = refs[:images - 1], refs[images - 1:]
        outs, refs = refs[:2], refs[2:]
        *refs, dsq, dnorm_ref = refs
    else:
        (dsq, dnorm_ref, dm_ref), refs = refs[:3], refs[3:]
    ds0, dout, dout_t, q_t, cross, dq, dk_t, dv_t = refs
    head = pl.program_id(0)
    width = w_ref.shape[1]
    depth = width // HEADS

    @pl.when(head == 0)
    def _():
        dsq[...] = jnp.zeros_like(dsq) if first else dsq_in[...]
        dnorm_ref[...] = jnp.zeros_like(dnorm_ref) if first else dnorm_in[...]

    @pl.when(head == 0)
    def _():
        unit, scale = norm_parts(s0_ref[0])
        grad = dx1_ref[0]
        dnorm_ref[0:1, :] += column_sum(grad * unit)
        dnorm_ref[6:7, :] += column_sum(grad)
        dtotal = norm_back(grad, unit, scale, norm_ref[0:1, :])
        ds0[...] = dtotal
        low = dtotal.astype(BF16)
        dsq[3] += tn(o_ref[0].astype(BF16), low)
        dmixed = nt(low, w_ref[3]).astype(BF16)
        dout[...] = dmixed
        dout_t[...] = dmixed.T
        q_t[...] = q_ref[0].T
        cross[...] = dmixed.astype(F32) * o_ref[0]
        dq[...] = jnp.zeros_like(dq)

    mask = head_mask(width, head)
    rows = pl.ds(pl.multiple_of(head * depth, depth), depth)
    weight = jnp.sum(cross[...] * mask.astype(F32), axis=1, keepdims=True)
    probs = p_ref[0, 0]
    dprobs = nt(dout[...] * mask, v_ref[0])
    dscores = (probs.astype(F32) * (dprobs - weight)).astype(BF16)
    dq[...] += nn(dscores, k_ref[0] * mask)
    dk_t[rows, :] = nn(q_t[rows, :], dscores)
    dv_t[rows, :] = nn(dout_t[rows, :], probs)

    @pl.when(head == HEADS - 1)
    def _():
        factor = 1.0 / math.sqrt(depth)
        dqb = (dq[...] * factor).astype(BF16)
        dkb = (dk_t[...] * factor).astype(BF16).T
        dvb = dv_t[...].astype(BF16).T
        dsq[0] += tn(keyed_ref[0], dqb)
        dsq[1] += tn(keyed_ref[0], dkb)
        dsq[2] += tn(lowm_ref[0], dvb)
        dm = ds0[...] + nt(dqb, w_ref[0]) + nt(dkb, w_ref[1]) + nt(dvb, w_ref[2])
        dmb = dm.astype(BF16)
        if not last:
            dm_ref[0] = dmb
        else:
            parts = [ref[0] for ref in dm_refs] + [dmb]
            dwin = sum(tn(part[0:tokens], ref[0]) for part, ref in zip(parts, f_refs))
            flip = flip_ref[0] > 0
            rows = PART_C[0]
            put_blocks(outs, flip, 0, dwin.astype(BF16).T)
            for pair in range(2):
                put_blocks(outs, flip, rows + 16 * pair, pair_rows(dsq[2 * pair], dsq[2 * pair + 1]))
            put_blocks(outs, flip, rows + 32, pair_rows(norm_columns(dnorm_ref[...], width), jnp.zeros((width, width), F32)))


def norm_columns(dnorm, width):
    wide = jnp.concatenate([dnorm, jnp.zeros((128 - dnorm.shape[0], width), F32)], axis=0).T
    return jnp.concatenate([wide, jnp.zeros((width, width - 128), F32)], axis=1)


def encode_back(image, images, flip, dx1, s0, norm, probs, keyed, lowm, q, k, v, o, square, features, *before):
    _, tokens, channels = features.shape
    padded, width = s0.shape[1:]
    first, last = image == 0, image == images - 1
    image_block = pl.BlockSpec((1, padded, width), lambda h: (image, 0, 0))
    whole = lambda shape: pl.BlockSpec(shape, lambda h: (0,) * len(shape))
    sums = [((4, width, width), F32), (norm.shape, F32)]
    part = ((BLOCKS // 2, sum(PART_C), width), BF16)
    outs = [part, part] if last else sums + [((1, padded, width), BF16)]
    scratch = [((padded, width), F32), ((padded, width), BF16), ((width, padded), BF16), ((width, padded), BF16),
               ((padded, width), F32), ((padded, width), F32), ((width, padded), F32), ((width, padded), F32)]
    extra, extra_specs = list(before[:2]), [] if first else [whole(shape) for shape, _ in sums]
    if last:
        extra += [features] * images + list(before[2:])
        extra_specs += [pl.BlockSpec((1, tokens, channels), lambda h, j=j: (j, 0, 0)) for j in range(images)]
        extra_specs += [whole((1, padded, width))] * (images - 1)
    return pl.pallas_call(
        functools.partial(encode_back_kernel, tokens, images, first, last),
        grid=(HEADS,),
        in_specs=[
            pl.BlockSpec(memory_space=pltpu.SMEM), image_block, image_block, whole(norm.shape),
            pl.BlockSpec((1, 1, padded, padded), lambda h: (image, h, 0, 0)),
        ] + [image_block] * 6 + [whole(square.shape)] + extra_specs,
        out_specs=[whole(shape) for shape, _ in outs],
        out_shape=[jax.ShapeDtypeStruct(shape, kind) for shape, kind in outs],
        scratch_shapes=[pltpu.VMEM(shape, kind) for shape, kind in scratch + (sums if last else [])],
        compiler_params=pltpu.CompilerParams(vmem_limit_bytes=VMEM_LIMIT),
        name="encode_back",
    )(flip, dx1, s0, norm, probs, keyed, lowm, q, k, v, o, square, *extra)


def stack_heads(value):
    return jnp.concatenate([value * head_mask(value.shape[1], head) for head in range(HEADS)], axis=0)


def pick_heads(stacked):
    rows, width = stacked.shape[0] // HEADS, stacked.shape[1]
    lane = lax.broadcasted_iota(jnp.int32, (1, width), 1)
    out = stacked[0:rows]
    for head in range(1, HEADS):
        out = jnp.where(lane >= head * (width // HEADS), stacked[head * rows:(head + 1) * rows], out)
    return out


def soft_gap(gap):
    return SOFT * jnp.log(1.0 + jnp.exp(-jnp.abs(gap) * (1.0 / SOFT)))


def sigmoid(value):
    return 1.0 / (1.0 + jnp.exp(-value))


def axis_terms(center, size, target_center, target_size):
    low_one, high_one = center - size / 2, center + size / 2
    low_two, high_two = target_center - target_size / 2, target_center + target_size / 2
    low_gap, high_gap = low_one - low_two, high_one - high_two
    low_soft, high_soft = soft_gap(low_gap), soft_gap(high_gap)
    inner = (jnp.minimum(high_one, high_two) - high_soft) - (jnp.maximum(low_one, low_two) + low_soft)
    overlap = jnp.maximum(inner, 0.0) + soft_gap(inner)
    hull = (jnp.maximum(high_one, high_two) + high_soft) - (jnp.minimum(low_one, low_two) - low_soft)
    return overlap, hull, sigmoid(inner / SOFT), sigmoid(low_gap / SOFT), sigmoid(high_gap / SOFT)


def box_loss(box, target, mask, box_count):
    l1_sum = 0.0
    grads = []
    for one, two in zip(box, target):
        offset = (one - two) / SOFT_L1
        root = jnp.sqrt(offset * offset + 1.0)
        l1_sum = l1_sum + mask * (SOFT_L1 * (root - 1.0))
        grads.append(5.0 * offset / root)
    ow, hw, pw, lw, uw = axis_terms(box[0], box[2], target[0], target[2])
    oh, hh, ph, lh, uh = axis_terms(box[1], box[3], target[1], target[3])
    inter = ow * oh
    union = box[2] * box[3] + target[2] * target[3] - inter
    hull = hw * hh
    by_union, by_hull = 1.0 / union, 1.0 / hull
    giou = inter * by_union - (hull - union) * by_hull
    share = inter * by_union * by_union
    g_inter = by_union + share - by_hull
    g_area = by_hull - share
    g_hull = -union * by_hull * by_hull
    for axis, (other, hull_other, slope, low_s, high_s, size_other) in enumerate(
        ((oh, hh, pw, lw, uw, box[3]), (ow, hw, ph, lh, uh, box[2]))
    ):
        flow = g_inter * other * slope
        wide = g_hull * hull_other
        g_high = flow * (1.0 - high_s) + wide * high_s
        g_low = -flow * low_s - wide * (1.0 - low_s)
        grads[axis] = grads[axis] - 2.0 * (g_low + g_high)
        grads[axis + 2] = grads[axis + 2] - 2.0 * ((g_high - g_low) / 2 + g_area * size_other)
    value = jnp.sum((5.0 * l1_sum + 2.0 * mask * (1.0 - giou)) / box_count, axis=1, keepdims=True)
    return value, [grad * mask / box_count for grad in grads]


def middle_kernel(tokens, queries, classes, inverse, count_rows, flip_ref, x1_ref, sine_ref, norm_ref, got_ref, col_ref, row_ref,
                  dx1_ref, keepa_ref, senda_ref, keepb_ref, sendb_ref, loss_ref, box_ref,
                  dsq_ref, dnorm_ref, w_ref, head_ref, g0, total1, tall_g, tall_s, small_g, small_s, kin, vin, kk, vv, probs2, mixed2, dsum, dq2, dmix2):
    images, padded, width = x1_ref.shape
    depth = width // HEADS
    rows_feed = FIRST[0]
    chunks = BLOCKS * rows_feed // width
    per_chunk = BLOCKS // chunks
    many = images * padded
    qrows = round_up(queries, 128)
    factor = 1.0 / math.sqrt(depth)
    gain = lambda row: norm_ref[row:row + 1, :]
    dnorm_ref[...] = jnp.zeros_like(dnorm_ref)

    at = 4 * rows_feed
    for pair in range(5):
        for j, one in enumerate(unpair(got_ref[:, at + 16 * pair:at + 16 * pair + 16, :])):
            w_ref[2 * pair + j] = one.astype(BF16)
    at += 80
    head_one, found = unpair(got_ref[:, at:at + 16, :])
    head_ref[...] = head_one[:, 0:head_ref.shape[1]].astype(BF16)
    box_count = jnp.sum(found[:, 0:1], axis=0, keepdims=True) * (1.0 / count_rows)
    box_ref[...] = box_count
    content, place = [one[:, 0:qrows].T for one in unpair(got_ref[:, at + 16:at + 32, :])]

    def weights(which, layer, chunk):
        start = (2 * which + layer) * rows_feed
        return got_ref[pl.ds(chunk * per_chunk, per_chunk), start:start + rows_feed, :].reshape(width, width)

    flip = flip_ref[0] > 0
    out_a, out_b = (keepa_ref, senda_ref), (keepb_ref, sendb_ref)

    def put_feed(refs, layer, chunk, value):
        value = value.reshape(per_chunk // 2, 2, rows_feed, width)
        place = pl.ds(chunk * (per_chunk // 2), per_chunk // 2), slice(layer * rows_feed, (layer + 1) * rows_feed)
        refs[0][place] = jnp.where(flip, value[:, 1], value[:, 0])
        refs[1][place] = jnp.where(flip, value[:, 0], value[:, 1])

    def feed(layer, source, g_ref, s_ref, out_ref):
        def step(chunk, carry):
            value, slope = gelu_parts(nt(source, weights(0, layer, chunk)))
            value = value.astype(BF16)
            g_ref[chunk] = value
            s_ref[chunk] = slope.astype(BF16)
            out_ref[...] += nn(value, weights(1, layer, chunk))
            return carry
        lax.fori_loop(0, chunks, step, 0)

    def feed_back(layer, source_t, grad, grad_t, g_ref, s_ref, out_ref):
        def step(chunk, carry):
            dg = nt(grad, weights(1, layer, chunk)).astype(BF16)
            du = (dg.astype(F32) * s_ref[chunk].astype(F32)).astype(BF16)
            put_feed(out_b, layer, chunk, nn(grad_t, g_ref[chunk]).astype(BF16).T)
            put_feed(out_a, layer, chunk, nn(source_t, du).astype(BF16).T)
            out_ref[...] += nn(du, weights(0, layer, chunk))
            return carry
        lax.fori_loop(0, chunks, step, 0)

    x1 = x1_ref[...].reshape(many, width)
    total1[...] = x1
    feed(0, x1.astype(BF16), tall_g, tall_s, total1)
    unit1, scale1 = norm_parts(total1[...])
    x2 = unit1 * gain(1) + gain(7)
    for image in range(images):
        part = x2[image * padded:(image + 1) * padded]
        keyed = (part + sine_ref[...]).astype(BF16)
        lowm = part.astype(BF16)
        kin[image] = keyed
        vin[image] = lowm
        kk[image] = nn(keyed, w_ref[5]).astype(BF16)
        vv[image] = nn(lowm, w_ref[6]).astype(BF16)

    asked = (content + place).astype(BF16)
    lowc = content.astype(BF16)
    q1 = nn(asked, w_ref[0]).astype(BF16)
    k1 = nn(asked, w_ref[1]).astype(BF16)
    v1 = nn(lowc, w_ref[2]).astype(BF16)
    q1s = stack_heads(q1)
    p1 = masked_softmax(nt(q1s, k1), depth, queries)
    mix1 = pick_heads(nn(p1, v1))
    mix1b = mix1.astype(BF16)
    unit2, scale2 = norm_parts(content + nn(mix1b, w_ref[3]))
    t1 = unit2 * gain(2) + gain(8)

    asked2 = (t1 + place).astype(BF16)
    q2 = nn(asked2, w_ref[4]).astype(BF16)
    q2s = stack_heads(q2)

    def cross(image, carry):
        probs = masked_softmax(nt(q2s, kk[image]), depth, tokens)
        probs2[image] = probs
        mixed2[image] = pick_heads(nn(probs, vv[image]))
        return carry
    lax.fori_loop(0, images, cross, 0)
    rows = images * qrows
    mix2 = mixed2[...].reshape(rows, width)
    mix2b = mix2.astype(BF16)
    t1s = jnp.concatenate([t1] * images, axis=0)
    unit3, scale3 = norm_parts(t1s + nn(mix2b, w_ref[7]))
    t2 = unit3 * gain(3) + gain(9)

    t2b = t2.astype(BF16)
    g0[...] = t2
    feed(1, t2b, small_g, small_s, g0)
    unit4, scale4 = norm_parts(g0[...])
    t3 = unit4 * gain(4) + gain(10)
    unit5, scale5 = norm_parts(t3)
    out = (unit5 * gain(5) + gain(11)).astype(BF16)

    logits = nn(out, head_ref[...])
    lane = lax.broadcasted_iota(jnp.int32, logits.shape, 1)
    weight = col_ref[:, 0:1]
    label = col_ref[:, 1:2].astype(jnp.int32)
    kept = jnp.where(lane < classes, logits, -1e30)
    top = jnp.max(kept, axis=1, keepdims=True)
    powers = jnp.exp(kept - top)
    norm_sum = jnp.sum(powers, axis=1, keepdims=True)
    chosen = lane == label
    ce = top + jnp.log(norm_sum) - jnp.sum(jnp.where(chosen, logits, 0.0), axis=1, keepdims=True)
    ce_sum = jnp.sum(weight * ce, axis=0, keepdims=True)
    dlogits = ((weight * inverse) * (powers / norm_sum - jnp.where(chosen, 1.0, 0.0))).astype(BF16)

    b1, slope_one = gelu_parts(nn(out, w_ref[8]))
    b1 = b1.astype(BF16)
    b2, slope_two = gelu_parts(nn(b1, w_ref[9]))
    b2 = b2.astype(BF16)
    raw = nn(b2, head_ref[...]).T
    box = [sigmoid(raw[classes + j:classes + j + 1, :]) for j in range(4)]
    target = [row_ref[1 + j:2 + j, :] for j in range(4)]
    box_value, dbox = box_loss(box, target, row_ref[0:1, :], box_count)
    loss_ref[...] = ce_sum * inverse + box_value
    draw = jnp.concatenate([grad * one * (1.0 - one) for grad, one in zip(dbox, box)], axis=0)
    lanes_in = head_ref.shape[1]
    spot = lax.broadcasted_iota(jnp.int32, (lanes_in, rows), 0)
    spread = jnp.zeros((lanes_in, rows), F32)
    for j in range(4):
        spread = jnp.where(spot == classes + j, draw[j:j + 1, :], spread)
    draw_rows = spread.T.astype(BF16)

    dhead = tn(out, dlogits) + tn(b2, draw_rows)
    du2 = (nt(draw_rows, head_ref[...]) * slope_two).astype(BF16)
    dsq_ref[9] = tn(b1, du2)
    du1 = (nt(du2, w_ref[9]) * slope_one).astype(BF16)
    dsq_ref[8] = tn(out, du1)
    dout = nt(dlogits, head_ref[...]) + nt(du1, w_ref[8])

    def through(grad, unit, scale, row):
        dnorm_ref[row:row + 1, :] = column_sum(grad * unit)
        dnorm_ref[row + 6:row + 7, :] = column_sum(grad)
        return norm_back(grad, unit, scale, gain(row))

    dt3 = through(dout, unit5, scale5, 5)
    ds3 = through(dt3, unit4, scale4, 4)
    g0[...] = ds3
    ds3b = ds3.astype(BF16)
    feed_back(1, t2b.T, ds3b, ds3b.T, small_g, small_s, g0)
    ds2 = through(g0[...], unit3, scale3, 3)
    ds2b = ds2.astype(BF16)
    dsq_ref[7] = tn(mix2b, ds2b)
    dmix2[...] = nt(ds2b, w_ref[7]).astype(BF16).reshape(images, qrows, width)
    dq2[...] = jnp.zeros_like(dq2)
    dsum[...] = jnp.zeros_like(dsum)

    def attention_back(dmix, mix, probs, stacked_q, keys, values):
        dms = stack_heads(dmix)
        both = dmix.astype(F32) * mix
        weight = jnp.concatenate(
            [jnp.sum(both * head_mask(width, head).astype(F32), axis=1, keepdims=True) for head in range(HEADS)],
            axis=0,
        )
        dscores = (probs.astype(F32) * (nt(dms, values) - weight)).astype(BF16)
        dq = pick_heads(nn(dscores, keys)) * factor
        dk = (tn(stacked_q, dscores) * factor).astype(BF16).T
        dv = tn(dms, probs).astype(BF16).T
        return dq, dk, dv

    def cross_back(image, carry):
        dq, dk, dv = attention_back(dmix2[image], mixed2[image], probs2[image], q2s, kk[image], vv[image])
        dq2[...] += dq
        dsum[0] += tn(kin[image], dk)
        dsum[1] += tn(vin[image], dv)
        dx1_ref[image] = nt(dk, w_ref[5]) + nt(dv, w_ref[6])
        return carry
    lax.fori_loop(0, images, cross_back, 0)
    dsq_ref[5] = dsum[0]
    dsq_ref[6] = dsum[1]
    dq2b = dq2[...].astype(BF16)
    dsq_ref[4] = tn(asked2, dq2b)
    dasked2 = nt(dq2b, w_ref[4])
    dt1 = dasked2
    for image in range(images):
        dt1 = dt1 + ds2[image * qrows:(image + 1) * qrows]
    ds1 = through(dt1, unit2, scale2, 2)
    ds1b = ds1.astype(BF16)
    dsq_ref[3] = tn(mix1b, ds1b)
    dmix1 = nt(ds1b, w_ref[3]).astype(BF16)
    dq, dk, dv = attention_back(dmix1, mix1, p1, q1s, k1, v1)
    dqb = dq.astype(BF16)
    dsq_ref[0] = tn(asked, dqb)
    dsq_ref[1] = tn(asked, dk)
    dsq_ref[2] = tn(lowc, dv)
    dasked = nt(dqb, w_ref[0]) + nt(dk, w_ref[1])
    dquery = [ds1 + dasked + nt(dv, w_ref[2]), dasked + dasked2]

    unit, scale = norm_parts(total1[...])
    dx2 = dx1_ref[...].reshape(many, width)
    ds = through(dx2, unit, scale, 1)
    total1[...] = ds
    dsb = ds.astype(BF16)
    x1b = x1_ref[...].reshape(many, width).astype(BF16)
    feed_back(0, x1b.T, dsb, dsb.T, tall_g, tall_s, total1)
    dx1_ref[...] = total1[...].reshape(images, padded, width)

    wide = lambda value: jnp.concatenate([value, jnp.zeros((value.shape[0], width - value.shape[1]), F32)], axis=1)
    at = 2 * rows_feed
    for pair in range(3):
        put_blocks(out_a, flip, at + 16 * pair, pair_rows(dsq_ref[2 * pair], dsq_ref[2 * pair + 1]))
    for pair in range(2):
        put_blocks(out_b, flip, at + 16 * pair, pair_rows(dsq_ref[6 + 2 * pair], dsq_ref[7 + 2 * pair]))
    put_blocks(out_b, flip, at + 32, pair_rows(wide(dhead), norm_columns(dnorm_ref[...], width)))
    put_blocks(out_b, flip, at + 48, pair_rows(wide(dquery[0].T), wide(dquery[1].T)))


def middle(flip, x1, sine, norm, got, col, row, tokens, queries, classes, inverse, count_rows):
    images, padded, width = x1.shape
    qrows = round_up(queries, 128)
    chunks = BLOCKS * FIRST[0] // width
    many, rows = images * padded, images * qrows
    vmem = pl.BlockSpec(memory_space=pltpu.VMEM)
    shapes = [
        ((images, padded, width), F32), ((BLOCKS // 2, sum(PART_A), width), BF16),
        ((BLOCKS // 2, sum(PART_A), width), BF16), ((BLOCKS // 2, sum(PART_B), width), BF16),
        ((BLOCKS // 2, sum(PART_B), width), BF16), ((1, 1), F32), ((1, 1), F32),
    ]
    return pl.pallas_call(
        functools.partial(middle_kernel, tokens, queries, classes, inverse, count_rows),
        in_specs=[pl.BlockSpec(memory_space=pltpu.SMEM)] + [vmem] * 6,
        out_specs=[vmem] * len(shapes),
        out_shape=[jax.ShapeDtypeStruct(shape, kind) for shape, kind in shapes],
        scratch_shapes=[
            pltpu.VMEM((10, width, width), F32), pltpu.VMEM((16, width), F32),
            pltpu.VMEM((10, width, width), BF16), pltpu.VMEM((width, 128), BF16),
            pltpu.VMEM((rows, width), F32), pltpu.VMEM((many, width), F32),
            pltpu.VMEM((chunks, many, width), BF16), pltpu.VMEM((chunks, many, width), BF16),
            pltpu.VMEM((chunks, rows, width), BF16), pltpu.VMEM((chunks, rows, width), BF16),
            pltpu.VMEM((images, padded, width), BF16), pltpu.VMEM((images, padded, width), BF16),
            pltpu.VMEM((images, padded, width), BF16), pltpu.VMEM((images, padded, width), BF16),
            pltpu.VMEM((images, HEADS * qrows, padded), BF16), pltpu.VMEM((images, qrows, width), F32),
            pltpu.VMEM((2, width, width), F32), pltpu.VMEM((qrows, width), F32),
            pltpu.VMEM((images, qrows, width), BF16),
        ],
        compiler_params=pltpu.CompilerParams(vmem_limit_bytes=VMEM_LIMIT),
        name="middle",
    )(flip, x1, sine, norm, got, col, row)


def sine_table(width, padded):
    cells = np.arange(SIDE * SIDE)
    half = width // 2
    index = np.arange(half)
    freqs = 10000.0 ** ((2 * (index // 2)) / half)
    parts = []
    for coord in (cells // SIDE + 1, cells % SIDE + 1):
        angle = (coord / (SIDE + 1e-06) * (2.0 * math.pi))[:, None] / freqs[None, :]
        parts.append(np.where(index[None, :] % 2 == 0, np.sin(angle), np.cos(angle)))
    table = np.concatenate(parts, axis=1).astype(np.float32)
    return np.concatenate([table, np.zeros((padded - table.shape[0], width), np.float32)], axis=0)


def round_up(value, unit):
    return -(-value // unit) * unit


def target_info(matches, labels, boxes, classes, qrows):
    images, queries = matches.shape
    pad = ((0, 0), (0, qrows - queries))
    matched = matches >= 0
    picker = matches[:, :, None] == jnp.arange(labels.shape[1])[None, None, :]
    label = jnp.where(matched, jnp.sum(jnp.where(picker, labels[:, None, :], 0), axis=2), classes - 1)
    weight = jnp.pad(jnp.where(matched, 1.0, NO_OBJECT), pad)
    label = jnp.pad(label, pad).astype(F32)
    col = jnp.stack([weight.reshape(-1), label.reshape(-1)], axis=1)
    mask = jnp.pad(matched.astype(F32), pad).reshape(1, -1)
    wanted = []
    for j in range(4):
        one = jnp.sum(jnp.where(picker, boxes[:, None, :, j], 0.0), axis=2)
        wanted.append(jnp.pad(jnp.where(matched, one, 0.5), pad, constant_values=0.5).reshape(1, -1))
    row = jnp.concatenate([mask] + wanted + [jnp.zeros((3, mask.shape[1]), F32)], axis=0)
    return col, row


AXES = ("dp", "fsdp")


def swap(value, bit, devices):
    return lax.ppermute(value, AXES, [(i, i ^ bit) for i in range(devices)])


def bits_of(devices):
    return [1 << j for j in range(devices.bit_length() - 1)]


def gather_rows(value, devices, beside):
    me = lax.axis_index(AXES)
    held = value[None]
    done = []
    for at, bit in enumerate(reversed(bits_of(devices))):
        if at in beside:
            held, ready = lax.optimization_barrier((held, beside[at]))
            done.append(ready)
        other = swap(held, bit, devices)
        mine = (me & bit) == 0
        held = jnp.where(mine, jnp.concatenate([held, other]), jnp.concatenate([other, held]))
    return held, done


def reverse_bits(index, count):
    return sum(((index >> j) & 1) << (count - 1 - j) for j in range(count))


def join(got, pieces):
    ratio = got.shape[0] // BLOCKS
    if ratio == 1:
        return got
    got = got.reshape(BLOCKS, ratio, got.shape[1], got.shape[2])
    out, at = [], 0
    for piece in pieces:
        rows = piece // ratio
        out.append(got[:, :, at:at + rows].reshape(BLOCKS, piece, got.shape[3]))
        at += rows
    return jnp.concatenate(out, axis=1)


def launch(keep, send, pieces, devices):
    bits = bits_of(devices)
    ratio = devices // BLOCKS
    tail = keep.shape[1:]
    if ratio == 1:
        shape = (2,) * (len(bits) - 1) + tail
        return swap(send, bits[0], devices).reshape(shape), keep.reshape(shape), list(reversed(bits[1:]))
    value = jnp.stack([keep, send], axis=1).reshape((BLOCKS,) + tail)
    out, at = [], 0
    for piece in pieces:
        out.append(value[:, at:at + piece].reshape(devices, piece // ratio, tail[1]))
        at += piece
    out = jnp.concatenate(out, axis=1)
    out = out.reshape((2,) * len(bits) + out.shape[1:])
    left = list(reversed(bits))
    return advance((jnp.zeros_like(out), out, left), bits[0], devices)


def halves(flight, bit):
    came, kept, left = flight
    axis = left.index(bit)
    mine = (lax.axis_index(AXES) // bit) % 2
    pick = lambda value, at: lax.dynamic_index_in_dim(value, at, axis, keepdims=False).astype(F32)
    out = (pick(kept, 1 - mine) + pick(came, 1 - mine)).astype(BF16)
    return out, pick(kept, mine) + pick(came, mine), [one for one in left if one != bit]


def advance(flight, bit, devices):
    out, kept, left = halves(flight, bit)
    return swap(out, bit, devices), kept, left


def merge(one, two):
    return tuple(jnp.concatenate([a, b], axis=-2) for a, b in zip(one[:2], two[:2])) + (one[2],)


def exact(left, right, dims=((1,), (0,))):
    return lax.dot_general(left, right, (dims, ((), ())), precision=lax.Precision.HIGHEST, preferred_element_type=F32)


def gram_kernel(mom_ref, grad_ref, x_ref, gram_ref, sums_ref):
    slot = mom_ref.shape[1]
    devices, _, width = grad_ref.shape
    sums = jnp.sum(grad_ref[:, slot:, :].astype(F32), axis=0)
    sums_ref[...] = sums
    squares = jnp.sum(sums[0:1, 0:3], axis=1, keepdims=True)
    factor = jnp.minimum(1.0, CLIP / (jnp.sqrt(squares) + 1e-06))
    x = BETA_M * mom_ref[...].astype(F32) + factor * grad_ref[:, :slot, :].astype(F32)
    x = x.reshape(devices * slot, width)
    x_ref[...] = x
    gram_ref[...] = exact(x, x, ((0,), (0,)))


def rough(left, right):
    left_high, right_high = left.astype(BF16), right.astype(BF16)
    left_low = (left - left_high.astype(F32)).astype(BF16)
    right_low = (right - right_high.astype(F32)).astype(BF16)
    return nn(left_high, right_high) + (nn(left_high, right_low) + nn(left_low, right_high))


def polish_kernel(x_ref, gram_ref, came_ref, out_ref):
    gram = gram_ref[...] + came_ref[...]
    diagonal = lax.broadcasted_iota(jnp.int32, gram.shape, 0) == lax.broadcasted_iota(jnp.int32, gram.shape, 1)
    eye = jnp.where(diagonal, 1.0, 0.0)
    square = jnp.sum(jnp.sum(gram * eye, axis=1, keepdims=True), axis=0, keepdims=True)
    scale = 1.0 / (jnp.sqrt(square) + 1e-07)
    gram = gram * (scale * scale)
    total = None
    for sweep in range(5):
        product = exact if sweep < 2 else rough
        poly = NS_A * eye + NS_B * gram + NS_C * product(gram, gram)
        total = poly if sweep == 0 else product(total, poly)
        if sweep < 4:
            gram = product(product(poly, gram), poly)
    out = rough(x_ref[...] * scale, total)
    out_ref[...] = out.reshape(out_ref.shape).astype(out_ref.dtype)


def plain_call(body, shapes, *args):
    vmem = pl.BlockSpec(memory_space=pltpu.VMEM)
    return pl.pallas_call(
        body,
        in_specs=[vmem] * len(args),
        out_specs=[vmem] * len(shapes),
        out_shape=[jax.ShapeDtypeStruct(shape, kind) for shape, kind in shapes],
        compiler_params=pltpu.CompilerParams(vmem_limit_bytes=VMEM_LIMIT),
        name=body.__name__,
    )(*args)


def to_slots(square, feeds, devices):
    count, rows, width = square.shape
    slot = feeds.shape[1] // 4
    feed_slots = feeds.reshape(feeds.shape[0] * 4, slot, width)
    square_slots = jnp.pad(square, ((0, devices - count - feed_slots.shape[0]), (0, slot - rows), (0, 0)))
    return jnp.concatenate([feed_slots, square_slots], axis=0)


def exchange(slots):
    return lax.all_to_all(slots, AXES, split_axis=0, concat_axis=0, tiled=True)


def adam(weight, first, second, gradient, rate, decay):
    first = ADAM_B1 * first + (1.0 - ADAM_B1) * gradient
    second = ADAM_B2 * second + (1.0 - ADAM_B2) * gradient * gradient
    fixed_first = first / (1.0 - ADAM_B1**STEP)
    fixed_second = second / (1.0 - ADAM_B2**STEP)
    weight = weight * (1.0 - rate * decay) - rate * fixed_first / (jnp.sqrt(fixed_second) + 1e-08)
    return weight, first, second, weight.astype(BF16)


def muon(weight, ortho, longest):
    fresh = weight * (1.0 - LR_M * DECAY_M) - LR_M * 0.2 * math.sqrt(longest) * ortho
    return fresh, fresh.astype(BF16)


def pack_kernel(win_ref, sq_ref, ex_ref, re_ref, head_ref, query_ref, norm_ref, matches_ref, one_ref, two_ref):
    one, two = pack(win_ref[...], sq_ref[...], ex_ref[...], re_ref[...], head_ref[...], query_ref[...], norm_ref[...],
                    matches_ref[...])
    one_ref[...] = one
    two_ref[...] = two


def pack(win, sq, ex, re, head, query, norm, matches):
    width = win.shape[1]
    rows = sq.shape[1]
    wide = lambda value: jnp.concatenate([value, jnp.zeros((value.shape[0], width - value.shape[1]), F32)], axis=1)
    flat = lambda value: [value[j] for j in range(value.shape[0])]
    found = jnp.where(matches >= 0, 1.0, 0.0)
    found = jnp.sum(jnp.sum(found, axis=1, keepdims=True), axis=0, keepdims=True)
    one = [win] + flat(sq[:4]) + [wide(norm), jnp.zeros((rows, width), F32)]
    two = flat(ex) + flat(re) + flat(sq[4:]) + [wide(head), jnp.broadcast_to(found, (rows, width))]
    two = two + [wide(query[0]), wide(query[1])]
    return jnp.concatenate(one).astype(BF16), jnp.concatenate(two).astype(BF16)


def per_device(devices, features, matches, target_labels, target_boxes,
               square_weight, square_momentum, expand_weight, expand_momentum, reduce_weight, reduce_momentum,
               input_weight, input_momentum, input_second, head_weight, head_momentum, head_second,
               query_weight, query_momentum, query_second, norm_weight, norm_momentum, norm_second):
    images, tokens, channels = features.shape
    count, rs, width = square_weight.shape
    pairs, _, rf = expand_weight.shape
    ri = input_weight.shape[0]
    rh, head_lanes = head_weight.shape
    _, queries, rq = query_weight.shape
    norms, rn = norm_weight.shape
    classes = head_lanes - 4
    padded, qrows = round_up(tokens, 128), round_up(queries, 128)
    hidden = rf * devices
    aligned = devices == BLOCKS
    steps = len(bits_of(devices))

    shards = (input_weight, square_weight, jnp.transpose(expand_weight, (0, 2, 1)), reduce_weight, head_weight,
              jnp.transpose(query_weight, (0, 2, 1)), norm_weight.T, matches)
    if aligned:
        first, second = plain_call(
            pack_kernel, [((sum(FIRST), width), BF16), ((sum(SECOND), width), BF16)], *shards)
    else:
        first, second = lax.optimization_barrier(pack(*shards))
    got_two = join(lax.all_gather(second, AXES, axis=0, tiled=False), SECOND)
    sine = jnp.asarray(sine_table(width, padded))
    laid = with_layout_constraint(features, Layout(major_to_minor=(0, 1, 2)))
    info = target_info(matches, target_labels, target_boxes, classes, qrows)
    got_one, (laid, (col, row)) = gather_rows(first, devices, {TIE[0]: laid, TIE[1]: info})
    order = [reverse_bits(block, steps) for block in range(BLOCKS)]
    if not aligned:
        got_one = join(jnp.stack([got_one[reverse_bits(j, steps)] for j in range(devices)]), FIRST)
        order = list(range(BLOCKS))

    expand_momentum_t = jnp.transpose(expand_momentum, (0, 2, 1))
    mom_slots = to_slots(
        square_momentum, jnp.concatenate([expand_momentum_t, reduce_momentum]), devices).astype(BF16)
    mom_in = exchange(mom_slots)

    inverse = 1.0 / (images * devices * queries)
    probs, keyed, lowm, q, k, v, o, s0, x1, sq_one, norm_all = encode(laid, got_one, order, sine)
    bits = bits_of(devices)
    flip = (lax.axis_index(AXES) % 2 if aligned else jnp.zeros((), jnp.int32)).reshape(1)
    dx1, keep_a, send_a, keep_b, send_b, loss, box_total = middle(
        flip, x1, sine, norm_all, got_two, col, row, tokens, queries, classes, inverse, rs)

    near, far = bits[1], bits[2]
    turns = [(near, far), (far, near)]
    flight_a, flight_b = launch(keep_a, send_a, PART_A, devices), launch(keep_b, send_b, PART_B, devices)
    sums = ()
    for image in range(images):
        if image and turns:
            half_a, half_b = [halves(flight, bit) for flight, bit in zip((flight_a, flight_b), turns.pop(0))]
            sums, (out_a, out_b) = lax.optimization_barrier((sums, (half_a[0], half_b[0])))
            flight_a = (swap(out_a, near, devices),) + half_a[1:]
            flight_b = (swap(out_b, far, devices),) + half_b[1:]
        sums = encode_back(
            image, images, flip, dx1, s0, norm_all, probs, keyed, lowm, q, k, v, o, sq_one, laid, *sums)
    flight_c = launch(*sums, PART_C, devices)
    for bit_a, bit_b in turns:
        flight_a, flight_b = advance(flight_a, bit_a, devices), advance(flight_b, bit_b, devices)
    rest = [bit for bit in bits if bit not in (bits[0], near, far)]
    turns_c = [far, near] + rest
    flight_ab = merge(flight_a, flight_b)
    for bit in rest:
        flight_ab = advance(flight_ab, bit, devices)
        flight_c = advance(flight_c, turns_c.pop(0), devices)
    for bit in turns_c:
        flight_c = advance(flight_c, bit, devices)

    rows_ab, rows_c = sum(PART_A + PART_B) * BLOCKS // devices, sum(PART_C) * BLOCKS // devices
    slot = rf // 4
    ready = (flight_ab[0], flight_ab[1], flight_c[0], flight_c[1], loss)
    shapes = [((rows_ab, width), F32), ((rows_c, width), F32), ((devices, slot + 8, width), BF16)]
    if aligned:
        sum_ab, sum_c, grad_slots = plain_call(prepare_kernel, shapes, *ready)
    else:
        sum_ab, sum_c, grad_slots = prepare(*ready, devices, lambda value: lax.reduce_precision(value, 8, 7))
    grad_in = exchange(grad_slots)
    x, gram, sums = plain_call(
        gram_kernel, [((devices * slot, width), F32), ((width, width), F32), ((8, width), F32)], mom_in, grad_in)
    feeds = 8 * pairs
    gram = gram + lax.ppermute(gram, AXES, [(i, i ^ 1) for i in range(feeds)])
    came = lax.ppermute(gram, AXES, [(i, i ^ 2) for i in range(feeds)])
    back = exchange(plain_call(polish_kernel, [((devices, slot, width), BF16)], x, gram, came)[0])

    turn = lambda value: jnp.transpose(value, (0, 2, 1))
    states = (square_momentum, expand_momentum_t, reduce_momentum,
              input_weight, input_momentum, input_second, head_weight, head_momentum, head_second,
              turn(query_weight), turn(query_momentum), turn(query_second),
              norm_weight.T, norm_momentum.T, norm_second.T)
    weights = (square_weight, turn(expand_weight), reduce_weight)
    if aligned:
        like = lambda value, kind: (value.shape, kind)
        shapes = [like(value, F32) for value in states[:3]]
        for value in states[3::3]:
            shapes += [like(value, F32)] * 3 + [like(value, BF16)]
        new = plain_call(adapt_kernel, shapes + [((1, 1), F32)] * 2, sum_ab, sum_c, sums, *states)
        shapes = [like(value, kind) for value in weights for kind in (F32, BF16)]
        fresh = plain_call(apply_kernel, shapes, back, *weights)
    else:
        new = adapt(sum_ab, sum_c, sums, *states)
        fresh = apply(back, hidden, *weights)
    square_mom, expand_mom, reduce_mom = new[:3]
    query_out = [turn(value) for value in new[11:15]]
    norm_out = [value.T for value in new[15:19]]
    return (
        (fresh[0], square_mom, fresh[1], turn(fresh[2]), turn(expand_mom), turn(fresh[3]),
         fresh[4], reduce_mom, fresh[5]) + tuple(new[3:11]) + tuple(query_out) + tuple(norm_out)
        + (new[19].reshape(()), box_total.reshape(()), new[20].reshape(()))
    )


def row_parts(sum_ab, sum_c):
    rf = sum_c.shape[0] * PART_C[0] // sum(PART_C)
    rs = rf // 8
    cut = lambda value, start, rows: value[start:start + rows]
    half = 2 * rf + 6 * rs
    feeds = [cut(sum_ab, j * rf, rf) for j in range(2)] + [cut(sum_ab, half + j * rf, rf) for j in range(2)]
    squares = [cut(sum_c, rf + j * rs, rs) for j in range(4)]
    squares += [cut(sum_ab, 2 * rf + j * rs, rs) for j in range(6)]
    at = half + 2 * rf
    squares += [cut(sum_ab, at + j * rs, rs) for j in range(4)]
    head, norm, content, place = [cut(sum_ab, at + (4 + j) * rs, rs) for j in range(4)]
    norm = norm + cut(sum_c, rf + 4 * rs, rs)
    return feeds, squares, cut(sum_c, 0, rf), head, [content, place], norm


def prepare(came_ab, kept_ab, came_c, kept_c, loss, devices, low):
    sum_ab = kept_ab.astype(F32) + came_ab.astype(F32)
    sum_c = kept_c.astype(F32) + came_c.astype(F32)
    width = sum_ab.shape[1]
    total = sum(
        jnp.sum(jnp.sum(value * value, axis=0, keepdims=True), axis=1, keepdims=True) for value in (sum_ab, sum_c))
    spot = [lax.broadcasted_iota(jnp.int32, (8, width), axis) for axis in (0, 1)]
    numbers = jnp.zeros((8, width), F32)
    for row, value in enumerate((total, loss)):
        for lane in range(3):
            high = low(value)
            numbers = jnp.where(jnp.logical_and(spot[0] == row, spot[1] == lane), high, numbers)
            value = value - high
    feeds, squares, _, _, _, _ = row_parts(sum_ab, sum_c)
    slot = feeds[0].shape[0] // 4
    rs = squares[0].shape[0]
    none = jnp.zeros((slot - rs, width), F32)
    spare = [jnp.zeros((slot, width), F32)] * (devices - 16 - len(squares))
    slots = [feed[j * slot:(j + 1) * slot] for feed in feeds for j in range(4)]
    slots += [jnp.concatenate([square, none]) for square in squares] + spare
    slots = jnp.stack([jnp.concatenate([one, numbers]) for one in slots])
    return sum_ab, sum_c, slots.astype(BF16)


def prepare_kernel(came_ab, kept_ab, came_c, kept_c, loss, sum_ab, sum_c, slots):
    sum_ab[...], sum_c[...], slots[...] = prepare(
        came_ab[...], kept_ab[...], came_c[...], kept_c[...], loss[...], slots.shape[0],
        lambda value: value.astype(BF16).astype(F32))


def adapt(sum_ab, sum_c, sums, square_mom, expand_mom, reduce_mom, *states):
    feeds, squares, win, head, query, norm = row_parts(sum_ab, sum_c)
    lane = lax.broadcasted_iota(jnp.int32, (1, sums.shape[1]), 1)
    total, loss = [jnp.sum(jnp.where(lane < 3, sums[j:j + 1, :], 0.0), axis=1, keepdims=True) for j in range(2)]
    size = jnp.sqrt(total)
    factor = jnp.minimum(1.0, CLIP / (size + 1e-06))
    out = [BETA_M * square_mom + factor * jnp.stack(squares),
           BETA_M * expand_mom + factor * jnp.stack(feeds[:2]),
           BETA_M * reduce_mom + factor * jnp.stack(feeds[2:])]
    query = jnp.stack([one[:, :states[6].shape[2]] for one in query])
    grads = (win, head[:, :states[3].shape[1]], query, norm[:, :states[9].shape[1]])
    for j, (grad, rate, decay) in enumerate(zip(grads, (0.04, 0.1, 0.5, 0.5), (0.0001, 0.0001, 0.0, 0.0))):
        out += adam(*states[3 * j:3 * j + 3], factor * grad, rate, decay)
    return out + [loss, size]


def adapt_kernel(*refs):
    count = 18
    for ref, value in zip(refs[count:], adapt(*[ref[...] for ref in refs[:count]])):
        ref[...] = value


def apply(back, hidden, square, expand, reduce):
    slot = back.shape[1]
    rf = 4 * slot
    rs = square.shape[1]
    feed = back[:16].astype(F32).reshape(4, rf, back.shape[2])
    ortho = back[16:16 + square.shape[0]].astype(F32)[:, :rs]
    return muon(square, ortho, square.shape[2]) + muon(expand, feed[:2], hidden) + muon(reduce, feed[2:], hidden)


def apply_kernel(back, square, expand, reduce, *outs):
    hidden = back.shape[0] * expand.shape[1]
    for ref, value in zip(outs, apply(back[...], hidden, square[...], expand[...], reduce[...])):
        ref[...] = value


def solution(mesh):
    both = ("dp", "fsdp")
    first = [P(both), P(both), P(both), P(both)]
    square, expand, reduce = P(None, both), P(None, None, both), P(None, both)
    rows, query, norm = P(both), P(None, None, both), P(None, both)
    in_specs = tuple(first + [square] * 2 + [expand] * 2 + [reduce] * 2 + [rows] * 6 + [query] * 3 + [norm] * 3)
    out_specs = tuple([square] * 3 + [expand] * 3 + [reduce] * 3 + [rows] * 8 + [query] * 4 + [norm] * 4 + [P()] * 3)
    return jax.shard_map(
        functools.partial(per_device, mesh.size), mesh=mesh, in_specs=in_specs, out_specs=out_specs, check_vma=False)
```

```python
import functools
import math

import jax
import jax.numpy as jnp
import numpy as np
from jax import lax
from jax.experimental import pallas as pl
from jax.experimental.layout import Layout, with_layout_constraint
from jax.experimental.pallas import tpu as pltpu
from jax.sharding import PartitionSpec as P

HEADS = 8
SIDE = 25
STEP = 10
NS_A = 3.4445
NS_B = -4.775
NS_C = 2.0315
CLIP = 0.02
BETA_M = 0.95
LR_M = 0.3
DECAY_M = 0.01
ADAM_B1 = 0.9
ADAM_B2 = 0.999
SOFT = 0.02
SOFT_L1 = 0.05
NO_OBJECT = 0.1
EPS = 1e-05
LOG2E = math.log2(math.e)
F32 = jnp.float32
BF16 = jnp.bfloat16
VMEM_LIMIT = 56 * 1024 * 1024


def cost(micros):
    return pl.CostEstimate(flops=int(micros * 1.1e9), bytes_accessed=int(micros * 3.5e6), transcendentals=0)


def nn(left, right):
    return lax.dot_general(left, right, (((1,), (0,)), ((), ())), preferred_element_type=F32)


def nt(left, right):
    return lax.dot_general(left, right, (((1,), (1,)), ((), ())), preferred_element_type=F32)


def tn(left, right):
    return lax.dot_general(left, right, (((0,), (0,)), ((), ())), preferred_element_type=F32)


BLOCKS = 32
FIRST = (64, 8, 8, 8, 8, 8, 8)
SECOND = (64,) * 4 + (8,) * 14
PART_A = (64, 64) + (8,) * 6
PART_B = (64, 64) + (8,) * 8
PART_C = (64,) + (8,) * 6


def by_core(value):
    rows = value.shape[0] // BLOCKS
    value = value.reshape(BLOCKS // 2, 2, rows, value.shape[1])
    return value[:, 0], value[:, 1]


def pair_rows(one, two):
    width = one.shape[1]
    both = [part.reshape(BLOCKS, part.shape[0] // BLOCKS, width) for part in (one, two)]
    return jnp.concatenate(both, axis=1).reshape(2 * one.shape[0], width)


def unpair(both):
    both = both.astype(F32)
    half = both.shape[1] // 2
    return [both[:, j * half:(j + 1) * half].reshape(BLOCKS * half, both.shape[2]) for j in range(2)]


def block_rows(me, block, start, count, got_ref, other_ref):
    far = me ^ block
    place = ((far >> 1) & 3) * 4 + (far >> 3)
    cut = slice(start, start + count)
    return jnp.where((far & 1) == 0, got_ref[place, cut, :], other_ref[place, cut, :])


def all_rows(me, start, got_ref, other_ref):
    return jnp.stack([block_rows(me, block, start, 16, got_ref, other_ref) for block in range(BLOCKS)])


def put_blocks(refs, flip, start, value):
    rows = value.shape[0] // BLOCKS
    even, odd = by_core(value)
    refs[0][:, start:start + rows, :] = jnp.where(flip, odd, even).astype(BF16)
    refs[1][:, start:start + rows, :] = jnp.where(flip, even, odd).astype(BF16)


def head_mask(width, head):
    lane = lax.broadcasted_iota(jnp.int32, (1, width), 1)
    depth = width // HEADS
    return jnp.logical_and(lane >= head * depth, lane < (head + 1) * depth).astype(F32).astype(BF16)


def norm_parts(total):
    center = total - jnp.mean(total, axis=-1, keepdims=True)
    spread = jnp.mean(center * center, axis=-1, keepdims=True)
    scale = lax.rsqrt(spread + EPS)
    return center * scale, scale


def norm_back(grad, unit, scale, gain):
    inner = grad * gain
    mean_inner = jnp.mean(inner, axis=-1, keepdims=True)
    mean_cross = jnp.mean(inner * unit, axis=-1, keepdims=True)
    return scale * (inner - mean_inner - unit * mean_cross)


def column_sum(value):
    return jnp.sum(value, axis=0, keepdims=True)


GELU_C = math.sqrt(2.0 / math.pi)
GELU_K = 0.044715 * GELU_C


def gelu_parts(value):
    square = value * value
    half = 0.5 + 0.5 * jnp.tanh(value * (GELU_C + GELU_K * square))
    out = value * half
    slope = half + out * (1.0 - half) * (2.0 * GELU_C + 6.0 * GELU_K * square)
    return out, slope


def masked_softmax(scores, depth, length):
    padded = scores.shape[1]
    start = (padded - 1) // 128 * 128
    if length < padded:
        scores = scores + jnp.where(lax.broadcasted_iota(jnp.int32, (1, padded), 1) < length, 0.0, -1e30)
    factor = LOG2E / math.sqrt(depth)
    top = jnp.max(scores, axis=1, keepdims=True)
    powers = jnp.exp2((scores - top) * factor)
    inverse = 1.0 / jnp.sum(powers, axis=1, keepdims=True)
    return (powers * inverse).astype(BF16)


def encode_kernel(tokens, me_ref, f_ref, got_ref, other_ref, sine_ref,
                  p_ref, keyed_ref, lowm_ref, q_ref, k_ref, v_ref, o_ref, s0_ref, x1_ref, w_ref, norm_ref, win_ref, k_t):
    head = pl.program_id(1)
    width = got_ref.shape[2]

    @pl.when(jnp.logical_and(pl.program_id(0) == 0, head == 0))
    def _():
        rows = FIRST[0]

        sources = (got_ref, other_ref)
        for block in range(BLOCKS):
            win_ref[block * rows:(block + 1) * rows, :] = block_rows(me_ref[0], block, 0, rows, *sources)
        for pair in range(2):
            for j, one in enumerate(unpair(all_rows(me_ref[0], rows + 16 * pair, *sources))):
                w_ref[2 * pair + j] = one.astype(BF16)
        norm_ref[...] = unpair(all_rows(me_ref[0], rows + 32, *sources))[0][:, 0:128].T[0:norm_ref.shape[0], :]

    @pl.when(head == 0)
    def _():
        padded = s0_ref.shape[1]
        s0_ref[0, tokens // 8 * 8:padded, :] = jnp.zeros((padded - tokens // 8 * 8, width), F32)
        s0_ref[0, 0:tokens, :] = nn(f_ref[0], win_ref[...])
        memory = s0_ref[0]
        keyed = (memory + sine_ref[...]).astype(BF16)
        lowm = memory.astype(BF16)
        keyed_ref[0] = keyed
        lowm_ref[0] = lowm
        q_ref[0] = nn(keyed, w_ref[0]).astype(BF16)
        keys = nn(keyed, w_ref[1]).astype(BF16)
        k_ref[0] = keys
        k_t[...] = keys.T
        v_ref[0] = nn(lowm, w_ref[2]).astype(BF16)
        o_ref[...] = jnp.zeros_like(o_ref)

    for at in range(4):
        mask = head_mask(width, head * 4 + at)
        vm = v_ref[0] * mask
        for start in range(0, q_ref.shape[1], 320):
            cut = slice(start, start + 320)
            scores = nn(q_ref[0, cut, :] * mask, k_t[...])
            probs = masked_softmax(scores, width // HEADS, tokens)
            p_ref[0, at, cut, :] = probs
            o_ref[0, cut, :] += nn(probs, vm)

    @pl.when(head == HEADS // 4 - 1)
    def _():
        total = s0_ref[0] + nn(o_ref[0].astype(BF16), w_ref[3])
        s0_ref[0] = total
        unit, scale = norm_parts(total)
        x1_ref[0] = unit * norm_ref[0:1, :] + norm_ref[6:7, :]


def encode(features, me, got, other, sine):
    images, tokens, depth = features.shape
    width = got.shape[2]
    padded = sine.shape[0]
    per_image = lambda kind: jax.ShapeDtypeStruct((images, padded, width), kind)
    image_block = pl.BlockSpec((1, padded, width), lambda i, h: (i, 0, 0))
    whole = lambda shape: pl.BlockSpec(shape, lambda i, h: (0,) * len(shape))
    return pl.pallas_call(
        functools.partial(encode_kernel, tokens),
        grid=(images, HEADS // 4),
        in_specs=[
            pl.BlockSpec(memory_space=pltpu.SMEM), pl.BlockSpec((1, tokens, depth), lambda i, h: (i, 0, 0)),
            whole(got.shape), whole(other.shape), whole(sine.shape),
        ],
        out_specs=[pl.BlockSpec((1, 4, padded, padded), lambda i, h: (i, h, 0, 0))] + [image_block] * 8
        + [whole((4, width, width)), whole((16, width))],
        out_shape=[jax.ShapeDtypeStruct((images, HEADS, padded, padded), BF16)]
        + [per_image(BF16)] * 5 + [per_image(F32)] * 3
        + [jax.ShapeDtypeStruct((4, width, width), BF16), jax.ShapeDtypeStruct((16, width), F32)],
        scratch_shapes=[pltpu.VMEM((depth, width), BF16), pltpu.VMEM((width, padded), BF16)],
        compiler_params=pltpu.CompilerParams(vmem_limit_bytes=VMEM_LIMIT),
        cost_estimate=cost(22),
        name="encode",
    )(me, features, got, other, sine)


def encode_back_kernel(tokens, images, first, last, *refs):
    (me_ref, dx1_ref, s0_ref, norm_ref, p_ref, keyed_ref, lowm_ref, q_ref, k_ref, v_ref, o_ref, w_ref), refs = (
        refs[:12], refs[12:])
    if not first:
        (dsq_in, dnorm_in), refs = refs[:2], refs[2:]
    if last:
        f_refs, refs = refs[:images], refs[images:]
        dm_refs, refs = refs[:images - 1], refs[images - 1:]
        outs, refs = refs[:2], refs[2:]
        *refs, dsq, dnorm_ref = refs
    else:
        (dsq, dnorm_ref, dm_ref), refs = refs[:3], refs[3:]
    ds0, dout, dout_t, q_t, v_t, cross, dq, dk_t, dv_t = refs
    head = pl.program_id(0)
    width = w_ref.shape[1]
    depth = width // HEADS

    @pl.when(head == 0)
    def _():
        dsq[...] = jnp.zeros_like(dsq) if first else dsq_in[...]
        dnorm_ref[...] = jnp.zeros_like(dnorm_ref) if first else dnorm_in[...]

    @pl.when(head == 0)
    def _():
        unit, scale = norm_parts(s0_ref[0])
        grad = dx1_ref[0]
        dnorm_ref[0:1, :] += column_sum(grad * unit)
        dnorm_ref[6:7, :] += column_sum(grad)
        dtotal = norm_back(grad, unit, scale, norm_ref[0:1, :])
        ds0[...] = dtotal
        low = dtotal.astype(BF16)
        dsq[3] += tn(o_ref[0].astype(BF16), low)
        dmixed = nt(low, w_ref[3]).astype(BF16)
        dout[...] = dmixed
        dout_t[...] = dmixed.T
        q_t[...] = q_ref[0].T
        v_t[...] = v_ref[0].T
        cross[...] = dmixed.astype(F32) * o_ref[0]
        dq[...] = jnp.zeros_like(dq)

    for at in range(4):
        one = head * 4 + at
        mask = head_mask(width, one)
        rows = pl.ds(pl.multiple_of(one * depth, depth), depth)
        weight = jnp.sum(cross[...] * mask.astype(F32), axis=1, keepdims=True)
        probs = p_ref[0, at]
        dprobs = nn(dout[...] * mask, v_t[...])
        dscores = (probs.astype(F32) * (dprobs - weight)).astype(BF16)
        dq[...] += nn(dscores, k_ref[0] * mask)
        dk_t[rows, :] = nn(q_t[rows, :], dscores)
        dv_t[rows, :] = nn(dout_t[rows, :], probs)

    @pl.when(head == HEADS // 4 - 1)
    def _():
        factor = 1.0 / math.sqrt(depth)
        dqb = (dq[...] * factor).astype(BF16)
        dkb = (dk_t[...] * factor).astype(BF16).T
        dvb = dv_t[...].astype(BF16).T
        dsq[0] += tn(keyed_ref[0], dqb)
        dsq[1] += tn(keyed_ref[0], dkb)
        dsq[2] += tn(lowm_ref[0], dvb)
        dm = ds0[...] + nt(dqb, w_ref[0]) + nt(dkb, w_ref[1]) + nt(dvb, w_ref[2])
        dmb = dm.astype(BF16)
        if not last:
            dm_ref[0] = dmb
        else:
            parts = [ref[0] for ref in dm_refs] + [dmb]
            dwin = sum(tn(part[0:tokens], ref[0]) for part, ref in zip(parts, f_refs))
            flip = (me_ref[0] & 1) > 0
            rows = PART_C[0]
            put_blocks(outs, flip, 0, dwin.astype(BF16).T)
            for pair in range(2):
                put_blocks(outs, flip, rows + 16 * pair, pair_rows(dsq[2 * pair], dsq[2 * pair + 1]))
            put_blocks(outs, flip, rows + 32, pair_rows(norm_columns(dnorm_ref[...], width), jnp.zeros((width, width), F32)))


def norm_columns(dnorm, width):
    wide = jnp.concatenate([dnorm, jnp.zeros((128 - dnorm.shape[0], width), F32)], axis=0).T
    return jnp.concatenate([wide, jnp.zeros((width, width - 128), F32)], axis=1)


def encode_back(image, images, me, dx1, s0, norm, probs, keyed, lowm, q, k, v, o, square, features, *before):
    _, tokens, channels = features.shape
    padded, width = s0.shape[1:]
    first, last = image == 0, image == images - 1
    image_block = pl.BlockSpec((1, padded, width), lambda h: (image, 0, 0))
    whole = lambda shape: pl.BlockSpec(shape, lambda h: (0,) * len(shape))
    sums = [((4, width, width), F32), (norm.shape, F32)]
    part = ((BLOCKS // 2, sum(PART_C), width), BF16)
    outs = [part, part] if last else sums + [((1, padded, width), BF16)]
    scratch = [((padded, width), F32), ((padded, width), BF16), ((width, padded), BF16), ((width, padded), BF16), ((width, padded), BF16),
               ((padded, width), F32), ((padded, width), F32), ((width, padded), F32), ((width, padded), F32)]
    extra, extra_specs = list(before[:2]), [] if first else [whole(shape) for shape, _ in sums]
    if last:
        extra += [features] * images + list(before[2:])
        extra_specs += [pl.BlockSpec((1, tokens, channels), lambda h, j=j: (j, 0, 0)) for j in range(images)]
        extra_specs += [whole((1, padded, width))] * (images - 1)
    return pl.pallas_call(
        functools.partial(encode_back_kernel, tokens, images, first, last),
        grid=(HEADS // 4,),
        in_specs=[
            pl.BlockSpec(memory_space=pltpu.SMEM), image_block, image_block, whole(norm.shape),
            pl.BlockSpec((1, 4, padded, padded), lambda h: (image, h, 0, 0)),
        ] + [image_block] * 6 + [whole(square.shape)] + extra_specs,
        out_specs=[whole(shape) for shape, _ in outs],
        out_shape=[jax.ShapeDtypeStruct(shape, kind) for shape, kind in outs],
        scratch_shapes=[pltpu.VMEM(shape, kind) for shape, kind in scratch + (sums if last else [])],
        compiler_params=pltpu.CompilerParams(vmem_limit_bytes=VMEM_LIMIT),
        cost_estimate=cost(17 if last else 12),
        name="encode_back",
    )(me, dx1, s0, norm, probs, keyed, lowm, q, k, v, o, square, *extra)


def stack_heads(value):
    return jnp.concatenate([value * head_mask(value.shape[1], head) for head in range(HEADS)], axis=0)


def pick_heads(stacked):
    rows, width = stacked.shape[0] // HEADS, stacked.shape[1]
    lane = lax.broadcasted_iota(jnp.int32, (1, width), 1)
    out = stacked[0:rows]
    for head in range(1, HEADS):
        out = jnp.where(lane >= head * (width // HEADS), stacked[head * rows:(head + 1) * rows], out)
    return out


def soft_gap(gap):
    return SOFT * jnp.log(1.0 + jnp.exp(-jnp.abs(gap) * (1.0 / SOFT)))


def sigmoid(value):
    return 1.0 / (1.0 + jnp.exp(-value))


def axis_terms(center, size, target_center, target_size):
    low_one, high_one = center - size / 2, center + size / 2
    low_two, high_two = target_center - target_size / 2, target_center + target_size / 2
    low_gap, high_gap = low_one - low_two, high_one - high_two
    low_soft, high_soft = soft_gap(low_gap), soft_gap(high_gap)
    inner = (jnp.minimum(high_one, high_two) - high_soft) - (jnp.maximum(low_one, low_two) + low_soft)
    overlap = jnp.maximum(inner, 0.0) + soft_gap(inner)
    hull = (jnp.maximum(high_one, high_two) + high_soft) - (jnp.minimum(low_one, low_two) - low_soft)
    return overlap, hull, sigmoid(inner / SOFT), sigmoid(low_gap / SOFT), sigmoid(high_gap / SOFT)


def box_loss(box, target, mask, box_count):
    l1_sum = 0.0
    grads = []
    for one, two in zip(box, target):
        offset = (one - two) / SOFT_L1
        root = jnp.sqrt(offset * offset + 1.0)
        l1_sum = l1_sum + mask * (SOFT_L1 * (root - 1.0))
        grads.append(5.0 * offset / root)
    ow, hw, pw, lw, uw = axis_terms(box[0], box[2], target[0], target[2])
    oh, hh, ph, lh, uh = axis_terms(box[1], box[3], target[1], target[3])
    inter = ow * oh
    union = box[2] * box[3] + target[2] * target[3] - inter
    hull = hw * hh
    by_union, by_hull = 1.0 / union, 1.0 / hull
    giou = inter * by_union - (hull - union) * by_hull
    share = inter * by_union * by_union
    g_inter = by_union + share - by_hull
    g_area = by_hull - share
    g_hull = -union * by_hull * by_hull
    for axis, (other, hull_other, slope, low_s, high_s, size_other) in enumerate(
        ((oh, hh, pw, lw, uw, box[3]), (ow, hw, ph, lh, uh, box[2]))
    ):
        flow = g_inter * other * slope
        wide = g_hull * hull_other
        g_high = flow * (1.0 - high_s) + wide * high_s
        g_low = -flow * low_s - wide * (1.0 - low_s)
        grads[axis] = grads[axis] - 2.0 * (g_low + g_high)
        grads[axis + 2] = grads[axis + 2] - 2.0 * ((g_high - g_low) / 2 + g_area * size_other)
    value = jnp.sum((5.0 * l1_sum + 2.0 * mask * (1.0 - giou)) / box_count, axis=1, keepdims=True)
    return value, [grad * mask / box_count for grad in grads]


def middle_kernel(tokens, queries, classes, inverse, count_rows, me_ref, x1_ref, sine_ref, norm_ref,
                  col_ref, row_ref, got0, got1, got2, got3, other0, other1, other2, other3,
                  dx1_ref, keepa_ref, senda_ref, keepb_ref, sendb_ref, loss_ref, box_ref, feed_ref, rest_ref, dsq_ref, dnorm_ref, w_ref, head_ref, g0, total1, tall_g, tall_s, small_g, small_s, kin, vin, kk, vv, probs2, mixed2, dsum, dq2, dmix2):
    images, padded, width = x1_ref.shape
    depth = width // HEADS
    rows_feed = FIRST[0]
    chunks = BLOCKS * rows_feed // width
    per_chunk = BLOCKS // chunks
    many = images * padded
    qrows = round_up(queries, 128)
    factor = 1.0 / math.sqrt(depth)
    gain = lambda row: norm_ref[row:row + 1, :]
    dnorm_ref[...] = jnp.zeros_like(dnorm_ref)

    me = me_ref[0]
    for core, sources in enumerate(((got0, got1, got2, got3), (other0, other1, other2, other3))):
        for near, source in enumerate(sources):
            for far in range(4):
                block = me ^ (far * 8 + near * 2 + core)
                place = pl.ds(pl.multiple_of(block * rows_feed, rows_feed), rows_feed)
                for which in range(4):
                    feed_ref[which, place, :] = source[far, which * rows_feed:(which + 1) * rows_feed, :]
                rest_ref[block] = source[far, 4 * rows_feed:, :]
    for pair in range(5):
        for j, one in enumerate(unpair(rest_ref[:, 16 * pair:16 * pair + 16, :])):
            w_ref[2 * pair + j] = one.astype(BF16)
    head_one, found = unpair(rest_ref[:, 80:96, :])
    head_ref[...] = head_one[:, 0:head_ref.shape[1]].astype(BF16)
    box_count = jnp.sum(found[:, 0:1], axis=0, keepdims=True) * (1.0 / count_rows)
    box_ref[...] = box_count
    content, place = [one[:, 0:qrows].T for one in unpair(rest_ref[:, 96:112, :])]

    def weights(which, layer, chunk):
        return feed_ref[2 * which + layer, pl.ds(pl.multiple_of(chunk * width, width), width), :]

    flip = (me & 1) > 0
    out_a, out_b = (keepa_ref, senda_ref), (keepb_ref, sendb_ref)

    def put_feed(which, layer, chunk, value):
        value = value.reshape(per_chunk // 2, 2, rows_feed, width)
        place = pl.ds(chunk * (per_chunk // 2), per_chunk // 2), slice(layer * rows_feed, (layer + 1) * rows_feed)
        keep, send = out_b if which else out_a
        keep[place] = jnp.where(flip, value[:, 1], value[:, 0])
        send[place] = jnp.where(flip, value[:, 0], value[:, 1])

    def feed(layer, source, g_ref, s_ref, out_ref):
        def step(chunk, carry):
            value, slope = gelu_parts(nt(source, weights(0, layer, chunk)))
            value = value.astype(BF16)
            g_ref[chunk] = value
            s_ref[chunk] = slope.astype(BF16)
            out_ref[...] += nn(value, weights(1, layer, chunk))
            return carry
        lax.fori_loop(0, chunks, step, 0, unroll=True)

    def feed_back(layer, source_t, grad, grad_t, g_ref, s_ref, out_ref):
        def step(chunk, carry):
            dg = nt(grad, weights(1, layer, chunk)).astype(BF16)
            du = (dg.astype(F32) * s_ref[chunk].astype(F32)).astype(BF16)
            put_feed(1, layer, chunk, nn(grad_t, g_ref[chunk]).astype(BF16).T)
            put_feed(0, layer, chunk, nn(source_t, du).astype(BF16).T)
            out_ref[...] += nn(du, weights(0, layer, chunk))
            return carry
        lax.fori_loop(0, chunks, step, 0, unroll=True)

    x1 = x1_ref[...].reshape(many, width)
    total1[...] = x1
    feed(0, x1.astype(BF16), tall_g, tall_s, total1)
    unit1, scale1 = norm_parts(total1[...])
    x2 = unit1 * gain(1) + gain(7)
    for image in range(images):
        part = x2[image * padded:(image + 1) * padded]
        keyed = (part + sine_ref[...]).astype(BF16)
        lowm = part.astype(BF16)
        kin[image] = keyed
        vin[image] = lowm
        kk[image] = nn(keyed, w_ref[5]).astype(BF16)
        vv[image] = nn(lowm, w_ref[6]).astype(BF16)

    asked = (content + place).astype(BF16)
    lowc = content.astype(BF16)
    q1 = nn(asked, w_ref[0]).astype(BF16)
    k1 = nn(asked, w_ref[1]).astype(BF16)
    v1 = nn(lowc, w_ref[2]).astype(BF16)
    q1s = stack_heads(q1)
    p1 = masked_softmax(nt(q1s, k1), depth, queries)
    mix1 = pick_heads(nn(p1, v1))
    mix1b = mix1.astype(BF16)
    unit2, scale2 = norm_parts(content + nn(mix1b, w_ref[3]))
    t1 = unit2 * gain(2) + gain(8)

    asked2 = (t1 + place).astype(BF16)
    q2 = nn(asked2, w_ref[4]).astype(BF16)
    q2s = stack_heads(q2)

    def cross(image, carry):
        probs = masked_softmax(nt(q2s, kk[image]), depth, tokens)
        probs2[image] = probs
        mixed2[image] = pick_heads(nn(probs, vv[image]))
        return carry
    lax.fori_loop(0, images, cross, 0, unroll=True)
    rows = images * qrows
    mix2 = mixed2[...].reshape(rows, width)
    mix2b = mix2.astype(BF16)
    t1s = jnp.concatenate([t1] * images, axis=0)
    unit3, scale3 = norm_parts(t1s + nn(mix2b, w_ref[7]))
    t2 = unit3 * gain(3) + gain(9)

    t2b = t2.astype(BF16)
    g0[...] = t2
    feed(1, t2b, small_g, small_s, g0)
    unit4, scale4 = norm_parts(g0[...])
    t3 = unit4 * gain(4) + gain(10)
    unit5, scale5 = norm_parts(t3)
    out = (unit5 * gain(5) + gain(11)).astype(BF16)

    logits = nn(out, head_ref[...])
    lane = lax.broadcasted_iota(jnp.int32, logits.shape, 1)
    weight = col_ref[:, 0:1]
    label = col_ref[:, 1:2].astype(jnp.int32)
    kept = jnp.where(lane < classes, logits, -1e30)
    top = jnp.max(kept, axis=1, keepdims=True)
    powers = jnp.exp(kept - top)
    norm_sum = jnp.sum(powers, axis=1, keepdims=True)
    chosen = lane == label
    ce = top + jnp.log(norm_sum) - jnp.sum(jnp.where(chosen, logits, 0.0), axis=1, keepdims=True)
    ce_sum = jnp.sum(weight * ce, axis=0, keepdims=True)
    dlogits = ((weight * inverse) * (powers / norm_sum - jnp.where(chosen, 1.0, 0.0))).astype(BF16)

    b1, slope_one = gelu_parts(nn(out, w_ref[8]))
    b1 = b1.astype(BF16)
    b2, slope_two = gelu_parts(nn(b1, w_ref[9]))
    b2 = b2.astype(BF16)
    raw = nn(b2, head_ref[...]).T
    box = [sigmoid(raw[classes + j:classes + j + 1, :]) for j in range(4)]
    target = [row_ref[1 + j:2 + j, :] for j in range(4)]
    box_value, dbox = box_loss(box, target, row_ref[0:1, :], box_count)
    loss_ref[...] = ce_sum * inverse + box_value
    draw = jnp.concatenate([grad * one * (1.0 - one) for grad, one in zip(dbox, box)], axis=0)
    lanes_in = head_ref.shape[1]
    spot = lax.broadcasted_iota(jnp.int32, (lanes_in, rows), 0)
    spread = jnp.zeros((lanes_in, rows), F32)
    for j in range(4):
        spread = jnp.where(spot == classes + j, draw[j:j + 1, :], spread)
    draw_rows = spread.T.astype(BF16)

    dhead = tn(out, dlogits) + tn(b2, draw_rows)
    du2 = (nt(draw_rows, head_ref[...]) * slope_two).astype(BF16)
    dsq_ref[9] = tn(b1, du2)
    du1 = (nt(du2, w_ref[9]) * slope_one).astype(BF16)
    dsq_ref[8] = tn(out, du1)
    dout = nt(dlogits, head_ref[...]) + nt(du1, w_ref[8])

    def through(grad, unit, scale, row):
        dnorm_ref[row:row + 1, :] = column_sum(grad * unit)
        dnorm_ref[row + 6:row + 7, :] = column_sum(grad)
        return norm_back(grad, unit, scale, gain(row))

    dt3 = through(dout, unit5, scale5, 5)
    ds3 = through(dt3, unit4, scale4, 4)
    g0[...] = ds3
    ds3b = ds3.astype(BF16)
    feed_back(1, t2b.T, ds3b, ds3b.T, small_g, small_s, g0)
    ds2 = through(g0[...], unit3, scale3, 3)
    ds2b = ds2.astype(BF16)
    dsq_ref[7] = tn(mix2b, ds2b)
    dmix2[...] = nt(ds2b, w_ref[7]).astype(BF16).reshape(images, qrows, width)
    dq2[...] = jnp.zeros_like(dq2)
    dsum[...] = jnp.zeros_like(dsum)

    def attention_back(dmix, mix, probs, stacked_q, keys, values):
        dms = stack_heads(dmix)
        both = dmix.astype(F32) * mix
        weight = jnp.concatenate(
            [jnp.sum(both * head_mask(width, head).astype(F32), axis=1, keepdims=True) for head in range(HEADS)],
            axis=0,
        )
        dscores = (probs.astype(F32) * (nt(dms, values) - weight)).astype(BF16)
        dq = pick_heads(nn(dscores, keys)) * factor
        dk = (tn(stacked_q, dscores) * factor).astype(BF16).T
        dv = tn(dms, probs).astype(BF16).T
        return dq, dk, dv

    def cross_back(image, carry):
        dq, dk, dv = attention_back(dmix2[image], mixed2[image], probs2[image], q2s, kk[image], vv[image])
        dq2[...] += dq
        dsum[0] += tn(kin[image], dk)
        dsum[1] += tn(vin[image], dv)
        dx1_ref[image] = nt(dk, w_ref[5]) + nt(dv, w_ref[6])
        return carry
    lax.fori_loop(0, images, cross_back, 0, unroll=True)
    dsq_ref[5] = dsum[0]
    dsq_ref[6] = dsum[1]
    dq2b = dq2[...].astype(BF16)
    dsq_ref[4] = tn(asked2, dq2b)
    dasked2 = nt(dq2b, w_ref[4])
    dt1 = dasked2
    for image in range(images):
        dt1 = dt1 + ds2[image * qrows:(image + 1) * qrows]
    ds1 = through(dt1, unit2, scale2, 2)
    ds1b = ds1.astype(BF16)
    dsq_ref[3] = tn(mix1b, ds1b)
    dmix1 = nt(ds1b, w_ref[3]).astype(BF16)
    dq, dk, dv = attention_back(dmix1, mix1, p1, q1s, k1, v1)
    dqb = dq.astype(BF16)
    dsq_ref[0] = tn(asked, dqb)
    dsq_ref[1] = tn(asked, dk)
    dsq_ref[2] = tn(lowc, dv)
    dasked = nt(dqb, w_ref[0]) + nt(dk, w_ref[1])
    dquery = [ds1 + dasked + nt(dv, w_ref[2]), dasked + dasked2]

    unit, scale = norm_parts(total1[...])
    dx2 = dx1_ref[...].reshape(many, width)
    ds = through(dx2, unit, scale, 1)
    total1[...] = ds
    dsb = ds.astype(BF16)
    x1b = x1_ref[...].reshape(many, width).astype(BF16)
    feed_back(0, x1b.T, dsb, dsb.T, tall_g, tall_s, total1)
    dx1_ref[...] = total1[...].reshape(images, padded, width)

    wide = lambda value: jnp.concatenate([value, jnp.zeros((value.shape[0], width - value.shape[1]), F32)], axis=1)
    at = 2 * rows_feed
    for pair in range(3):
        put_blocks(out_a, flip, at + 16 * pair, pair_rows(dsq_ref[2 * pair], dsq_ref[2 * pair + 1]))
    for pair in range(2):
        put_blocks(out_b, flip, at + 16 * pair, pair_rows(dsq_ref[6 + 2 * pair], dsq_ref[7 + 2 * pair]))
    put_blocks(out_b, flip, at + 32, pair_rows(wide(dhead), norm_columns(dnorm_ref[...], width)))
    put_blocks(out_b, flip, at + 48, pair_rows(wide(dquery[0].T), wide(dquery[1].T)))


def middle(me, x1, sine, norm, col, row, pieces, tokens, queries, classes, inverse, count_rows):
    images, padded, width = x1.shape
    qrows = round_up(queries, 128)
    chunks = BLOCKS * FIRST[0] // width
    many, rows = images * padded, images * qrows
    vmem = pl.BlockSpec(memory_space=pltpu.VMEM)
    shapes = [
        ((images, padded, width), F32), ((BLOCKS // 2, sum(PART_A), width), BF16),
        ((BLOCKS // 2, sum(PART_A), width), BF16), ((BLOCKS // 2, sum(PART_B), width), BF16),
        ((BLOCKS // 2, sum(PART_B), width), BF16), ((1, 1), F32), ((1, 1), F32),
    ]
    return pl.pallas_call(
        functools.partial(middle_kernel, tokens, queries, classes, inverse, count_rows),
        in_specs=[pl.BlockSpec(memory_space=pltpu.SMEM)] + [vmem] * (5 + len(pieces)),
        out_specs=[vmem] * len(shapes),
        out_shape=[jax.ShapeDtypeStruct(shape, kind) for shape, kind in shapes],
        scratch_shapes=[
            pltpu.VMEM((4, chunks * width, width), BF16), pltpu.VMEM((BLOCKS, sum(SECOND) - 4 * FIRST[0], width), BF16),
            pltpu.VMEM((10, width, width), F32), pltpu.VMEM((16, width), F32),
            pltpu.VMEM((10, width, width), BF16), pltpu.VMEM((width, 128), BF16),
            pltpu.VMEM((rows, width), F32), pltpu.VMEM((many, width), F32),
            pltpu.VMEM((chunks, many, width), BF16), pltpu.VMEM((chunks, many, width), BF16),
            pltpu.VMEM((chunks, rows, width), BF16), pltpu.VMEM((chunks, rows, width), BF16),
            pltpu.VMEM((images, padded, width), BF16), pltpu.VMEM((images, padded, width), BF16),
            pltpu.VMEM((images, padded, width), BF16), pltpu.VMEM((images, padded, width), BF16),
            pltpu.VMEM((images, HEADS * qrows, padded), BF16), pltpu.VMEM((images, qrows, width), F32),
            pltpu.VMEM((2, width, width), F32), pltpu.VMEM((qrows, width), F32),
            pltpu.VMEM((images, qrows, width), BF16),
        ],
        compiler_params=pltpu.CompilerParams(vmem_limit_bytes=VMEM_LIMIT),
        cost_estimate=cost(35),
        name="middle",
    )(me, x1, sine, norm, col, row, *pieces)


def sine_table(width, padded):
    cells = np.arange(SIDE * SIDE)
    half = width // 2
    index = np.arange(half)
    freqs = 10000.0 ** ((2 * (index // 2)) / half)
    parts = []
    for coord in (cells // SIDE + 1, cells % SIDE + 1):
        angle = (coord / (SIDE + 1e-06) * (2.0 * math.pi))[:, None] / freqs[None, :]
        parts.append(np.where(index[None, :] % 2 == 0, np.sin(angle), np.cos(angle)))
    table = np.concatenate(parts, axis=1).astype(np.float32)
    return np.concatenate([table, np.zeros((padded - table.shape[0], width), np.float32)], axis=0)


def round_up(value, unit):
    return -(-value // unit) * unit


def target_info(matches, labels, boxes, classes, qrows):
    images, queries = matches.shape
    pad = ((0, 0), (0, qrows - queries))
    matched = matches >= 0
    picker = matches[:, :, None] == jnp.arange(labels.shape[1])[None, None, :]
    label = jnp.where(matched, jnp.sum(jnp.where(picker, labels[:, None, :], 0), axis=2), classes - 1)
    weight = jnp.pad(jnp.where(matched, 1.0, NO_OBJECT), pad)
    label = jnp.pad(label, pad).astype(F32)
    col = jnp.stack([weight.reshape(-1), label.reshape(-1)], axis=1)
    mask = jnp.pad(matched.astype(F32), pad).reshape(1, -1)
    wanted = []
    for j in range(4):
        one = jnp.sum(jnp.where(picker, boxes[:, None, :, j], 0.0), axis=2)
        wanted.append(jnp.pad(jnp.where(matched, one, 0.5), pad, constant_values=0.5).reshape(1, -1))
    row = jnp.concatenate([mask] + wanted + [jnp.zeros((3, mask.shape[1]), F32)], axis=0)
    return col, row


AXES = ("dp", "fsdp")


def swap(value, bit, devices):
    return lax.ppermute(value, AXES, [(i, i ^ bit) for i in range(devices)])


def bits_of(devices):
    return [1 << j for j in range(devices.bit_length() - 1)]


def groups_of(devices):
    bits = bits_of(devices)
    return [(bits[j], bits[j + 1]) for j in range(len(bits) - 2, 0, -2)]


def place_of(far, devices):
    place = 0
    for low, _ in reversed(groups_of(devices)):
        place = place * 4 + (far // low) % 4
    return place


def gather_four(held, pair, devices):
    low, high = pair
    return [held] + [swap(held, bits, devices) for bits in (low, high, low | high)]


def gather_round(held, pair, devices):
    return jnp.concatenate(gather_four(held, pair, devices))


def natural_order(got, other, me, pieces):
    devices = 2 * got.shape[0]
    both = jnp.concatenate([got, other])
    table = jnp.asarray([(j & 1) * (devices // 2) + place_of(j, devices) for j in range(devices)])
    blocks = join(both[table[jnp.arange(devices) ^ me]], pieces)
    chips = sorted(range(0, BLOCKS, 2), key=lambda block: place_of(block, BLOCKS))
    return [jnp.stack([blocks[block + core] for block in chips]) for core in range(2)]


def join(got, pieces):
    ratio = got.shape[0] // BLOCKS
    if ratio == 1:
        return got
    got = got.reshape(BLOCKS, ratio, got.shape[1], got.shape[2])
    out, at = [], 0
    for piece in pieces:
        rows = piece // ratio
        out.append(got[:, :, at:at + rows].reshape(BLOCKS, piece, got.shape[3]))
        at += rows
    return jnp.concatenate(out, axis=1)


def launch(keep, send, pieces, devices):
    bits = bits_of(devices)
    ratio = devices // BLOCKS
    tail = keep.shape[1:]
    if ratio == 1:
        shape = (2,) * (len(bits) - 1) + tail
        return swap(send, bits[0], devices).reshape(shape), keep.reshape(shape), list(reversed(bits[1:]))
    value = jnp.stack([keep, send], axis=1).reshape((BLOCKS,) + tail)
    out, at = [], 0
    for piece in pieces:
        out.append(value[:, at:at + piece].reshape(devices, piece // ratio, tail[1]))
        at += piece
    out = jnp.concatenate(out, axis=1)
    out = out.reshape((2,) * len(bits) + out.shape[1:])
    left = list(reversed(bits))
    return advance((jnp.zeros_like(out), out, left), bits[0], devices)


def halves(flight, bit):
    came, kept, left = flight
    axis = left.index(bit)
    mine = (lax.axis_index(AXES) // bit) % 2
    pick = lambda value, at: lax.dynamic_index_in_dim(value, at, axis, keepdims=False).astype(F32)
    out = (pick(kept, 1 - mine) + pick(came, 1 - mine)).astype(BF16)
    return out, pick(kept, mine) + pick(came, mine), [one for one in left if one != bit]


def advance(flight, bit, devices):
    out, kept, left = halves(flight, bit)
    return swap(out, bit, devices), kept, left


def parts_of_four(flight, low, high, devices):
    *addends, left = flight
    axes = [left.index(bit) for bit in (low, high)]
    mine = [(lax.axis_index(AXES) // bit) % 2 for bit in (low, high)]
    out = []
    for bits in (low, high, low | high, 0):
        total = 0.0
        for value in addends:
            for axis, bit, at in sorted(zip(axes, (low, high), mine), key=lambda one: -one[0]):
                at = 1 - at if bits & bit else at
                value = lax.dynamic_index_in_dim(value, at, axis, keepdims=False)
            total = total + value.astype(F32)
        out.append(total.astype(BF16) if bits else total)
    return out


def send_four(parts, flight, low, high, devices):
    came = [swap(one, bits, devices) for one, bits in zip(parts, (low, high, low | high))]
    return (parts[3], *came, [bit for bit in flight[-1] if bit not in (low, high)])


def exact(left, right, dims=((1,), (0,))):
    return lax.dot_general(left, right, (dims, ((), ())), precision=lax.Precision.HIGHEST, preferred_element_type=F32)


def gram_kernel(mom_ref, grad_ref, x_ref, gram_ref, sums_ref):
    slot = mom_ref.shape[1]
    devices, _, width = grad_ref.shape
    sums = jnp.sum(grad_ref[:, slot:, :].astype(F32), axis=0)
    sums_ref[...] = sums
    squares = jnp.sum(sums[0:1, 0:3], axis=1, keepdims=True)
    factor = jnp.minimum(1.0, CLIP / (jnp.sqrt(squares) + 1e-06))
    x = BETA_M * mom_ref[...].astype(F32) + factor * grad_ref[:, :slot, :].astype(F32)
    x = x.reshape(devices * slot, width)
    x_ref[...] = x
    gram_ref[...] = exact(x, x, ((0,), (0,)))


def rough(left, right):
    left_high, right_high = left.astype(BF16), right.astype(BF16)
    left_low = (left - left_high.astype(F32)).astype(BF16)
    right_low = (right - right_high.astype(F32)).astype(BF16)
    return nn(left_high, right_high) + (nn(left_high, right_low) + nn(left_low, right_high))


def polish_kernel(x_ref, gram_ref, came_ref, out_ref):
    gram = gram_ref[...] + came_ref[...]
    diagonal = lax.broadcasted_iota(jnp.int32, gram.shape, 0) == lax.broadcasted_iota(jnp.int32, gram.shape, 1)
    eye = jnp.where(diagonal, 1.0, 0.0)
    square = jnp.sum(jnp.sum(gram * eye, axis=1, keepdims=True), axis=0, keepdims=True)
    scale = 1.0 / (jnp.sqrt(square) + 1e-07)
    gram = gram * (scale * scale)
    total = None
    for sweep in range(5):
        product = exact if sweep < 2 else rough
        poly = NS_A * eye + NS_B * gram + NS_C * product(gram, gram)
        total = poly if sweep == 0 else product(total, poly)
        if sweep < 4:
            gram = product(product(poly, gram), poly)
    out = rough(x_ref[...] * scale, total)
    out_ref[...] = out.reshape(out_ref.shape).astype(out_ref.dtype)


def plain_call(body, shapes, *args):
    vmem = pl.BlockSpec(memory_space=pltpu.VMEM)
    return pl.pallas_call(
        body,
        in_specs=[vmem] * len(args),
        out_specs=[vmem] * len(shapes),
        out_shape=[jax.ShapeDtypeStruct(shape, kind) for shape, kind in shapes],
        compiler_params=pltpu.CompilerParams(vmem_limit_bytes=VMEM_LIMIT),
        cost_estimate=cost(2),
        name=body.__name__,
    )(*args)


def to_slots(square, feeds, devices):
    count, rows, width = square.shape
    slot = feeds.shape[1] // 4
    feed_slots = feeds.reshape(feeds.shape[0] * 4, slot, width)
    square_slots = jnp.pad(square, ((0, devices - count - feed_slots.shape[0]), (0, slot - rows), (0, 0)))
    return jnp.concatenate([feed_slots, square_slots], axis=0)


def exchange(slots):
    return lax.all_to_all(slots, AXES, split_axis=0, concat_axis=0, tiled=True)


def adam(weight, first, second, gradient, rate, decay):
    first = ADAM_B1 * first + (1.0 - ADAM_B1) * gradient
    second = ADAM_B2 * second + (1.0 - ADAM_B2) * gradient * gradient
    fixed_first = first / (1.0 - ADAM_B1**STEP)
    fixed_second = second / (1.0 - ADAM_B2**STEP)
    weight = weight * (1.0 - rate * decay) - rate * fixed_first / (jnp.sqrt(fixed_second) + 1e-08)
    return weight, first, second, weight.astype(BF16)


def muon(weight, ortho, longest):
    fresh = weight * (1.0 - LR_M * DECAY_M) - LR_M * 0.2 * math.sqrt(longest) * ortho
    return fresh, fresh.astype(BF16)


def pack_kernel(win_ref, sq_ref, ex_ref, re_ref, head_ref, query_ref, norm_ref, matches_ref, one_ref, two_ref):
    one, two = pack(win_ref[...], sq_ref[...], ex_ref[...], re_ref[...], head_ref[...], query_ref[...], norm_ref[...],
                    matches_ref[...])
    one_ref[...] = one
    two_ref[...] = two


def pack(win, sq, ex, re, head, query, norm, matches):
    width = win.shape[1]
    rows = sq.shape[1]
    wide = lambda value: jnp.concatenate([value, jnp.zeros((value.shape[0], width - value.shape[1]), F32)], axis=1)
    flat = lambda value: [value[j] for j in range(value.shape[0])]
    found = jnp.where(matches >= 0, 1.0, 0.0)
    found = jnp.sum(jnp.sum(found, axis=1, keepdims=True), axis=0, keepdims=True)
    one = [win] + flat(sq[:4]) + [wide(norm), jnp.zeros((rows, width), F32)]
    two = flat(ex) + flat(re) + flat(sq[4:]) + [wide(head), jnp.broadcast_to(found, (rows, width))]
    two = two + [wide(query[0]), wide(query[1])]
    return jnp.concatenate(one).astype(BF16), jnp.concatenate(two).astype(BF16)


def per_device(devices, features, matches, target_labels, target_boxes,
               square_weight, square_momentum, expand_weight, expand_momentum, reduce_weight, reduce_momentum,
               input_weight, input_momentum, input_second, head_weight, head_momentum, head_second,
               query_weight, query_momentum, query_second, norm_weight, norm_momentum, norm_second):
    images, tokens, channels = features.shape
    count, rs, width = square_weight.shape
    pairs, _, rf = expand_weight.shape
    ri = input_weight.shape[0]
    rh, head_lanes = head_weight.shape
    _, queries, rq = query_weight.shape
    norms, rn = norm_weight.shape
    classes = head_lanes - 4
    padded, qrows = round_up(tokens, 128), round_up(queries, 128)
    hidden = rf * devices
    aligned = devices == BLOCKS

    shards = (input_weight, square_weight, jnp.transpose(expand_weight, (0, 2, 1)), reduce_weight, head_weight,
              jnp.transpose(query_weight, (0, 2, 1)), norm_weight.T, matches)
    if aligned:
        first, second = plain_call(
            pack_kernel, [((sum(FIRST), width), BF16), ((sum(SECOND), width), BF16)], *shards)
    else:
        first, second = lax.optimization_barrier(pack(*shards))
    sine = jnp.asarray(sine_table(width, padded))
    laid = with_layout_constraint(features, Layout(major_to_minor=(0, 1, 2)))
    info = target_info(matches, target_labels, target_boxes, classes, qrows)
    expand_momentum_t = jnp.transpose(expand_momentum, (0, 2, 1))
    mom_slots = to_slots(
        square_momentum, jnp.concatenate([expand_momentum_t, reduce_momentum]), devices).astype(BF16)
    mom_in = exchange(mom_slots)

    held_one, held_two = first[None], second[None]
    pairs_of_bits = groups_of(devices)
    for pair in pairs_of_bits[:-1]:
        held_one, held_two = lax.optimization_barrier((gather_round(held_one, pair, devices), held_two))
        held_one, (col, row) = lax.optimization_barrier((held_one, info))
        rest_two = gather_round(held_two, pair, devices) if pair == pairs_of_bits[-2] else None
        if rest_two is None:
            held_two = gather_round(held_two, pair, devices)
    held_one = gather_round(held_one, pairs_of_bits[-1], devices)
    held_one, held_two, laid = lax.optimization_barrier((held_one, rest_two, laid))
    other_one = swap(held_one, 1, devices)
    pieces_two = gather_four(held_two, pairs_of_bits[-1], devices)
    me = lax.axis_index(AXES)
    if not aligned:
        held_one, other_one = natural_order(held_one, other_one, me, FIRST)
        me = jnp.zeros((), jnp.int32)
    me = me.reshape(1)

    inverse = 1.0 / (images * devices * queries)
    probs, keyed, lowm, q, k, v, o, s0, x1, sq_one, norm_all = encode(laid, me, held_one, other_one, sine)
    pieces_two, x1 = lax.optimization_barrier((pieces_two, x1))
    pieces_two = pieces_two + [swap(one, 1, devices) for one in pieces_two]
    if not aligned:
        both = [jnp.concatenate(pieces_two[:4]), jnp.concatenate(pieces_two[4:])]
        both = natural_order(*both, lax.axis_index(AXES), SECOND)
        pieces_two = [one[4 * j:4 * j + 4] for one in both for j in range(4)]
    dx1, keep_a, send_a, keep_b, send_b, loss, box_total = middle(
        me, x1, sine, norm_all, col, row, pieces_two, tokens, queries, classes, inverse, rs)

    bits = bits_of(devices)
    near, far = bits[1], bits[2]
    turns = [(near, far), (far, near)]
    flight_a, flight_b = launch(keep_a, send_a, PART_A, devices), launch(keep_b, send_b, PART_B, devices)
    sums = ()
    for image in range(images):
        if image and turns:
            half_a, half_b = [halves(flight, bit) for flight, bit in zip((flight_a, flight_b), turns.pop(0))]
            sums, (out_a, out_b) = lax.optimization_barrier((sums, (half_a[0], half_b[0])))
            flight_a = (swap(out_a, near, devices),) + half_a[1:]
            flight_b = (swap(out_b, far, devices),) + half_b[1:]
        sums = encode_back(
            image, images, me, dx1, s0, norm_all, probs, keyed, lowm, q, k, v, o, sq_one, laid, *sums)
    sums, ready_a, ready_b = lax.optimization_barrier((sums, flight_a[:2], flight_b[:2]))
    flight_a, flight_b = (*ready_a, flight_a[2]), (*ready_b, flight_b[2])
    flight_c = launch(*sums, PART_C, devices)
    for bit_a, bit_b in turns:
        flight_a, flight_b = advance(flight_a, bit_a, devices), advance(flight_b, bit_b, devices)
    rest = [bit for bit in bits if bit not in (bits[0], near, far)]
    half_a, half_b = halves(flight_a, rest[0]), halves(flight_b, rest[0])
    out, kept = [jnp.concatenate([a, b], axis=-2) for a, b in zip(half_a[:2], half_b[:2])]
    flight = (swap(out, rest[0], devices), kept, half_a[2])
    for bit in rest[1:]:
        flight = advance(flight, bit, devices)
    for pair in reversed(pairs_of_bits):
        flight_c = send_four(parts_of_four(flight_c, *pair, devices), flight_c, *pair, devices)

    rows_ab, rows_c = sum(PART_A + PART_B) * BLOCKS // devices, sum(PART_C) * BLOCKS // devices
    slot = rf // 4
    ready, ready_c = flight[:-1], flight_c[:-1]
    shapes = [((rows_ab, width), F32), ((rows_c, width), F32), ((devices, slot + 8, width), BF16)]
    if aligned:
        sum_ab, sum_c, grad_slots = plain_call(prepare_kernel, shapes, *ready, *ready_c, loss)
    else:
        sum_ab, sum_c, grad_slots = prepare(ready, ready_c, loss, devices, lambda value: lax.reduce_precision(value, 8, 7))
    grad_in = exchange(grad_slots)
    x, gram, sums = plain_call(
        gram_kernel, [((devices * slot, width), F32), ((width, width), F32), ((8, width), F32)], mom_in, grad_in)
    feeds = 8 * pairs
    gram = gram + lax.ppermute(gram, AXES, [(i, i ^ 1) for i in range(feeds)])
    came = lax.ppermute(gram, AXES, [(i, i ^ 2) for i in range(feeds)])
    back = exchange(plain_call(polish_kernel, [((devices, slot, width), BF16)], x, gram, came)[0])

    turn = lambda value: jnp.transpose(value, (0, 2, 1))
    states = (square_momentum, expand_momentum_t, reduce_momentum,
              input_weight, input_momentum, input_second, head_weight, head_momentum, head_second,
              turn(query_weight), turn(query_momentum), turn(query_second),
              norm_weight.T, norm_momentum.T, norm_second.T)
    weights = (square_weight, turn(expand_weight), reduce_weight)
    if aligned:
        like = lambda value, kind: (value.shape, kind)
        shapes = [like(value, F32) for value in states[:3]]
        for value in states[3::3]:
            shapes += [like(value, F32)] * 3 + [like(value, BF16)]
        new = plain_call(adapt_kernel, shapes + [((1, 1), F32)] * 2, sum_ab, sum_c, sums, *states)
        shapes = [like(value, kind) for value in weights for kind in (F32, BF16)]
        fresh = plain_call(apply_kernel, shapes, back, *weights)
    else:
        new = adapt(sum_ab, sum_c, sums, *states)
        fresh = apply(back, hidden, *weights)
    square_mom, expand_mom, reduce_mom = new[:3]
    query_out = [turn(value) for value in new[11:15]]
    norm_out = [value.T for value in new[15:19]]
    return (
        (fresh[0], square_mom, fresh[1], turn(fresh[2]), turn(expand_mom), turn(fresh[3]),
         fresh[4], reduce_mom, fresh[5]) + tuple(new[3:11]) + tuple(query_out) + tuple(norm_out)
        + (new[19].reshape(()), box_total.reshape(()), new[20].reshape(()))
    )


def row_parts(sum_ab, sum_c):
    rf = sum_c.shape[0] * PART_C[0] // sum(PART_C)
    rs = rf // 8
    cut = lambda value, start, rows: value[start:start + rows]
    half = 2 * rf + 6 * rs
    feeds = [cut(sum_ab, j * rf, rf) for j in range(2)] + [cut(sum_ab, half + j * rf, rf) for j in range(2)]
    squares = [cut(sum_c, rf + j * rs, rs) for j in range(4)]
    squares += [cut(sum_ab, 2 * rf + j * rs, rs) for j in range(6)]
    at = half + 2 * rf
    squares += [cut(sum_ab, at + j * rs, rs) for j in range(4)]
    head, norm, content, place = [cut(sum_ab, at + (4 + j) * rs, rs) for j in range(4)]
    norm = norm + cut(sum_c, rf + 4 * rs, rs)
    return feeds, squares, cut(sum_c, 0, rf), head, [content, place], norm


def prepare(parts_ab, parts_c, loss, devices, low):
    sum_ab, sum_c = [sum(value.astype(F32) for value in some) for some in (parts_ab, parts_c)]
    width = sum_ab.shape[1]
    total = sum(
        jnp.sum(jnp.sum(value * value, axis=0, keepdims=True), axis=1, keepdims=True) for value in (sum_ab, sum_c))
    spot = [lax.broadcasted_iota(jnp.int32, (8, width), axis) for axis in (0, 1)]
    numbers = jnp.zeros((8, width), F32)
    for row, value in enumerate((total, loss)):
        for lane in range(3):
            high = low(value)
            numbers = jnp.where(jnp.logical_and(spot[0] == row, spot[1] == lane), high, numbers)
            value = value - high
    feeds, squares, _, _, _, _ = row_parts(sum_ab, sum_c)
    slot = feeds[0].shape[0] // 4
    rs = squares[0].shape[0]
    none = jnp.zeros((slot - rs, width), F32)
    spare = [jnp.zeros((slot, width), F32)] * (devices - 16 - len(squares))
    slots = [feed[j * slot:(j + 1) * slot] for feed in feeds for j in range(4)]
    slots += [jnp.concatenate([square, none]) for square in squares] + spare
    slots = jnp.stack([jnp.concatenate([one, numbers]) for one in slots])
    return sum_ab, sum_c, slots.astype(BF16)


def prepare_kernel(*refs):
    *parts, loss, sum_ab, sum_c, slots = refs
    sum_ab[...], sum_c[...], slots[...] = prepare(
        [ref[...] for ref in parts[:2]], [ref[...] for ref in parts[2:]], loss[...], slots.shape[0], lambda value: value.astype(BF16).astype(F32))


def adapt(sum_ab, sum_c, sums, square_mom, expand_mom, reduce_mom, *states):
    feeds, squares, win, head, query, norm = row_parts(sum_ab, sum_c)
    lane = lax.broadcasted_iota(jnp.int32, (1, sums.shape[1]), 1)
    total, loss = [jnp.sum(jnp.where(lane < 3, sums[j:j + 1, :], 0.0), axis=1, keepdims=True) for j in range(2)]
    size = jnp.sqrt(total)
    factor = jnp.minimum(1.0, CLIP / (size + 1e-06))
    out = [BETA_M * square_mom + factor * jnp.stack(squares),
           BETA_M * expand_mom + factor * jnp.stack(feeds[:2]),
           BETA_M * reduce_mom + factor * jnp.stack(feeds[2:])]
    query = jnp.stack([one[:, :states[6].shape[2]] for one in query])
    grads = (win, head[:, :states[3].shape[1]], query, norm[:, :states[9].shape[1]])
    for j, (grad, rate, decay) in enumerate(zip(grads, (0.04, 0.1, 0.5, 0.5), (0.0001, 0.0001, 0.0, 0.0))):
        out += adam(*states[3 * j:3 * j + 3], factor * grad, rate, decay)
    return out + [loss, size]


def adapt_kernel(*refs):
    count = 18
    for ref, value in zip(refs[count:], adapt(*[ref[...] for ref in refs[:count]])):
        ref[...] = value


def apply(back, hidden, square, expand, reduce):
    slot = back.shape[1]
    rf = 4 * slot
    rs = square.shape[1]
    feed = back[:16].astype(F32).reshape(4, rf, back.shape[2])
    ortho = back[16:16 + square.shape[0]].astype(F32)[:, :rs]
    return muon(square, ortho, square.shape[2]) + muon(expand, feed[:2], hidden) + muon(reduce, feed[2:], hidden)


def apply_kernel(back, square, expand, reduce, *outs):
    hidden = back.shape[0] * expand.shape[1]
    for ref, value in zip(outs, apply(back[...], hidden, square[...], expand[...], reduce[...])):
        ref[...] = value


def solution(mesh):
    both = ("dp", "fsdp")
    first = [P(both), P(both), P(both), P(both)]
    square, expand, reduce = P(None, both), P(None, None, both), P(None, both)
    rows, query, norm = P(both), P(None, None, both), P(None, both)
    in_specs = tuple(first + [square] * 2 + [expand] * 2 + [reduce] * 2 + [rows] * 6 + [query] * 3 + [norm] * 3)
    out_specs = tuple([square] * 3 + [expand] * 3 + [reduce] * 3 + [rows] * 8 + [query] * 4 + [norm] * 4 + [P()] * 3)
    return jax.shard_map(
        functools.partial(per_device, mesh.size), mesh=mesh, in_specs=in_specs, out_specs=out_specs, check_vma=False)
```

```python
import functools
import math

import jax
import jax.numpy as jnp
import numpy as np
from jax import lax
from jax.experimental import pallas as pl
from jax.experimental.layout import Layout, with_layout_constraint
from jax.experimental.pallas import tpu as pltpu
from jax.sharding import PartitionSpec as P

HEADS = 8
SIDE = 25
STEP = 10
NS_A = 3.4445
NS_B = -4.775
NS_C = 2.0315
CLIP = 0.02
BETA_M = 0.95
LR_M = 0.3
DECAY_M = 0.01
ADAM_B1 = 0.9
ADAM_B2 = 0.999
SOFT = 0.02
SOFT_L1 = 0.05
NO_OBJECT = 0.1
EPS = 1e-05
LOG2E = math.log2(math.e)
F32 = jnp.float32
BF16 = jnp.bfloat16
VMEM_LIMIT = 56 * 1024 * 1024


def cost(micros):
    return pl.CostEstimate(flops=int(micros * 1.1e9), bytes_accessed=int(micros * 3.5e6), transcendentals=0)


def nn(left, right):
    return lax.dot_general(left, right, (((1,), (0,)), ((), ())), preferred_element_type=F32)


def nt(left, right):
    return lax.dot_general(left, right, (((1,), (1,)), ((), ())), preferred_element_type=F32)


def tn(left, right):
    return lax.dot_general(left, right, (((0,), (0,)), ((), ())), preferred_element_type=F32)


BLOCKS = 32
FIRST = (64, 8, 8, 8, 8, 8, 8)
SECOND = (64,) * 4 + (8,) * 14
PIECES = ((0, 1, 4, 5), (8, 9, 12, 13), (2, 3, 10, 11), (6, 7, 14, 15))
PART_A = (64, 64) + (8,) * 6
PART_B = (64, 64) + (8,) * 8
PART_C = (64,) + (8,) * 6


def by_core(value):
    rows = value.shape[0] // BLOCKS
    value = value.reshape(BLOCKS // 2, 2, rows, value.shape[1])
    return value[:, 0], value[:, 1]


def pair_rows(one, two):
    width = one.shape[1]
    both = [part.reshape(BLOCKS, part.shape[0] // BLOCKS, width) for part in (one, two)]
    return jnp.concatenate(both, axis=1).reshape(2 * one.shape[0], width)


def unpair(both):
    both = both.astype(F32)
    half = both.shape[1] // 2
    return [both[:, j * half:(j + 1) * half].reshape(BLOCKS * half, both.shape[2]) for j in range(2)]


def block_rows(me, block, start, count, got_ref, other_ref):
    far = me ^ block
    place = ((far >> 1) & 3) * 4 + (far >> 3)
    cut = slice(start, start + count)
    return jnp.where((far & 1) == 0, got_ref[place, cut, :], other_ref[place, cut, :])


def all_rows(me, start, got_ref, other_ref):
    return jnp.stack([block_rows(me, block, start, 16, got_ref, other_ref) for block in range(BLOCKS)])


def put_blocks(refs, flip, start, value):
    rows = value.shape[0] // BLOCKS
    even, odd = by_core(value)
    refs[0][:, start:start + rows, :] = jnp.where(flip, odd, even).astype(BF16)
    refs[1][:, start:start + rows, :] = jnp.where(flip, even, odd).astype(BF16)


def head_mask(width, head):
    lane = lax.broadcasted_iota(jnp.int32, (1, width), 1)
    depth = width // HEADS
    return jnp.logical_and(lane >= head * depth, lane < (head + 1) * depth).astype(F32).astype(BF16)


def norm_parts(total):
    center = total - jnp.mean(total, axis=-1, keepdims=True)
    spread = jnp.mean(center * center, axis=-1, keepdims=True)
    scale = lax.rsqrt(spread + EPS)
    return center * scale, scale


def norm_back(grad, unit, scale, gain):
    inner = grad * gain
    mean_inner = jnp.mean(inner, axis=-1, keepdims=True)
    mean_cross = jnp.mean(inner * unit, axis=-1, keepdims=True)
    return scale * (inner - mean_inner - unit * mean_cross)


def column_sum(value):
    return jnp.sum(value, axis=0, keepdims=True)


GELU_C = math.sqrt(2.0 / math.pi)
GELU_K = 0.044715 * GELU_C


def gelu_parts(value):
    square = value * value
    half = 0.5 + 0.5 * jnp.tanh(value * (GELU_C + GELU_K * square))
    out = value * half
    slope = half + out * (1.0 - half) * (2.0 * GELU_C + 6.0 * GELU_K * square)
    return out, slope


def masked_softmax(scores, depth, length):
    padded = scores.shape[1]
    start = (padded - 1) // 128 * 128
    if length < padded:
        scores = scores + jnp.where(lax.broadcasted_iota(jnp.int32, (1, padded), 1) < length, 0.0, -1e30)
    factor = LOG2E / math.sqrt(depth)
    top = jnp.max(scores, axis=1, keepdims=True)
    powers = jnp.exp2((scores - top) * factor)
    inverse = 1.0 / jnp.sum(powers, axis=1, keepdims=True)
    return (powers * inverse).astype(BF16)


def encode_kernel(tokens, me_ref, f_ref, got_ref, other_ref, sine_ref,
                  p_ref, keyed_ref, lowm_ref, q_ref, k_ref, v_ref, o_ref, s0_ref, x1_ref, w_ref, norm_ref, win_ref, k_t):
    head = pl.program_id(1)
    width = got_ref.shape[2]

    @pl.when(jnp.logical_and(pl.program_id(0) == 0, head == 0))
    def _():
        rows = FIRST[0]

        sources = (got_ref, other_ref)
        for block in range(BLOCKS):
            win_ref[block * rows:(block + 1) * rows, :] = block_rows(me_ref[0], block, 0, rows, *sources)
        for pair in range(2):
            for j, one in enumerate(unpair(all_rows(me_ref[0], rows + 16 * pair, *sources))):
                w_ref[2 * pair + j] = one.astype(BF16)
        norm_ref[...] = unpair(all_rows(me_ref[0], rows + 32, *sources))[0][:, 0:128].T[0:norm_ref.shape[0], :]

    @pl.when(head == 0)
    def _():
        padded = s0_ref.shape[1]
        s0_ref[0, tokens // 8 * 8:padded, :] = jnp.zeros((padded - tokens // 8 * 8, width), F32)
        s0_ref[0, 0:tokens, :] = nn(f_ref[0], win_ref[...])
        memory = s0_ref[0]
        keyed = (memory + sine_ref[...]).astype(BF16)
        lowm = memory.astype(BF16)
        keyed_ref[0] = keyed
        lowm_ref[0] = lowm
        q_ref[0] = nn(keyed, w_ref[0]).astype(BF16)
        keys = nn(keyed, w_ref[1]).astype(BF16)
        k_ref[0] = keys
        k_t[...] = keys.T
        v_ref[0] = nn(lowm, w_ref[2]).astype(BF16)
        o_ref[...] = jnp.zeros_like(o_ref)

    for at in range(4):
        mask = head_mask(width, head * 4 + at)
        vm = v_ref[0] * mask
        for start in range(0, q_ref.shape[1], 320):
            cut = slice(start, start + 320)
            scores = nn(q_ref[0, cut, :] * mask, k_t[...])
            probs = masked_softmax(scores, width // HEADS, tokens)
            p_ref[0, at, cut, :] = probs
            o_ref[0, cut, :] += nn(probs, vm)

    @pl.when(head == HEADS // 4 - 1)
    def _():
        total = s0_ref[0] + nn(o_ref[0].astype(BF16), w_ref[3])
        s0_ref[0] = total
        unit, scale = norm_parts(total)
        x1_ref[0] = unit * norm_ref[0:1, :] + norm_ref[6:7, :]


def encode(features, me, got, other, sine):
    images, tokens, depth = features.shape
    width = got.shape[2]
    padded = sine.shape[0]
    per_image = lambda kind: jax.ShapeDtypeStruct((images, padded, width), kind)
    image_block = pl.BlockSpec((1, padded, width), lambda i, h: (i, 0, 0))
    whole = lambda shape: pl.BlockSpec(shape, lambda i, h: (0,) * len(shape))
    return pl.pallas_call(
        functools.partial(encode_kernel, tokens),
        grid=(images, HEADS // 4),
        in_specs=[
            pl.BlockSpec(memory_space=pltpu.SMEM), pl.BlockSpec((1, tokens, depth), lambda i, h: (i, 0, 0)),
            whole(got.shape), whole(other.shape), whole(sine.shape),
        ],
        out_specs=[pl.BlockSpec((1, 4, padded, padded), lambda i, h: (i, h, 0, 0))] + [image_block] * 8
        + [whole((4, width, width)), whole((16, width))],
        out_shape=[jax.ShapeDtypeStruct((images, HEADS, padded, padded), BF16)]
        + [per_image(BF16)] * 5 + [per_image(F32)] * 3
        + [jax.ShapeDtypeStruct((4, width, width), BF16), jax.ShapeDtypeStruct((16, width), F32)],
        scratch_shapes=[pltpu.VMEM((depth, width), BF16), pltpu.VMEM((width, padded), BF16)],
        compiler_params=pltpu.CompilerParams(vmem_limit_bytes=VMEM_LIMIT),
        cost_estimate=cost(22),
        name="encode",
    )(me, features, got, other, sine)


def encode_back_kernel(tokens, images, first, last, *refs):
    (me_ref, dx1_ref, s0_ref, norm_ref, p_ref, keyed_ref, lowm_ref, q_ref, k_ref, v_ref, o_ref, w_ref), refs = (
        refs[:12], refs[12:])
    if not first:
        (dsq_in, dnorm_in), refs = refs[:2], refs[2:]
    if last:
        f_refs, refs = refs[:images], refs[images:]
        dm_refs, refs = refs[:images - 1], refs[images - 1:]
        outs, refs = refs[:2], refs[2:]
        *refs, dsq, dnorm_ref = refs
    else:
        (dsq, dnorm_ref, dm_ref), refs = refs[:3], refs[3:]
    ds0, dout, dout_t, q_t, v_t, cross, dq, dk_t, dv_t = refs
    head = pl.program_id(0)
    width = w_ref.shape[1]
    depth = width // HEADS

    @pl.when(head == 0)
    def _():
        dsq[...] = jnp.zeros_like(dsq) if first else dsq_in[...]
        dnorm_ref[...] = jnp.zeros_like(dnorm_ref) if first else dnorm_in[...]

    @pl.when(head == 0)
    def _():
        unit, scale = norm_parts(s0_ref[0])
        grad = dx1_ref[0]
        dnorm_ref[0:1, :] += column_sum(grad * unit)
        dnorm_ref[6:7, :] += column_sum(grad)
        dtotal = norm_back(grad, unit, scale, norm_ref[0:1, :])
        ds0[...] = dtotal
        low = dtotal.astype(BF16)
        dsq[3] += tn(o_ref[0].astype(BF16), low)
        dmixed = nt(low, w_ref[3]).astype(BF16)
        dout[...] = dmixed
        dout_t[...] = dmixed.T
        q_t[...] = q_ref[0].T
        v_t[...] = v_ref[0].T
        cross[...] = dmixed.astype(F32) * o_ref[0]
        dq[...] = jnp.zeros_like(dq)

    for at in range(4):
        one = head * 4 + at
        mask = head_mask(width, one)
        rows = pl.ds(pl.multiple_of(one * depth, depth), depth)
        weight = jnp.sum(cross[...] * mask.astype(F32), axis=1, keepdims=True)
        probs = p_ref[0, at]
        dprobs = nn(dout[...] * mask, v_t[...])
        dscores = (probs.astype(F32) * (dprobs - weight)).astype(BF16)
        dq[...] += nn(dscores, k_ref[0] * mask)
        dk_t[rows, :] = nn(q_t[rows, :], dscores)
        dv_t[rows, :] = nn(dout_t[rows, :], probs)

    @pl.when(head == HEADS // 4 - 1)
    def _():
        factor = 1.0 / math.sqrt(depth)
        dqb = (dq[...] * factor).astype(BF16)
        dkb = (dk_t[...] * factor).astype(BF16).T
        dvb = dv_t[...].astype(BF16).T
        dsq[0] += tn(keyed_ref[0], dqb)
        dsq[1] += tn(keyed_ref[0], dkb)
        dsq[2] += tn(lowm_ref[0], dvb)
        dm = ds0[...] + nt(dqb, w_ref[0]) + nt(dkb, w_ref[1]) + nt(dvb, w_ref[2])
        dmb = dm.astype(BF16)
        if not last:
            dm_ref[0] = dmb
        else:
            parts = [ref[0] for ref in dm_refs] + [dmb]
            dwin = sum(tn(part[0:tokens], ref[0]) for part, ref in zip(parts, f_refs))
            flip = (me_ref[0] & 1) > 0
            rows = PART_C[0]
            put_blocks(outs, flip, 0, dwin.astype(BF16).T)
            for pair in range(2):
                put_blocks(outs, flip, rows + 16 * pair, pair_rows(dsq[2 * pair], dsq[2 * pair + 1]))
            put_blocks(outs, flip, rows + 32, pair_rows(norm_columns(dnorm_ref[...], width), jnp.zeros((width, width), F32)))


def norm_columns(dnorm, width):
    wide = jnp.concatenate([dnorm, jnp.zeros((128 - dnorm.shape[0], width), F32)], axis=0).T
    return jnp.concatenate([wide, jnp.zeros((width, width - 128), F32)], axis=1)


def encode_back(image, images, me, dx1, s0, norm, probs, keyed, lowm, q, k, v, o, square, features, *before):
    _, tokens, channels = features.shape
    padded, width = s0.shape[1:]
    first, last = image == 0, image == images - 1
    image_block = pl.BlockSpec((1, padded, width), lambda h: (image, 0, 0))
    whole = lambda shape: pl.BlockSpec(shape, lambda h: (0,) * len(shape))
    sums = [((4, width, width), F32), (norm.shape, F32)]
    part = ((BLOCKS // 2, sum(PART_C), width), BF16)
    outs = [part, part] if last else sums + [((1, padded, width), BF16)]
    scratch = [((padded, width), F32), ((padded, width), BF16), ((width, padded), BF16), ((width, padded), BF16), ((width, padded), BF16),
               ((padded, width), F32), ((padded, width), F32), ((width, padded), F32), ((width, padded), F32)]
    extra, extra_specs = list(before[:2]), [] if first else [whole(shape) for shape, _ in sums]
    if last:
        extra += [features] * images + list(before[2:])
        extra_specs += [pl.BlockSpec((1, tokens, channels), lambda h, j=j: (j, 0, 0)) for j in range(images)]
        extra_specs += [whole((1, padded, width))] * (images - 1)
    return pl.pallas_call(
        functools.partial(encode_back_kernel, tokens, images, first, last),
        grid=(HEADS // 4,),
        in_specs=[
            pl.BlockSpec(memory_space=pltpu.SMEM), image_block, image_block, whole(norm.shape),
            pl.BlockSpec((1, 4, padded, padded), lambda h: (image, h, 0, 0)),
        ] + [image_block] * 6 + [whole(square.shape)] + extra_specs,
        out_specs=[whole(shape) for shape, _ in outs],
        out_shape=[jax.ShapeDtypeStruct(shape, kind) for shape, kind in outs],
        scratch_shapes=[pltpu.VMEM(shape, kind) for shape, kind in scratch + (sums if last else [])],
        compiler_params=pltpu.CompilerParams(vmem_limit_bytes=VMEM_LIMIT),
        cost_estimate=cost(17 if last else 12),
        name="encode_back",
    )(me, dx1, s0, norm, probs, keyed, lowm, q, k, v, o, square, *extra)


def stack_heads(value):
    return jnp.concatenate([value * head_mask(value.shape[1], head) for head in range(HEADS)], axis=0)


def pick_heads(stacked):
    rows, width = stacked.shape[0] // HEADS, stacked.shape[1]
    lane = lax.broadcasted_iota(jnp.int32, (1, width), 1)
    out = stacked[0:rows]
    for head in range(1, HEADS):
        out = jnp.where(lane >= head * (width // HEADS), stacked[head * rows:(head + 1) * rows], out)
    return out


def soft_gap(gap):
    return SOFT * jnp.log(1.0 + jnp.exp(-jnp.abs(gap) * (1.0 / SOFT)))


def sigmoid(value):
    return 1.0 / (1.0 + jnp.exp(-value))


def axis_terms(center, size, target_center, target_size):
    low_one, high_one = center - size / 2, center + size / 2
    low_two, high_two = target_center - target_size / 2, target_center + target_size / 2
    low_gap, high_gap = low_one - low_two, high_one - high_two
    low_soft, high_soft = soft_gap(low_gap), soft_gap(high_gap)
    inner = (jnp.minimum(high_one, high_two) - high_soft) - (jnp.maximum(low_one, low_two) + low_soft)
    overlap = jnp.maximum(inner, 0.0) + soft_gap(inner)
    hull = (jnp.maximum(high_one, high_two) + high_soft) - (jnp.minimum(low_one, low_two) - low_soft)
    return overlap, hull, sigmoid(inner / SOFT), sigmoid(low_gap / SOFT), sigmoid(high_gap / SOFT)


def box_loss(box, target, mask, box_count):
    l1_sum = 0.0
    grads = []
    for one, two in zip(box, target):
        offset = (one - two) / SOFT_L1
        root = jnp.sqrt(offset * offset + 1.0)
        l1_sum = l1_sum + mask * (SOFT_L1 * (root - 1.0))
        grads.append(5.0 * offset / root)
    ow, hw, pw, lw, uw = axis_terms(box[0], box[2], target[0], target[2])
    oh, hh, ph, lh, uh = axis_terms(box[1], box[3], target[1], target[3])
    inter = ow * oh
    union = box[2] * box[3] + target[2] * target[3] - inter
    hull = hw * hh
    by_union, by_hull = 1.0 / union, 1.0 / hull
    giou = inter * by_union - (hull - union) * by_hull
    share = inter * by_union * by_union
    g_inter = by_union + share - by_hull
    g_area = by_hull - share
    g_hull = -union * by_hull * by_hull
    for axis, (other, hull_other, slope, low_s, high_s, size_other) in enumerate(
        ((oh, hh, pw, lw, uw, box[3]), (ow, hw, ph, lh, uh, box[2]))
    ):
        flow = g_inter * other * slope
        wide = g_hull * hull_other
        g_high = flow * (1.0 - high_s) + wide * high_s
        g_low = -flow * low_s - wide * (1.0 - low_s)
        grads[axis] = grads[axis] - 2.0 * (g_low + g_high)
        grads[axis + 2] = grads[axis + 2] - 2.0 * ((g_high - g_low) / 2 + g_area * size_other)
    value = jnp.sum((5.0 * l1_sum + 2.0 * mask * (1.0 - giou)) / box_count, axis=1, keepdims=True)
    return value, [grad * mask / box_count for grad in grads]


def middle_kernel(tokens, queries, classes, inverse, count_rows, me_ref, x1_ref, sine_ref, norm_ref,
                  col_ref, row_ref, got0, got1, got2, got3, other0, other1, other2, other3,
                  dx1_ref, keepa_ref, senda_ref, keepb_ref, sendb_ref, loss_ref, box_ref, feed_ref, rest_ref, dsq_ref, dnorm_ref, w_ref, head_ref, g0, total1, tall_g, tall_s, small_g, small_s, kin, vin, kk, vv, probs2, mixed2, dsum, dq2, dmix2):
    images, padded, width = x1_ref.shape
    depth = width // HEADS
    rows_feed = FIRST[0]
    chunks = BLOCKS * rows_feed // width
    per_chunk = BLOCKS // chunks
    many = images * padded
    qrows = round_up(queries, 128)
    factor = 1.0 / math.sqrt(depth)
    gain = lambda row: norm_ref[row:row + 1, :]
    dnorm_ref[...] = jnp.zeros_like(dnorm_ref)

    me = me_ref[0]
    for core, sources in enumerate(((got0, got1, got2, got3), (other0, other1, other2, other3))):
        for source, spots in zip(sources, PIECES):
            for entry, spot in enumerate(spots):
                block = me ^ ((spot % 4) * 8 + (spot // 4) * 2 + core)
                place = pl.ds(pl.multiple_of(block * rows_feed, rows_feed), rows_feed)
                for which in range(4):
                    feed_ref[which, place, :] = source[entry, which * rows_feed:(which + 1) * rows_feed, :]
                rest_ref[block] = source[entry, 4 * rows_feed:, :]
    for pair in range(5):
        for j, one in enumerate(unpair(rest_ref[:, 16 * pair:16 * pair + 16, :])):
            w_ref[2 * pair + j] = one.astype(BF16)
    head_one, found = unpair(rest_ref[:, 80:96, :])
    head_ref[...] = head_one[:, 0:head_ref.shape[1]].astype(BF16)
    box_count = jnp.sum(found[:, 0:1], axis=0, keepdims=True) * (1.0 / count_rows)
    box_ref[...] = box_count
    content, place = [one[:, 0:qrows].T for one in unpair(rest_ref[:, 96:112, :])]

    def weights(which, layer, chunk):
        return feed_ref[2 * which + layer, pl.ds(pl.multiple_of(chunk * width, width), width), :]

    flip = (me & 1) > 0
    out_a, out_b = (keepa_ref, senda_ref), (keepb_ref, sendb_ref)

    def put_feed(which, layer, chunk, value):
        value = value.reshape(per_chunk // 2, 2, rows_feed, width)
        place = pl.ds(chunk * (per_chunk // 2), per_chunk // 2), slice(layer * rows_feed, (layer + 1) * rows_feed)
        keep, send = out_b if which else out_a
        keep[place] = jnp.where(flip, value[:, 1], value[:, 0])
        send[place] = jnp.where(flip, value[:, 0], value[:, 1])

    def feed(layer, source, g_ref, s_ref, out_ref):
        def step(chunk, carry):
            value, slope = gelu_parts(nt(source, weights(0, layer, chunk)))
            value = value.astype(BF16)
            g_ref[chunk] = value
            s_ref[chunk] = slope.astype(BF16)
            out_ref[...] += nn(value, weights(1, layer, chunk))
            return carry
        lax.fori_loop(0, chunks, step, 0, unroll=True)

    def feed_back(layer, source_t, grad, grad_t, g_ref, s_ref, out_ref):
        def step(chunk, carry):
            dg = nt(grad, weights(1, layer, chunk)).astype(BF16)
            du = (dg.astype(F32) * s_ref[chunk].astype(F32)).astype(BF16)
            put_feed(1, layer, chunk, nn(grad_t, g_ref[chunk]).astype(BF16).T)
            put_feed(0, layer, chunk, nn(source_t, du).astype(BF16).T)
            out_ref[...] += nn(du, weights(0, layer, chunk))
            return carry
        lax.fori_loop(0, chunks, step, 0, unroll=True)

    x1 = x1_ref[...].reshape(many, width)
    total1[...] = x1
    feed(0, x1.astype(BF16), tall_g, tall_s, total1)
    unit1, scale1 = norm_parts(total1[...])
    x2 = unit1 * gain(1) + gain(7)
    for image in range(images):
        part = x2[image * padded:(image + 1) * padded]
        keyed = (part + sine_ref[...]).astype(BF16)
        lowm = part.astype(BF16)
        kin[image] = keyed
        vin[image] = lowm
        kk[image] = nn(keyed, w_ref[5]).astype(BF16)
        vv[image] = nn(lowm, w_ref[6]).astype(BF16)

    asked = (content + place).astype(BF16)
    lowc = content.astype(BF16)
    q1 = nn(asked, w_ref[0]).astype(BF16)
    k1 = nn(asked, w_ref[1]).astype(BF16)
    v1 = nn(lowc, w_ref[2]).astype(BF16)
    q1s = stack_heads(q1)
    p1 = masked_softmax(nt(q1s, k1), depth, queries)
    mix1 = pick_heads(nn(p1, v1))
    mix1b = mix1.astype(BF16)
    unit2, scale2 = norm_parts(content + nn(mix1b, w_ref[3]))
    t1 = unit2 * gain(2) + gain(8)

    asked2 = (t1 + place).astype(BF16)
    q2 = nn(asked2, w_ref[4]).astype(BF16)
    q2s = stack_heads(q2)

    def cross(image, carry):
        probs = masked_softmax(nt(q2s, kk[image]), depth, tokens)
        probs2[image] = probs
        mixed2[image] = pick_heads(nn(probs, vv[image]))
        return carry
    lax.fori_loop(0, images, cross, 0, unroll=True)
    rows = images * qrows
    mix2 = mixed2[...].reshape(rows, width)
    mix2b = mix2.astype(BF16)
    t1s = jnp.concatenate([t1] * images, axis=0)
    unit3, scale3 = norm_parts(t1s + nn(mix2b, w_ref[7]))
    t2 = unit3 * gain(3) + gain(9)

    t2b = t2.astype(BF16)
    g0[...] = t2
    feed(1, t2b, small_g, small_s, g0)
    unit4, scale4 = norm_parts(g0[...])
    t3 = unit4 * gain(4) + gain(10)
    unit5, scale5 = norm_parts(t3)
    out = (unit5 * gain(5) + gain(11)).astype(BF16)

    logits = nn(out, head_ref[...])
    lane = lax.broadcasted_iota(jnp.int32, logits.shape, 1)
    weight = col_ref[:, 0:1]
    label = col_ref[:, 1:2].astype(jnp.int32)
    kept = jnp.where(lane < classes, logits, -1e30)
    top = jnp.max(kept, axis=1, keepdims=True)
    powers = jnp.exp(kept - top)
    norm_sum = jnp.sum(powers, axis=1, keepdims=True)
    chosen = lane == label
    ce = top + jnp.log(norm_sum) - jnp.sum(jnp.where(chosen, logits, 0.0), axis=1, keepdims=True)
    ce_sum = jnp.sum(weight * ce, axis=0, keepdims=True)
    dlogits = ((weight * inverse) * (powers / norm_sum - jnp.where(chosen, 1.0, 0.0))).astype(BF16)

    b1, slope_one = gelu_parts(nn(out, w_ref[8]))
    b1 = b1.astype(BF16)
    b2, slope_two = gelu_parts(nn(b1, w_ref[9]))
    b2 = b2.astype(BF16)
    raw = nn(b2, head_ref[...]).T
    box = [sigmoid(raw[classes + j:classes + j + 1, :]) for j in range(4)]
    target = [row_ref[1 + j:2 + j, :] for j in range(4)]
    box_value, dbox = box_loss(box, target, row_ref[0:1, :], box_count)
    loss_ref[...] = ce_sum * inverse + box_value
    draw = jnp.concatenate([grad * one * (1.0 - one) for grad, one in zip(dbox, box)], axis=0)
    lanes_in = head_ref.shape[1]
    spot = lax.broadcasted_iota(jnp.int32, (lanes_in, rows), 0)
    spread = jnp.zeros((lanes_in, rows), F32)
    for j in range(4):
        spread = jnp.where(spot == classes + j, draw[j:j + 1, :], spread)
    draw_rows = spread.T.astype(BF16)

    dhead = tn(out, dlogits) + tn(b2, draw_rows)
    du2 = (nt(draw_rows, head_ref[...]) * slope_two).astype(BF16)
    dsq_ref[9] = tn(b1, du2)
    du1 = (nt(du2, w_ref[9]) * slope_one).astype(BF16)
    dsq_ref[8] = tn(out, du1)
    dout = nt(dlogits, head_ref[...]) + nt(du1, w_ref[8])

    def through(grad, unit, scale, row):
        dnorm_ref[row:row + 1, :] = column_sum(grad * unit)
        dnorm_ref[row + 6:row + 7, :] = column_sum(grad)
        return norm_back(grad, unit, scale, gain(row))

    dt3 = through(dout, unit5, scale5, 5)
    ds3 = through(dt3, unit4, scale4, 4)
    g0[...] = ds3
    ds3b = ds3.astype(BF16)
    feed_back(1, t2b.T, ds3b, ds3b.T, small_g, small_s, g0)
    ds2 = through(g0[...], unit3, scale3, 3)
    ds2b = ds2.astype(BF16)
    dsq_ref[7] = tn(mix2b, ds2b)
    dmix2[...] = nt(ds2b, w_ref[7]).astype(BF16).reshape(images, qrows, width)
    dq2[...] = jnp.zeros_like(dq2)
    dsum[...] = jnp.zeros_like(dsum)

    def attention_back(dmix, mix, probs, stacked_q, keys, values):
        dms = stack_heads(dmix)
        both = dmix.astype(F32) * mix
        weight = jnp.concatenate(
            [jnp.sum(both * head_mask(width, head).astype(F32), axis=1, keepdims=True) for head in range(HEADS)],
            axis=0,
        )
        dscores = (probs.astype(F32) * (nt(dms, values) - weight)).astype(BF16)
        dq = pick_heads(nn(dscores, keys)) * factor
        dk = (tn(stacked_q, dscores) * factor).astype(BF16).T
        dv = tn(dms, probs).astype(BF16).T
        return dq, dk, dv

    def cross_back(image, carry):
        dq, dk, dv = attention_back(dmix2[image], mixed2[image], probs2[image], q2s, kk[image], vv[image])
        dq2[...] += dq
        dsum[0] += tn(kin[image], dk)
        dsum[1] += tn(vin[image], dv)
        dx1_ref[image] = nt(dk, w_ref[5]) + nt(dv, w_ref[6])
        return carry
    lax.fori_loop(0, images, cross_back, 0, unroll=True)
    dsq_ref[5] = dsum[0]
    dsq_ref[6] = dsum[1]
    dq2b = dq2[...].astype(BF16)
    dsq_ref[4] = tn(asked2, dq2b)
    dasked2 = nt(dq2b, w_ref[4])
    dt1 = dasked2
    for image in range(images):
        dt1 = dt1 + ds2[image * qrows:(image + 1) * qrows]
    ds1 = through(dt1, unit2, scale2, 2)
    ds1b = ds1.astype(BF16)
    dsq_ref[3] = tn(mix1b, ds1b)
    dmix1 = nt(ds1b, w_ref[3]).astype(BF16)
    dq, dk, dv = attention_back(dmix1, mix1, p1, q1s, k1, v1)
    dqb = dq.astype(BF16)
    dsq_ref[0] = tn(asked, dqb)
    dsq_ref[1] = tn(asked, dk)
    dsq_ref[2] = tn(lowc, dv)
    dasked = nt(dqb, w_ref[0]) + nt(dk, w_ref[1])
    dquery = [ds1 + dasked + nt(dv, w_ref[2]), dasked + dasked2]

    unit, scale = norm_parts(total1[...])
    dx2 = dx1_ref[...].reshape(many, width)
    ds = through(dx2, unit, scale, 1)
    total1[...] = ds
    dsb = ds.astype(BF16)
    x1b = x1_ref[...].reshape(many, width).astype(BF16)
    feed_back(0, x1b.T, dsb, dsb.T, tall_g, tall_s, total1)
    dx1_ref[...] = total1[...].reshape(images, padded, width)

    wide = lambda value: jnp.concatenate([value, jnp.zeros((value.shape[0], width - value.shape[1]), F32)], axis=1)
    at = 2 * rows_feed
    for pair in range(3):
        put_blocks(out_a, flip, at + 16 * pair, pair_rows(dsq_ref[2 * pair], dsq_ref[2 * pair + 1]))
    for pair in range(2):
        put_blocks(out_b, flip, at + 16 * pair, pair_rows(dsq_ref[6 + 2 * pair], dsq_ref[7 + 2 * pair]))
    put_blocks(out_b, flip, at + 32, pair_rows(wide(dhead), norm_columns(dnorm_ref[...], width)))
    put_blocks(out_b, flip, at + 48, pair_rows(wide(dquery[0].T), wide(dquery[1].T)))


def middle(me, x1, sine, norm, col, row, pieces, tokens, queries, classes, inverse, count_rows):
    images, padded, width = x1.shape
    qrows = round_up(queries, 128)
    chunks = BLOCKS * FIRST[0] // width
    many, rows = images * padded, images * qrows
    vmem = pl.BlockSpec(memory_space=pltpu.VMEM)
    shapes = [
        ((images, padded, width), F32), ((BLOCKS // 2, sum(PART_A), width), BF16),
        ((BLOCKS // 2, sum(PART_A), width), BF16), ((BLOCKS // 2, sum(PART_B), width), BF16),
        ((BLOCKS // 2, sum(PART_B), width), BF16), ((1, 1), F32), ((1, 1), F32),
    ]
    return pl.pallas_call(
        functools.partial(middle_kernel, tokens, queries, classes, inverse, count_rows),
        in_specs=[pl.BlockSpec(memory_space=pltpu.SMEM)] + [vmem] * (5 + len(pieces)),
        out_specs=[vmem] * len(shapes),
        out_shape=[jax.ShapeDtypeStruct(shape, kind) for shape, kind in shapes],
        scratch_shapes=[
            pltpu.VMEM((4, chunks * width, width), BF16), pltpu.VMEM((BLOCKS, sum(SECOND) - 4 * FIRST[0], width), BF16),
            pltpu.VMEM((10, width, width), F32), pltpu.VMEM((16, width), F32),
            pltpu.VMEM((10, width, width), BF16), pltpu.VMEM((width, 128), BF16),
            pltpu.VMEM((rows, width), F32), pltpu.VMEM((many, width), F32),
            pltpu.VMEM((chunks, many, width), BF16), pltpu.VMEM((chunks, many, width), BF16),
            pltpu.VMEM((chunks, rows, width), BF16), pltpu.VMEM((chunks, rows, width), BF16),
            pltpu.VMEM((images, padded, width), BF16), pltpu.VMEM((images, padded, width), BF16),
            pltpu.VMEM((images, padded, width), BF16), pltpu.VMEM((images, padded, width), BF16),
            pltpu.VMEM((images, HEADS * qrows, padded), BF16), pltpu.VMEM((images, qrows, width), F32),
            pltpu.VMEM((2, width, width), F32), pltpu.VMEM((qrows, width), F32),
            pltpu.VMEM((images, qrows, width), BF16),
        ],
        compiler_params=pltpu.CompilerParams(vmem_limit_bytes=VMEM_LIMIT),
        cost_estimate=cost(35),
        name="middle",
    )(me, x1, sine, norm, col, row, *pieces)


def sine_table(width, padded):
    cells = np.arange(SIDE * SIDE)
    half = width // 2
    index = np.arange(half)
    freqs = 10000.0 ** ((2 * (index // 2)) / half)
    parts = []
    for coord in (cells // SIDE + 1, cells % SIDE + 1):
        angle = (coord / (SIDE + 1e-06) * (2.0 * math.pi))[:, None] / freqs[None, :]
        parts.append(np.where(index[None, :] % 2 == 0, np.sin(angle), np.cos(angle)))
    table = np.concatenate(parts, axis=1).astype(np.float32)
    return np.concatenate([table, np.zeros((padded - table.shape[0], width), np.float32)], axis=0)


def round_up(value, unit):
    return -(-value // unit) * unit


def target_info(matches, labels, boxes, classes, qrows):
    images, queries = matches.shape
    pad = ((0, 0), (0, qrows - queries))
    matched = matches >= 0
    picker = matches[:, :, None] == jnp.arange(labels.shape[1])[None, None, :]
    label = jnp.where(matched, jnp.sum(jnp.where(picker, labels[:, None, :], 0), axis=2), classes - 1)
    weight = jnp.pad(jnp.where(matched, 1.0, NO_OBJECT), pad)
    label = jnp.pad(label, pad).astype(F32)
    col = jnp.stack([weight.reshape(-1), label.reshape(-1)], axis=1)
    mask = jnp.pad(matched.astype(F32), pad).reshape(1, -1)
    wanted = []
    for j in range(4):
        one = jnp.sum(jnp.where(picker, boxes[:, None, :, j], 0.0), axis=2)
        wanted.append(jnp.pad(jnp.where(matched, one, 0.5), pad, constant_values=0.5).reshape(1, -1))
    row = jnp.concatenate([mask] + wanted + [jnp.zeros((3, mask.shape[1]), F32)], axis=0)
    return col, row


AXES = ("dp", "fsdp")


def swap(value, bit, devices):
    return lax.ppermute(value, AXES, [(i, i ^ bit) for i in range(devices)])


def bits_of(devices):
    return [1 << j for j in range(devices.bit_length() - 1)]


def groups_of(devices):
    bits = bits_of(devices)
    return [(bits[j], bits[j + 1]) for j in range(len(bits) - 2, 0, -2)]


def place_of(far, devices):
    place = 0
    for low, _ in reversed(groups_of(devices)):
        place = place * 4 + (far // low) % 4
    return place


def gather_four(held, pair, devices):
    low, high = pair
    return [held] + [swap(held, bits, devices) for bits in (low, high, low | high)]


def gather_round(held, pair, devices):
    return jnp.concatenate(gather_four(held, pair, devices))


def natural_order(got, other, me, pieces):
    devices = 2 * got.shape[0]
    both = jnp.concatenate([got, other])
    table = jnp.asarray([(j & 1) * (devices // 2) + place_of(j, devices) for j in range(devices)])
    blocks = join(both[table[jnp.arange(devices) ^ me]], pieces)
    chips = sorted(range(0, BLOCKS, 2), key=lambda block: place_of(block, BLOCKS))
    return [jnp.stack([blocks[block + core] for block in chips]) for core in range(2)]


def join(got, pieces):
    ratio = got.shape[0] // BLOCKS
    if ratio == 1:
        return got
    got = got.reshape(BLOCKS, ratio, got.shape[1], got.shape[2])
    out, at = [], 0
    for piece in pieces:
        rows = piece // ratio
        out.append(got[:, :, at:at + rows].reshape(BLOCKS, piece, got.shape[3]))
        at += rows
    return jnp.concatenate(out, axis=1)


def launch(keep, send, pieces, devices):
    bits = bits_of(devices)
    ratio = devices // BLOCKS
    tail = keep.shape[1:]
    if ratio == 1:
        shape = (2,) * (len(bits) - 1) + tail
        return swap(send, bits[0], devices).reshape(shape), keep.reshape(shape), list(reversed(bits[1:]))
    value = jnp.stack([keep, send], axis=1).reshape((BLOCKS,) + tail)
    out, at = [], 0
    for piece in pieces:
        out.append(value[:, at:at + piece].reshape(devices, piece // ratio, tail[1]))
        at += piece
    out = jnp.concatenate(out, axis=1)
    out = out.reshape((2,) * len(bits) + out.shape[1:])
    left = list(reversed(bits))
    return advance((jnp.zeros_like(out), out, left), bits[0], devices)


def halves(flight, bit):
    came, kept, left = flight
    axis = left.index(bit)
    mine = (lax.axis_index(AXES) // bit) % 2
    pick = lambda value, at: lax.dynamic_index_in_dim(value, at, axis, keepdims=False).astype(F32)
    out = (pick(kept, 1 - mine) + pick(came, 1 - mine)).astype(BF16)
    return out, pick(kept, mine) + pick(came, mine), [one for one in left if one != bit]


def advance(flight, bit, devices):
    out, kept, left = halves(flight, bit)
    return swap(out, bit, devices), kept, left


def parts_of_four(flight, low, high, devices):
    *addends, left = flight
    axes = [left.index(bit) for bit in (low, high)]
    mine = [(lax.axis_index(AXES) // bit) % 2 for bit in (low, high)]
    out = []
    for bits in (low, high, low | high, 0):
        total = 0.0
        for value in addends:
            for axis, bit, at in sorted(zip(axes, (low, high), mine), key=lambda one: -one[0]):
                at = 1 - at if bits & bit else at
                value = lax.dynamic_index_in_dim(value, at, axis, keepdims=False)
            total = total + value.astype(F32)
        out.append(total.astype(BF16) if bits else total)
    return out


def send_four(parts, flight, low, high, devices):
    came = [swap(one, bits, devices) for one, bits in zip(parts, (low, high, low | high))]
    return (parts[3], *came, [bit for bit in flight[-1] if bit not in (low, high)])


def exact(left, right, dims=((1,), (0,))):
    return lax.dot_general(left, right, (dims, ((), ())), precision=lax.Precision.HIGHEST, preferred_element_type=F32)


def gram_kernel(mom_ref, grad_ref, x_ref, gram_ref, sums_ref):
    slot = mom_ref.shape[1]
    devices, _, width = grad_ref.shape
    sums = jnp.sum(grad_ref[:, slot:, :].astype(F32), axis=0)
    sums_ref[...] = sums
    squares = jnp.sum(sums[0:1, 0:3], axis=1, keepdims=True)
    factor = jnp.minimum(1.0, CLIP / (jnp.sqrt(squares) + 1e-06))
    x = BETA_M * mom_ref[...].astype(F32) + factor * grad_ref[:, :slot, :].astype(F32)
    x = x.reshape(devices * slot, width)
    x_ref[...] = x
    gram = exact(x, x, ((0,), (0,)))
    half = width // 2
    for at, (top, left) in enumerate(((0, 0), (0, half), (half, half))):
        gram_ref[at * half:(at + 1) * half, :] = gram[top:top + half, left:left + half]


def rough(left, right):
    left_high, right_high = left.astype(BF16), right.astype(BF16)
    left_low = (left - left_high.astype(F32)).astype(BF16)
    right_low = (right - right_high.astype(F32)).astype(BF16)
    return nn(left_high, right_high) + (nn(left_high, right_low) + nn(left_low, right_high))


def polish_kernel(x_ref, gram_ref, one_ref, two_ref, three_ref, out_ref):
    packed = (gram_ref[...] + one_ref[...]) + (two_ref[...] + three_ref[...])
    half = packed.shape[1]
    first, cross, last = [packed[at * half:(at + 1) * half] for at in range(3)]
    gram = jnp.concatenate([
        jnp.concatenate([first, cross], axis=1), jnp.concatenate([cross.T, last], axis=1)], axis=0)
    diagonal = lax.broadcasted_iota(jnp.int32, gram.shape, 0) == lax.broadcasted_iota(jnp.int32, gram.shape, 1)
    eye = jnp.where(diagonal, 1.0, 0.0)
    square = jnp.sum(jnp.sum(gram * eye, axis=1, keepdims=True), axis=0, keepdims=True)
    scale = 1.0 / (jnp.sqrt(square) + 1e-07)
    gram = gram * (scale * scale)
    total = None
    for sweep in range(5):
        product = exact if sweep < 2 else rough
        poly = NS_A * eye + NS_B * gram + NS_C * product(gram, gram)
        total = poly if sweep == 0 else product(total, poly)
        if sweep < 4:
            gram = product(product(poly, gram), poly)
    out = rough(x_ref[...] * scale, total)
    out_ref[...] = out.reshape(out_ref.shape).astype(out_ref.dtype)


def plain_call(body, shapes, *args, near=()):
    vmem = pl.BlockSpec(memory_space=pltpu.VMEM)
    args = [pltpu.with_memory_space_constraint(arg, pltpu.VMEM) if at in near else arg for at, arg in enumerate(args)]
    return pl.pallas_call(
        body,
        in_specs=[vmem] * len(args),
        out_specs=[vmem] * len(shapes),
        out_shape=[
            pltpu.VMEM(shape, kind) if stays else jax.ShapeDtypeStruct(shape, kind)
            for shape, kind, *stays in shapes],
        compiler_params=pltpu.CompilerParams(vmem_limit_bytes=VMEM_LIMIT),
        cost_estimate=cost(2),
        name=body.__name__,
    )(*args)


def to_slots(square, feeds, devices):
    count, rows, width = square.shape
    slot = feeds.shape[1] // 4
    feed_slots = feeds.reshape(feeds.shape[0] * 4, slot, width)
    square_slots = jnp.pad(square, ((0, devices - count - feed_slots.shape[0]), (0, slot - rows), (0, 0)))
    return jnp.concatenate([feed_slots, square_slots], axis=0)


def exchange(slots):
    return lax.all_to_all(slots, AXES, split_axis=0, concat_axis=0, tiled=True)


def adam(weight, first, second, gradient, rate, decay):
    first = ADAM_B1 * first + (1.0 - ADAM_B1) * gradient
    second = ADAM_B2 * second + (1.0 - ADAM_B2) * gradient * gradient
    fixed_first = first / (1.0 - ADAM_B1**STEP)
    fixed_second = second / (1.0 - ADAM_B2**STEP)
    weight = weight * (1.0 - rate * decay) - rate * fixed_first / (jnp.sqrt(fixed_second) + 1e-08)
    return weight, first, second, weight.astype(BF16)


def muon(weight, ortho, longest):
    fresh = weight * (1.0 - LR_M * DECAY_M) - LR_M * 0.2 * math.sqrt(longest) * ortho
    return fresh, fresh.astype(BF16)


def pack_kernel(win_ref, sq_ref, ex_ref, re_ref, head_ref, query_ref, norm_ref, matches_ref, one_ref, two_ref):
    one, two = pack(win_ref[...], sq_ref[...], ex_ref[...], re_ref[...], head_ref[...], query_ref[...], norm_ref[...],
                    matches_ref[...])
    one_ref[...] = one
    two_ref[...] = two


def pack(win, sq, ex, re, head, query, norm, matches):
    width = win.shape[1]
    rows = sq.shape[1]
    wide = lambda value: jnp.concatenate([value, jnp.zeros((value.shape[0], width - value.shape[1]), F32)], axis=1)
    flat = lambda value: [value[j] for j in range(value.shape[0])]
    found = jnp.where(matches >= 0, 1.0, 0.0)
    found = jnp.sum(jnp.sum(found, axis=1, keepdims=True), axis=0, keepdims=True)
    one = [win] + flat(sq[:4]) + [wide(norm), jnp.zeros((rows, width), F32)]
    two = flat(ex) + flat(re) + flat(sq[4:]) + [wide(head), jnp.broadcast_to(found, (rows, width))]
    two = two + [wide(query[0]), wide(query[1])]
    return jnp.concatenate(one).astype(BF16), jnp.concatenate(two).astype(BF16)


def per_device(devices, features, matches, target_labels, target_boxes,
               square_weight, square_momentum, expand_weight, expand_momentum, reduce_weight, reduce_momentum,
               input_weight, input_momentum, input_second, head_weight, head_momentum, head_second,
               query_weight, query_momentum, query_second, norm_weight, norm_momentum, norm_second):
    images, tokens, channels = features.shape
    count, rs, width = square_weight.shape
    pairs, _, rf = expand_weight.shape
    ri = input_weight.shape[0]
    rh, head_lanes = head_weight.shape
    _, queries, rq = query_weight.shape
    norms, rn = norm_weight.shape
    classes = head_lanes - 4
    padded, qrows = round_up(tokens, 128), round_up(queries, 128)
    hidden = rf * devices
    aligned = devices == BLOCKS

    shards = (input_weight, square_weight, jnp.transpose(expand_weight, (0, 2, 1)), reduce_weight, head_weight,
              jnp.transpose(query_weight, (0, 2, 1)), norm_weight.T, matches)
    if aligned:
        first, second = plain_call(
            pack_kernel, [((sum(FIRST), width), BF16), ((sum(SECOND), width), BF16)], *shards)
    else:
        first, second = lax.optimization_barrier(pack(*shards))
    sine = jnp.asarray(sine_table(width, padded))
    laid = with_layout_constraint(features, Layout(major_to_minor=(0, 1, 2)))
    info = target_info(matches, target_labels, target_boxes, classes, qrows)
    expand_momentum_t = jnp.transpose(expand_momentum, (0, 2, 1))
    mom_slots = to_slots(
        square_momentum, jnp.concatenate([expand_momentum_t, reduce_momentum]), devices).astype(BF16)

    held_one, held_two = first[None], second[None]
    pairs_of_bits = groups_of(devices)
    for pair in pairs_of_bits[:-1]:
        held_one, held_two = lax.optimization_barrier((gather_round(held_one, pair, devices), held_two))
        held_one, (col, row) = lax.optimization_barrier((held_one, info))
        four = gather_four(held_two, pair, devices)
        held_two = jnp.concatenate(four) if pair != pairs_of_bits[-2] else None
    near, far = pairs_of_bits[-1]
    held_one = gather_round(held_one, pairs_of_bits[-1], devices)
    held_one, four, laid, mom_slots = lax.optimization_barrier((held_one, four, laid, mom_slots))
    mom_in = exchange(mom_slots)
    two_a, two_b = jnp.concatenate(four[:2]), jnp.concatenate(four[2:])
    other_one = swap(held_one, 1, devices)
    two_a = jnp.concatenate([two_a, swap(two_a, near, devices)])
    two_b = jnp.concatenate([two_b, swap(two_b, far, devices)])
    held_one, other_one, two_a, two_b = lax.optimization_barrier((held_one, other_one, two_a, two_b))
    far_a, far_b = swap(two_a, far, devices), swap(two_b, near, devices)
    me = lax.axis_index(AXES)
    if not aligned:
        held_one, other_one = natural_order(held_one, other_one, me, FIRST)
        me = jnp.zeros((), jnp.int32)
    me = me.reshape(1)

    inverse = 1.0 / (images * devices * queries)
    probs, keyed, lowm, q, k, v, o, s0, x1, sq_one, norm_all = encode(laid, me, held_one, other_one, sine)
    far_a, far_b, x1, mom_in = lax.optimization_barrier((far_a, far_b, x1, mom_in))
    pieces_two = [two_a, far_a, two_b, far_b]
    pieces_two = pieces_two + [swap(one, 1, devices) for one in pieces_two]
    if not aligned:
        half = two_a.shape[0] // 2
        both = []
        for a, ax, b, by in (pieces_two[:4], pieces_two[4:]):
            both.append(jnp.concatenate([
                a[:half], b[:half], a[half:], by[:half], ax[:half], b[half:], ax[half:], by[half:]]))
        both = natural_order(*both, lax.axis_index(AXES), SECOND)
        pieces_two = [jnp.stack([one[spot] for spot in spots]) for one in both for spots in PIECES]
    dx1, keep_a, send_a, keep_b, send_b, loss, box_total = middle(
        me, x1, sine, norm_all, col, row, pieces_two, tokens, queries, classes, inverse, rs)

    bits = bits_of(devices)
    near, far = bits[1], bits[2]
    turns = [(near, far), (far, near)]
    flight_a, flight_b = launch(keep_a, send_a, PART_A, devices), launch(keep_b, send_b, PART_B, devices)
    sums = ()
    for image in range(images):
        if image and turns:
            half_a, half_b = [halves(flight, bit) for flight, bit in zip((flight_a, flight_b), turns.pop(0))]
            sums, (out_a, out_b) = lax.optimization_barrier((sums, (half_a[0], half_b[0])))
            flight_a = (swap(out_a, near, devices),) + half_a[1:]
            flight_b = (swap(out_b, far, devices),) + half_b[1:]
        sums = encode_back(
            image, images, me, dx1, s0, norm_all, probs, keyed, lowm, q, k, v, o, sq_one, laid, *sums)
    sums, ready_a, ready_b = lax.optimization_barrier((sums, flight_a[:2], flight_b[:2]))
    flight_a, flight_b = (*ready_a, flight_a[2]), (*ready_b, flight_b[2])
    flight_c = launch(*sums, PART_C, devices)
    for bit_a, bit_b in turns:
        flight_a, flight_b = advance(flight_a, bit_a, devices), advance(flight_b, bit_b, devices)
    rest = [bit for bit in bits if bit not in (bits[0], near, far)]
    half_a, half_b = halves(flight_a, rest[0]), halves(flight_b, rest[0])
    out, kept = [jnp.concatenate([a, b], axis=-2) for a, b in zip(half_a[:2], half_b[:2])]
    flight = (swap(out, rest[0], devices), kept, half_a[2])
    for bit in rest[1:]:
        flight = advance(flight, bit, devices)
    for pair in reversed(pairs_of_bits):
        flight_c = send_four(parts_of_four(flight_c, *pair, devices), flight_c, *pair, devices)

    rows_ab, rows_c = sum(PART_A + PART_B) * BLOCKS // devices, sum(PART_C) * BLOCKS // devices
    slot = rf // 4
    ready, ready_c = flight[:-1], flight_c[:-1]
    shapes = [((rows_ab, width), F32, 1), ((rows_c, width), F32, 1), ((devices, slot + 8, width), BF16, 1)]
    if aligned:
        sum_ab, sum_c, grad_slots = plain_call(prepare_kernel, shapes, *ready, *ready_c, loss, near=range(len(ready) + len(ready_c)))
    else:
        sum_ab, sum_c, grad_slots = prepare(ready, ready_c, loss, devices, lambda value: lax.reduce_precision(value, 8, 7))
    grad_in = exchange(grad_slots)
    x, gram, sums = plain_call(
        gram_kernel, [((devices * slot, width), F32, 1), ((3 * width // 2, width // 2), F32, 1), ((8, width), F32, 1)],
        mom_in, grad_in, near=(1,))
    feeds = 8 * pairs
    came = [lax.ppermute(gram, AXES, [(i, i ^ bits) for i in range(feeds)]) for bits in (2, 3, 1)]
    back = exchange(plain_call(
        polish_kernel, [((devices, slot, width), BF16, 1)], x, gram, *came, near=range(5))[0])

    turn = lambda value: jnp.transpose(value, (0, 2, 1))
    states = (square_momentum, expand_momentum_t, reduce_momentum,
              input_weight, input_momentum, input_second, head_weight, head_momentum, head_second,
              turn(query_weight), turn(query_momentum), turn(query_second),
              norm_weight.T, norm_momentum.T, norm_second.T)
    weights = (square_weight, turn(expand_weight), reduce_weight)
    if aligned:
        like = lambda value, kind: (value.shape, kind)
        shapes = [like(value, F32) for value in states[:3]]
        for value in states[3::3]:
            shapes += [like(value, F32)] * 3 + [like(value, BF16)]
        new = plain_call(adapt_kernel, shapes + [((1, 1), F32)] * 2, sum_ab, sum_c, sums, *states, near=range(3))
        shapes = [like(value, kind) for value in weights for kind in (F32, BF16)]
        fresh = plain_call(apply_kernel, shapes, back, *weights, near=(0,))
    else:
        new = adapt(sum_ab, sum_c, sums, *states)
        fresh = apply(back, hidden, *weights)
    square_mom, expand_mom, reduce_mom = new[:3]
    query_out = [turn(value) for value in new[11:15]]
    norm_out = [value.T for value in new[15:19]]
    return (
        (fresh[0], square_mom, fresh[1], turn(fresh[2]), turn(expand_mom), turn(fresh[3]),
         fresh[4], reduce_mom, fresh[5]) + tuple(new[3:11]) + tuple(query_out) + tuple(norm_out)
        + (new[19].reshape(()), box_total.reshape(()), new[20].reshape(()))
    )


def row_parts(sum_ab, sum_c):
    rf = sum_c.shape[0] * PART_C[0] // sum(PART_C)
    rs = rf // 8
    cut = lambda value, start, rows: value[start:start + rows]
    half = 2 * rf + 6 * rs
    feeds = [cut(sum_ab, j * rf, rf) for j in range(2)] + [cut(sum_ab, half + j * rf, rf) for j in range(2)]
    squares = [cut(sum_c, rf + j * rs, rs) for j in range(4)]
    squares += [cut(sum_ab, 2 * rf + j * rs, rs) for j in range(6)]
    at = half + 2 * rf
    squares += [cut(sum_ab, at + j * rs, rs) for j in range(4)]
    head, norm, content, place = [cut(sum_ab, at + (4 + j) * rs, rs) for j in range(4)]
    norm = norm + cut(sum_c, rf + 4 * rs, rs)
    return feeds, squares, cut(sum_c, 0, rf), head, [content, place], norm


def prepare(parts_ab, parts_c, loss, devices, low):
    sum_ab, sum_c = [sum(value.astype(F32) for value in some) for some in (parts_ab, parts_c)]
    width = sum_ab.shape[1]
    total = sum(
        jnp.sum(jnp.sum(value * value, axis=0, keepdims=True), axis=1, keepdims=True) for value in (sum_ab, sum_c))
    spot = [lax.broadcasted_iota(jnp.int32, (8, width), axis) for axis in (0, 1)]
    numbers = jnp.zeros((8, width), F32)
    for row, value in enumerate((total, loss)):
        for lane in range(3):
            high = low(value)
            numbers = jnp.where(jnp.logical_and(spot[0] == row, spot[1] == lane), high, numbers)
            value = value - high
    feeds, squares, _, _, _, _ = row_parts(sum_ab, sum_c)
    slot = feeds[0].shape[0] // 4
    rs = squares[0].shape[0]
    none = jnp.zeros((slot - rs, width), F32)
    spare = [jnp.zeros((slot, width), F32)] * (devices - 16 - len(squares))
    slots = [feed[j * slot:(j + 1) * slot] for feed in feeds for j in range(4)]
    slots += [jnp.concatenate([square, none]) for square in squares] + spare
    slots = jnp.stack([jnp.concatenate([one, numbers]) for one in slots])
    return sum_ab, sum_c, slots.astype(BF16)


def prepare_kernel(*refs):
    *parts, loss, sum_ab, sum_c, slots = refs
    sum_ab[...], sum_c[...], slots[...] = prepare(
        [ref[...] for ref in parts[:2]], [ref[...] for ref in parts[2:]], loss[...], slots.shape[0], lambda value: value.astype(BF16).astype(F32))


def adapt(sum_ab, sum_c, sums, square_mom, expand_mom, reduce_mom, *states):
    feeds, squares, win, head, query, norm = row_parts(sum_ab, sum_c)
    lane = lax.broadcasted_iota(jnp.int32, (1, sums.shape[1]), 1)
    total, loss = [jnp.sum(jnp.where(lane < 3, sums[j:j + 1, :], 0.0), axis=1, keepdims=True) for j in range(2)]
    size = jnp.sqrt(total)
    factor = jnp.minimum(1.0, CLIP / (size + 1e-06))
    out = [BETA_M * square_mom + factor * jnp.stack(squares),
           BETA_M * expand_mom + factor * jnp.stack(feeds[:2]),
           BETA_M * reduce_mom + factor * jnp.stack(feeds[2:])]
    query = jnp.stack([one[:, :states[6].shape[2]] for one in query])
    grads = (win, head[:, :states[3].shape[1]], query, norm[:, :states[9].shape[1]])
    for j, (grad, rate, decay) in enumerate(zip(grads, (0.04, 0.1, 0.5, 0.5), (0.0001, 0.0001, 0.0, 0.0))):
        out += adam(*states[3 * j:3 * j + 3], factor * grad, rate, decay)
    return out + [loss, size]


def adapt_kernel(*refs):
    count = 18
    for ref, value in zip(refs[count:], adapt(*[ref[...] for ref in refs[:count]])):
        ref[...] = value


def apply(back, hidden, square, expand, reduce):
    slot = back.shape[1]
    rf = 4 * slot
    rs = square.shape[1]
    feed = back[:16].astype(F32).reshape(4, rf, back.shape[2])
    ortho = back[16:16 + square.shape[0]].astype(F32)[:, :rs]
    return muon(square, ortho, square.shape[2]) + muon(expand, feed[:2], hidden) + muon(reduce, feed[2:], hidden)


def apply_kernel(back, square, expand, reduce, *outs):
    hidden = back.shape[0] * expand.shape[1]
    for ref, value in zip(outs, apply(back[...], hidden, square[...], expand[...], reduce[...])):
        ref[...] = value


def solution(mesh):
    both = ("dp", "fsdp")
    first = [P(both), P(both), P(both), P(both)]
    square, expand, reduce = P(None, both), P(None, None, both), P(None, both)
    rows, query, norm = P(both), P(None, None, both), P(None, both)
    in_specs = tuple(first + [square] * 2 + [expand] * 2 + [reduce] * 2 + [rows] * 6 + [query] * 3 + [norm] * 3)
    out_specs = tuple([square] * 3 + [expand] * 3 + [reduce] * 3 + [rows] * 8 + [query] * 4 + [norm] * 4 + [P()] * 3)
    return jax.shard_map(
        functools.partial(per_device, mesh.size), mesh=mesh, in_specs=in_specs, out_specs=out_specs, check_vma=False)
```

```python
import functools
import math

import jax
import jax.numpy as jnp
import numpy as np
from jax import lax
from jax.experimental import pallas as pl
from jax.experimental.layout import Layout, with_layout_constraint
from jax.experimental.pallas import tpu as pltpu
from jax.sharding import PartitionSpec as P

HEADS = 8
SIDE = 25
STEP = 10
NS_A = 3.4445
NS_B = -4.775
NS_C = 2.0315
CLIP = 0.02
BETA_M = 0.95
LR_M = 0.3
DECAY_M = 0.01
ADAM_B1 = 0.9
ADAM_B2 = 0.999
SOFT = 0.02
SOFT_L1 = 0.05
NO_OBJECT = 0.1
EPS = 1e-05
LOG2E = math.log2(math.e)
F32 = jnp.float32
BF16 = jnp.bfloat16
VMEM_LIMIT = 56 * 1024 * 1024


def cost(micros):
    return pl.CostEstimate(flops=int(micros * 1.1e9), bytes_accessed=int(micros * 3.5e6), transcendentals=0)


def nn(left, right):
    return lax.dot_general(left, right, (((1,), (0,)), ((), ())), preferred_element_type=F32)


def nt(left, right):
    return lax.dot_general(left, right, (((1,), (1,)), ((), ())), preferred_element_type=F32)


def tn(left, right):
    return lax.dot_general(left, right, (((0,), (0,)), ((), ())), preferred_element_type=F32)


BLOCKS = 32
FIRST = (64, 8, 8, 8, 8, 8, 8)
SECOND = (64,) * 4 + (8,) * 14
PIECES = ((0, 1, 4, 5), (8, 9, 12, 13), (2, 3, 10, 11), (6, 7, 14, 15))
PART_A = (64, 64) + (8,) * 6
PART_B = (64, 64) + (8,) * 8
PART_C = (64,) + (8,) * 6


def by_core(value):
    rows = value.shape[0] // BLOCKS
    value = value.reshape(BLOCKS // 2, 2, rows, value.shape[1])
    return value[:, 0], value[:, 1]


def pair_rows(one, two):
    width = one.shape[1]
    both = [part.reshape(BLOCKS, part.shape[0] // BLOCKS, width) for part in (one, two)]
    return jnp.concatenate(both, axis=1).reshape(2 * one.shape[0], width)


def unpair(both):
    both = both.astype(F32)
    half = both.shape[1] // 2
    return [both[:, j * half:(j + 1) * half].reshape(BLOCKS * half, both.shape[2]) for j in range(2)]


def block_rows(me, block, start, count, got_ref, other_ref):
    far = me ^ block
    place = ((far >> 1) & 3) * 4 + (far >> 3)
    cut = slice(start, start + count)
    return jnp.where((far & 1) == 0, got_ref[place, cut, :], other_ref[place, cut, :])


def all_rows(me, start, got_ref, other_ref):
    return jnp.stack([block_rows(me, block, start, 16, got_ref, other_ref) for block in range(BLOCKS)])


def put_blocks(refs, flip, start, value):
    rows = value.shape[0] // BLOCKS
    even, odd = by_core(value)
    refs[0][:, start:start + rows, :] = jnp.where(flip, odd, even).astype(BF16)
    refs[1][:, start:start + rows, :] = jnp.where(flip, even, odd).astype(BF16)


def head_mask(width, head):
    lane = lax.broadcasted_iota(jnp.int32, (1, width), 1)
    depth = width // HEADS
    return jnp.logical_and(lane >= head * depth, lane < (head + 1) * depth).astype(F32).astype(BF16)


def norm_parts(total):
    center = total - jnp.mean(total, axis=-1, keepdims=True)
    spread = jnp.mean(center * center, axis=-1, keepdims=True)
    scale = lax.rsqrt(spread + EPS)
    return center * scale, scale


def norm_back(grad, unit, scale, gain):
    inner = grad * gain
    mean_inner = jnp.mean(inner, axis=-1, keepdims=True)
    mean_cross = jnp.mean(inner * unit, axis=-1, keepdims=True)
    return scale * (inner - mean_inner - unit * mean_cross)


def column_sum(value):
    return jnp.sum(value, axis=0, keepdims=True)


GELU_C = math.sqrt(2.0 / math.pi)
GELU_K = 0.044715 * GELU_C


def gelu_parts(value):
    square = value * value
    half = 0.5 + 0.5 * jnp.tanh(value * (GELU_C + GELU_K * square))
    out = value * half
    slope = half + out * (1.0 - half) * (2.0 * GELU_C + 6.0 * GELU_K * square)
    return out, slope


def masked_softmax(scores, depth, length):
    padded = scores.shape[1]
    start = (padded - 1) // 128 * 128
    if length < padded:
        scores = scores + jnp.where(lax.broadcasted_iota(jnp.int32, (1, padded), 1) < length, 0.0, -1e30)
    factor = LOG2E / math.sqrt(depth)
    top = jnp.max(scores, axis=1, keepdims=True)
    powers = jnp.exp2((scores - top) * factor)
    inverse = 1.0 / jnp.sum(powers, axis=1, keepdims=True)
    return (powers * inverse).astype(BF16)


def encode_kernel(tokens, me_ref, f_ref, got_ref, other_ref, sine_ref,
                  p_ref, keyed_ref, lowm_ref, q_ref, k_ref, v_ref, o_ref, s0_ref, x1_ref, w_ref, norm_ref, win_ref, k_t):
    head = pl.program_id(1)
    width = got_ref.shape[2]

    @pl.when(jnp.logical_and(pl.program_id(0) == 0, head == 0))
    def _():
        rows = FIRST[0]

        sources = (got_ref, other_ref)
        for block in range(BLOCKS):
            win_ref[block * rows:(block + 1) * rows, :] = block_rows(me_ref[0], block, 0, rows, *sources)
        for pair in range(2):
            for j, one in enumerate(unpair(all_rows(me_ref[0], rows + 16 * pair, *sources))):
                w_ref[2 * pair + j] = one.astype(BF16)
        norm_ref[...] = unpair(all_rows(me_ref[0], rows + 32, *sources))[0][:, 0:128].T[0:norm_ref.shape[0], :]

    @pl.when(head == 0)
    def _():
        padded = s0_ref.shape[1]
        s0_ref[0, tokens // 8 * 8:padded, :] = jnp.zeros((padded - tokens // 8 * 8, width), F32)
        s0_ref[0, 0:tokens, :] = nn(f_ref[0], win_ref[...])
        memory = s0_ref[0]
        keyed = (memory + sine_ref[...]).astype(BF16)
        lowm = memory.astype(BF16)
        keyed_ref[0] = keyed
        lowm_ref[0] = lowm
        q_ref[0] = nn(keyed, w_ref[0]).astype(BF16)
        keys = nn(keyed, w_ref[1]).astype(BF16)
        k_ref[0] = keys
        k_t[...] = keys.T
        v_ref[0] = nn(lowm, w_ref[2]).astype(BF16)
        o_ref[...] = jnp.zeros_like(o_ref)

    for at in range(8):
        mask = head_mask(width, head * 8 + at)
        vm = v_ref[0] * mask
        for start in range(0, q_ref.shape[1], 320):
            cut = slice(start, start + 320)
            scores = nn(q_ref[0, cut, :] * mask, k_t[...])
            probs = masked_softmax(scores, width // HEADS, tokens)
            p_ref[0, at, cut, :] = probs
            o_ref[0, cut, :] += nn(probs, vm)

    @pl.when(head == HEADS // 8 - 1)
    def _():
        total = s0_ref[0] + nn(o_ref[0].astype(BF16), w_ref[3])
        s0_ref[0] = total
        unit, scale = norm_parts(total)
        x1_ref[0] = unit * norm_ref[0:1, :] + norm_ref[6:7, :]


def encode(features, me, got, other, sine):
    images, tokens, depth = features.shape
    width = got.shape[2]
    padded = sine.shape[0]
    per_image = lambda kind: jax.ShapeDtypeStruct((images, padded, width), kind)
    image_block = pl.BlockSpec((1, padded, width), lambda i, h: (i, 0, 0))
    whole = lambda shape: pl.BlockSpec(shape, lambda i, h: (0,) * len(shape))
    return pl.pallas_call(
        functools.partial(encode_kernel, tokens),
        grid=(images, HEADS // 8),
        in_specs=[
            pl.BlockSpec(memory_space=pltpu.SMEM), pl.BlockSpec((1, tokens, depth), lambda i, h: (i, 0, 0)),
            whole(got.shape), whole(other.shape), whole(sine.shape),
        ],
        out_specs=[pl.BlockSpec((1, 8, padded, padded), lambda i, h: (i, h, 0, 0))] + [image_block] * 8
        + [whole((4, width, width)), whole((16, width))],
        out_shape=[jax.ShapeDtypeStruct((images, HEADS, padded, padded), BF16)]
        + [per_image(BF16)] * 5 + [per_image(F32)] * 3
        + [jax.ShapeDtypeStruct((4, width, width), BF16), jax.ShapeDtypeStruct((16, width), F32)],
        scratch_shapes=[pltpu.VMEM((depth, width), BF16), pltpu.VMEM((width, padded), BF16)],
        compiler_params=pltpu.CompilerParams(vmem_limit_bytes=VMEM_LIMIT),
        cost_estimate=cost(22),
        name="encode",
    )(me, features, got, other, sine)


def encode_back_kernel(tokens, images, first, last, *refs):
    (me_ref, dx1_ref, s0_ref, norm_ref, p_ref, keyed_ref, lowm_ref, q_ref, k_ref, v_ref, o_ref, w_ref), refs = (
        refs[:12], refs[12:])
    if not first:
        (dsq_in, dnorm_in), refs = refs[:2], refs[2:]
    if last:
        f_refs, refs = refs[:images], refs[images:]
        dm_refs, refs = refs[:images - 1], refs[images - 1:]
        outs, refs = refs[:2], refs[2:]
        *refs, dsq, dnorm_ref = refs
    else:
        (dsq, dnorm_ref, dm_ref), refs = refs[:3], refs[3:]
    ds0, dout, dout_t, q_t, v_t, cross, dq, dk_t, dv_t = refs
    head = pl.program_id(0)
    width = w_ref.shape[1]
    depth = width // HEADS

    @pl.when(head == 0)
    def _():
        dsq[...] = jnp.zeros_like(dsq) if first else dsq_in[...]
        dnorm_ref[...] = jnp.zeros_like(dnorm_ref) if first else dnorm_in[...]

    @pl.when(head == 0)
    def _():
        unit, scale = norm_parts(s0_ref[0])
        grad = dx1_ref[0]
        dnorm_ref[0:1, :] += column_sum(grad * unit)
        dnorm_ref[6:7, :] += column_sum(grad)
        dtotal = norm_back(grad, unit, scale, norm_ref[0:1, :])
        ds0[...] = dtotal
        low = dtotal.astype(BF16)
        dsq[3] += tn(o_ref[0].astype(BF16), low)
        dmixed = nt(low, w_ref[3]).astype(BF16)
        dout[...] = dmixed
        dout_t[...] = dmixed.T
        q_t[...] = q_ref[0].T
        v_t[...] = v_ref[0].T
        cross[...] = dmixed.astype(F32) * o_ref[0]
        dq[...] = jnp.zeros_like(dq)

    for at in range(4):
        one = head * 4 + at
        mask = head_mask(width, one)
        rows = pl.ds(pl.multiple_of(one * depth, depth), depth)
        weight = jnp.sum(cross[...] * mask.astype(F32), axis=1, keepdims=True)
        probs = p_ref[0, at]
        dprobs = nn(dout[...] * mask, v_t[...])
        dscores = (probs.astype(F32) * (dprobs - weight)).astype(BF16)
        dq[...] += nn(dscores, k_ref[0] * mask)
        dk_t[rows, :] = nn(q_t[rows, :], dscores)
        dv_t[rows, :] = nn(dout_t[rows, :], probs)

    @pl.when(head == HEADS // 4 - 1)
    def _():
        factor = 1.0 / math.sqrt(depth)
        dqb = (dq[...] * factor).astype(BF16)
        dkb = (dk_t[...] * factor).astype(BF16).T
        dvb = dv_t[...].astype(BF16).T
        dsq[0] += tn(keyed_ref[0], dqb)
        dsq[1] += tn(keyed_ref[0], dkb)
        dsq[2] += tn(lowm_ref[0], dvb)
        dm = ds0[...] + nt(dqb, w_ref[0]) + nt(dkb, w_ref[1]) + nt(dvb, w_ref[2])
        dmb = dm.astype(BF16)
        if not last:
            dm_ref[0] = dmb
        else:
            parts = [ref[0] for ref in dm_refs] + [dmb]
            dwin = sum(tn(part[0:tokens], ref[0]) for part, ref in zip(parts, f_refs))
            flip = (me_ref[0] & 1) > 0
            rows = PART_C[0]
            put_blocks(outs, flip, 0, dwin.astype(BF16).T)
            for pair in range(2):
                put_blocks(outs, flip, rows + 16 * pair, pair_rows(dsq[2 * pair], dsq[2 * pair + 1]))
            put_blocks(outs, flip, rows + 32, pair_rows(norm_columns(dnorm_ref[...], width), jnp.zeros((width, width), F32)))


def norm_columns(dnorm, width):
    wide = jnp.concatenate([dnorm, jnp.zeros((128 - dnorm.shape[0], width), F32)], axis=0).T
    return jnp.concatenate([wide, jnp.zeros((width, width - 128), F32)], axis=1)


def encode_back(image, images, me, dx1, s0, norm, probs, keyed, lowm, q, k, v, o, square, features, *before):
    _, tokens, channels = features.shape
    padded, width = s0.shape[1:]
    first, last = image == 0, image == images - 1
    image_block = pl.BlockSpec((1, padded, width), lambda h: (image, 0, 0))
    whole = lambda shape: pl.BlockSpec(shape, lambda h: (0,) * len(shape))
    sums = [((4, width, width), F32), (norm.shape, F32)]
    part = ((BLOCKS // 2, sum(PART_C), width), BF16)
    outs = [part, part] if last else sums + [((1, padded, width), BF16)]
    scratch = [((padded, width), F32), ((padded, width), BF16), ((width, padded), BF16), ((width, padded), BF16), ((width, padded), BF16),
               ((padded, width), F32), ((padded, width), F32), ((width, padded), F32), ((width, padded), F32)]
    extra, extra_specs = list(before[:2]), [] if first else [whole(shape) for shape, _ in sums]
    if last:
        extra += [features] * images + list(before[2:])
        extra_specs += [pl.BlockSpec((1, tokens, channels), lambda h, j=j: (j, 0, 0)) for j in range(images)]
        extra_specs += [whole((1, padded, width))] * (images - 1)
    return pl.pallas_call(
        functools.partial(encode_back_kernel, tokens, images, first, last),
        grid=(HEADS // 4,),
        in_specs=[
            pl.BlockSpec(memory_space=pltpu.SMEM), image_block, image_block, whole(norm.shape),
            pl.BlockSpec((1, 4, padded, padded), lambda h: (image, h, 0, 0)),
        ] + [image_block] * 6 + [whole(square.shape)] + extra_specs,
        out_specs=[whole(shape) for shape, _ in outs],
        out_shape=[jax.ShapeDtypeStruct(shape, kind) for shape, kind in outs],
        scratch_shapes=[pltpu.VMEM(shape, kind) for shape, kind in scratch + (sums if last else [])],
        compiler_params=pltpu.CompilerParams(vmem_limit_bytes=VMEM_LIMIT),
        cost_estimate=cost(17 if last else 12),
        name="encode_back",
    )(me, dx1, s0, norm, probs, keyed, lowm, q, k, v, o, square, *extra)


def stack_heads(value):
    return jnp.concatenate([value * head_mask(value.shape[1], head) for head in range(HEADS)], axis=0)


def pick_heads(stacked):
    rows, width = stacked.shape[0] // HEADS, stacked.shape[1]
    lane = lax.broadcasted_iota(jnp.int32, (1, width), 1)
    out = stacked[0:rows]
    for head in range(1, HEADS):
        out = jnp.where(lane >= head * (width // HEADS), stacked[head * rows:(head + 1) * rows], out)
    return out


def soft_gap(gap):
    return SOFT * jnp.log(1.0 + jnp.exp(-jnp.abs(gap) * (1.0 / SOFT)))


def sigmoid(value):
    return 1.0 / (1.0 + jnp.exp(-value))


def axis_terms(center, size, target_center, target_size):
    low_one, high_one = center - size / 2, center + size / 2
    low_two, high_two = target_center - target_size / 2, target_center + target_size / 2
    low_gap, high_gap = low_one - low_two, high_one - high_two
    low_soft, high_soft = soft_gap(low_gap), soft_gap(high_gap)
    inner = (jnp.minimum(high_one, high_two) - high_soft) - (jnp.maximum(low_one, low_two) + low_soft)
    overlap = jnp.maximum(inner, 0.0) + soft_gap(inner)
    hull = (jnp.maximum(high_one, high_two) + high_soft) - (jnp.minimum(low_one, low_two) - low_soft)
    return overlap, hull, sigmoid(inner / SOFT), sigmoid(low_gap / SOFT), sigmoid(high_gap / SOFT)


def box_loss(box, target, mask, box_count):
    l1_sum = 0.0
    grads = []
    for one, two in zip(box, target):
        offset = (one - two) / SOFT_L1
        root = jnp.sqrt(offset * offset + 1.0)
        l1_sum = l1_sum + mask * (SOFT_L1 * (root - 1.0))
        grads.append(5.0 * offset / root)
    ow, hw, pw, lw, uw = axis_terms(box[0], box[2], target[0], target[2])
    oh, hh, ph, lh, uh = axis_terms(box[1], box[3], target[1], target[3])
    inter = ow * oh
    union = box[2] * box[3] + target[2] * target[3] - inter
    hull = hw * hh
    by_union, by_hull = 1.0 / union, 1.0 / hull
    giou = inter * by_union - (hull - union) * by_hull
    share = inter * by_union * by_union
    g_inter = by_union + share - by_hull
    g_area = by_hull - share
    g_hull = -union * by_hull * by_hull
    for axis, (other, hull_other, slope, low_s, high_s, size_other) in enumerate(
        ((oh, hh, pw, lw, uw, box[3]), (ow, hw, ph, lh, uh, box[2]))
    ):
        flow = g_inter * other * slope
        wide = g_hull * hull_other
        g_high = flow * (1.0 - high_s) + wide * high_s
        g_low = -flow * low_s - wide * (1.0 - low_s)
        grads[axis] = grads[axis] - 2.0 * (g_low + g_high)
        grads[axis + 2] = grads[axis + 2] - 2.0 * ((g_high - g_low) / 2 + g_area * size_other)
    value = jnp.sum((5.0 * l1_sum + 2.0 * mask * (1.0 - giou)) / box_count, axis=1, keepdims=True)
    return value, [grad * mask / box_count for grad in grads]


def middle_kernel(tokens, queries, classes, inverse, count_rows, me_ref, x1_ref, sine_ref, norm_ref,
                  col_ref, row_ref, got0, got1, got2, got3, other0, other1, other2, other3,
                  dx1_ref, keepa_ref, senda_ref, keepb_ref, sendb_ref, loss_ref, box_ref, feed_ref, rest_ref, dsq_ref, dnorm_ref, w_ref, head_ref, g0, total1, tall_g, tall_s, small_g, small_s, kin, vin, kk, vv, probs2, mixed2, dsum, dq2, dmix2):
    images, padded, width = x1_ref.shape
    depth = width // HEADS
    rows_feed = FIRST[0]
    chunks = BLOCKS * rows_feed // width
    per_chunk = BLOCKS // chunks
    many = images * padded
    qrows = round_up(queries, 128)
    factor = 1.0 / math.sqrt(depth)
    gain = lambda row: norm_ref[row:row + 1, :]
    dnorm_ref[...] = jnp.zeros_like(dnorm_ref)

    me = me_ref[0]
    for core, sources in enumerate(((got0, got1, got2, got3), (other0, other1, other2, other3))):
        for source, spots in zip(sources, PIECES):
            for entry, spot in enumerate(spots):
                block = me ^ ((spot % 4) * 8 + (spot // 4) * 2 + core)
                place = pl.ds(pl.multiple_of(block * rows_feed, rows_feed), rows_feed)
                for which in range(4):
                    feed_ref[which, place, :] = source[entry, which * rows_feed:(which + 1) * rows_feed, :]
                rest_ref[block] = source[entry, 4 * rows_feed:, :]
    for pair in range(5):
        for j, one in enumerate(unpair(rest_ref[:, 16 * pair:16 * pair + 16, :])):
            w_ref[2 * pair + j] = one.astype(BF16)
    head_one, found = unpair(rest_ref[:, 80:96, :])
    head_ref[...] = head_one[:, 0:head_ref.shape[1]].astype(BF16)
    box_count = jnp.sum(found[:, 0:1], axis=0, keepdims=True) * (1.0 / count_rows)
    box_ref[...] = box_count
    content, place = [one[:, 0:qrows].T for one in unpair(rest_ref[:, 96:112, :])]

    def weights(which, layer, chunk):
        return feed_ref[2 * which + layer, pl.ds(pl.multiple_of(chunk * width, width), width), :]

    flip = (me & 1) > 0
    out_a, out_b = (keepa_ref, senda_ref), (keepb_ref, sendb_ref)

    def put_feed(which, layer, chunk, value):
        value = value.reshape(per_chunk // 2, 2, rows_feed, width)
        place = pl.ds(chunk * (per_chunk // 2), per_chunk // 2), slice(layer * rows_feed, (layer + 1) * rows_feed)
        keep, send = out_b if which else out_a
        keep[place] = jnp.where(flip, value[:, 1], value[:, 0])
        send[place] = jnp.where(flip, value[:, 0], value[:, 1])

    def feed(layer, source, g_ref, s_ref, out_ref):
        def step(chunk, carry):
            value, slope = gelu_parts(nt(source, weights(0, layer, chunk)))
            value = value.astype(BF16)
            g_ref[chunk] = value
            s_ref[chunk] = slope.astype(BF16)
            out_ref[...] += nn(value, weights(1, layer, chunk))
            return carry
        lax.fori_loop(0, chunks, step, 0, unroll=True)

    def feed_back(layer, source_t, grad, grad_t, g_ref, s_ref, out_ref):
        def step(chunk, carry):
            dg = nt(grad, weights(1, layer, chunk)).astype(BF16)
            du = (dg.astype(F32) * s_ref[chunk].astype(F32)).astype(BF16)
            put_feed(1, layer, chunk, nn(grad_t, g_ref[chunk]).astype(BF16).T)
            put_feed(0, layer, chunk, nn(source_t, du).astype(BF16).T)
            out_ref[...] += nn(du, weights(0, layer, chunk))
            return carry
        lax.fori_loop(0, chunks, step, 0, unroll=True)

    x1 = x1_ref[...].reshape(many, width)
    total1[...] = x1
    feed(0, x1.astype(BF16), tall_g, tall_s, total1)
    unit1, scale1 = norm_parts(total1[...])
    x2 = unit1 * gain(1) + gain(7)
    for image in range(images):
        part = x2[image * padded:(image + 1) * padded]
        keyed = (part + sine_ref[...]).astype(BF16)
        lowm = part.astype(BF16)
        kin[image] = keyed
        vin[image] = lowm
        kk[image] = nn(keyed, w_ref[5]).astype(BF16)
        vv[image] = nn(lowm, w_ref[6]).astype(BF16)

    asked = (content + place).astype(BF16)
    lowc = content.astype(BF16)
    q1 = nn(asked, w_ref[0]).astype(BF16)
    k1 = nn(asked, w_ref[1]).astype(BF16)
    v1 = nn(lowc, w_ref[2]).astype(BF16)
    q1s = stack_heads(q1)
    p1 = masked_softmax(nt(q1s, k1), depth, queries)
    mix1 = pick_heads(nn(p1, v1))
    mix1b = mix1.astype(BF16)
    unit2, scale2 = norm_parts(content + nn(mix1b, w_ref[3]))
    t1 = unit2 * gain(2) + gain(8)

    asked2 = (t1 + place).astype(BF16)
    q2 = nn(asked2, w_ref[4]).astype(BF16)
    q2s = stack_heads(q2)

    def cross(image, carry):
        probs = masked_softmax(nt(q2s, kk[image]), depth, tokens)
        probs2[image] = probs
        mixed2[image] = pick_heads(nn(probs, vv[image]))
        return carry
    lax.fori_loop(0, images, cross, 0, unroll=True)
    rows = images * qrows
    mix2 = mixed2[...].reshape(rows, width)
    mix2b = mix2.astype(BF16)
    t1s = jnp.concatenate([t1] * images, axis=0)
    unit3, scale3 = norm_parts(t1s + nn(mix2b, w_ref[7]))
    t2 = unit3 * gain(3) + gain(9)

    t2b = t2.astype(BF16)
    g0[...] = t2
    feed(1, t2b, small_g, small_s, g0)
    unit4, scale4 = norm_parts(g0[...])
    t3 = unit4 * gain(4) + gain(10)
    unit5, scale5 = norm_parts(t3)
    out = (unit5 * gain(5) + gain(11)).astype(BF16)

    logits = nn(out, head_ref[...])
    lane = lax.broadcasted_iota(jnp.int32, logits.shape, 1)
    weight = col_ref[:, 0:1]
    label = col_ref[:, 1:2].astype(jnp.int32)
    kept = jnp.where(lane < classes, logits, -1e30)
    top = jnp.max(kept, axis=1, keepdims=True)
    powers = jnp.exp(kept - top)
    norm_sum = jnp.sum(powers, axis=1, keepdims=True)
    chosen = lane == label
    ce = top + jnp.log(norm_sum) - jnp.sum(jnp.where(chosen, logits, 0.0), axis=1, keepdims=True)
    ce_sum = jnp.sum(weight * ce, axis=0, keepdims=True)
    dlogits = ((weight * inverse) * (powers / norm_sum - jnp.where(chosen, 1.0, 0.0))).astype(BF16)

    b1, slope_one = gelu_parts(nn(out, w_ref[8]))
    b1 = b1.astype(BF16)
    b2, slope_two = gelu_parts(nn(b1, w_ref[9]))
    b2 = b2.astype(BF16)
    raw = nn(b2, head_ref[...]).T
    box = [sigmoid(raw[classes + j:classes + j + 1, :]) for j in range(4)]
    target = [row_ref[1 + j:2 + j, :] for j in range(4)]
    box_value, dbox = box_loss(box, target, row_ref[0:1, :], box_count)
    loss_ref[...] = ce_sum * inverse + box_value
    draw = jnp.concatenate([grad * one * (1.0 - one) for grad, one in zip(dbox, box)], axis=0)
    lanes_in = head_ref.shape[1]
    spot = lax.broadcasted_iota(jnp.int32, (lanes_in, rows), 0)
    spread = jnp.zeros((lanes_in, rows), F32)
    for j in range(4):
        spread = jnp.where(spot == classes + j, draw[j:j + 1, :], spread)
    draw_rows = spread.T.astype(BF16)

    dhead = tn(out, dlogits) + tn(b2, draw_rows)
    du2 = (nt(draw_rows, head_ref[...]) * slope_two).astype(BF16)
    dsq_ref[9] = tn(b1, du2)
    du1 = (nt(du2, w_ref[9]) * slope_one).astype(BF16)
    dsq_ref[8] = tn(out, du1)
    dout = nt(dlogits, head_ref[...]) + nt(du1, w_ref[8])

    def through(grad, unit, scale, row):
        dnorm_ref[row:row + 1, :] = column_sum(grad * unit)
        dnorm_ref[row + 6:row + 7, :] = column_sum(grad)
        return norm_back(grad, unit, scale, gain(row))

    dt3 = through(dout, unit5, scale5, 5)
    ds3 = through(dt3, unit4, scale4, 4)
    g0[...] = ds3
    ds3b = ds3.astype(BF16)
    feed_back(1, t2b.T, ds3b, ds3b.T, small_g, small_s, g0)
    ds2 = through(g0[...], unit3, scale3, 3)
    ds2b = ds2.astype(BF16)
    dsq_ref[7] = tn(mix2b, ds2b)
    dmix2[...] = nt(ds2b, w_ref[7]).astype(BF16).reshape(images, qrows, width)
    dq2[...] = jnp.zeros_like(dq2)
    dsum[...] = jnp.zeros_like(dsum)

    def attention_back(dmix, mix, probs, stacked_q, keys, values):
        dms = stack_heads(dmix)
        both = dmix.astype(F32) * mix
        weight = jnp.concatenate(
            [jnp.sum(both * head_mask(width, head).astype(F32), axis=1, keepdims=True) for head in range(HEADS)],
            axis=0,
        )
        dscores = (probs.astype(F32) * (nt(dms, values) - weight)).astype(BF16)
        dq = pick_heads(nn(dscores, keys)) * factor
        dk = (tn(stacked_q, dscores) * factor).astype(BF16).T
        dv = tn(dms, probs).astype(BF16).T
        return dq, dk, dv

    def cross_back(image, carry):
        dq, dk, dv = attention_back(dmix2[image], mixed2[image], probs2[image], q2s, kk[image], vv[image])
        dq2[...] += dq
        dsum[0] += tn(kin[image], dk)
        dsum[1] += tn(vin[image], dv)
        dx1_ref[image] = nt(dk, w_ref[5]) + nt(dv, w_ref[6])
        return carry
    lax.fori_loop(0, images, cross_back, 0, unroll=True)
    dsq_ref[5] = dsum[0]
    dsq_ref[6] = dsum[1]
    dq2b = dq2[...].astype(BF16)
    dsq_ref[4] = tn(asked2, dq2b)
    dasked2 = nt(dq2b, w_ref[4])
    dt1 = dasked2
    for image in range(images):
        dt1 = dt1 + ds2[image * qrows:(image + 1) * qrows]
    ds1 = through(dt1, unit2, scale2, 2)
    ds1b = ds1.astype(BF16)
    dsq_ref[3] = tn(mix1b, ds1b)
    dmix1 = nt(ds1b, w_ref[3]).astype(BF16)
    dq, dk, dv = attention_back(dmix1, mix1, p1, q1s, k1, v1)
    dqb = dq.astype(BF16)
    dsq_ref[0] = tn(asked, dqb)
    dsq_ref[1] = tn(asked, dk)
    dsq_ref[2] = tn(lowc, dv)
    dasked = nt(dqb, w_ref[0]) + nt(dk, w_ref[1])
    dquery = [ds1 + dasked + nt(dv, w_ref[2]), dasked + dasked2]

    unit, scale = norm_parts(total1[...])
    dx2 = dx1_ref[...].reshape(many, width)
    ds = through(dx2, unit, scale, 1)
    total1[...] = ds
    dsb = ds.astype(BF16)
    x1b = x1_ref[...].reshape(many, width).astype(BF16)
    feed_back(0, x1b.T, dsb, dsb.T, tall_g, tall_s, total1)
    dx1_ref[...] = total1[...].reshape(images, padded, width)

    wide = lambda value: jnp.concatenate([value, jnp.zeros((value.shape[0], width - value.shape[1]), F32)], axis=1)
    at = 2 * rows_feed
    for pair in range(3):
        put_blocks(out_a, flip, at + 16 * pair, pair_rows(dsq_ref[2 * pair], dsq_ref[2 * pair + 1]))
    for pair in range(2):
        put_blocks(out_b, flip, at + 16 * pair, pair_rows(dsq_ref[6 + 2 * pair], dsq_ref[7 + 2 * pair]))
    put_blocks(out_b, flip, at + 32, pair_rows(wide(dhead), norm_columns(dnorm_ref[...], width)))
    put_blocks(out_b, flip, at + 48, pair_rows(wide(dquery[0].T), wide(dquery[1].T)))


def middle(me, x1, sine, norm, col, row, pieces, tokens, queries, classes, inverse, count_rows):
    images, padded, width = x1.shape
    qrows = round_up(queries, 128)
    chunks = BLOCKS * FIRST[0] // width
    many, rows = images * padded, images * qrows
    vmem = pl.BlockSpec(memory_space=pltpu.VMEM)
    shapes = [
        ((images, padded, width), F32), ((BLOCKS // 2, sum(PART_A), width), BF16),
        ((BLOCKS // 2, sum(PART_A), width), BF16), ((BLOCKS // 2, sum(PART_B), width), BF16),
        ((BLOCKS // 2, sum(PART_B), width), BF16), ((1, 1), F32), ((1, 1), F32),
    ]
    return pl.pallas_call(
        functools.partial(middle_kernel, tokens, queries, classes, inverse, count_rows),
        in_specs=[pl.BlockSpec(memory_space=pltpu.SMEM)] + [vmem] * (5 + len(pieces)),
        out_specs=[vmem] * len(shapes),
        out_shape=[jax.ShapeDtypeStruct(shape, kind) for shape, kind in shapes],
        scratch_shapes=[
            pltpu.VMEM((4, chunks * width, width), BF16), pltpu.VMEM((BLOCKS, sum(SECOND) - 4 * FIRST[0], width), BF16),
            pltpu.VMEM((10, width, width), F32), pltpu.VMEM((16, width), F32),
            pltpu.VMEM((10, width, width), BF16), pltpu.VMEM((width, 128), BF16),
            pltpu.VMEM((rows, width), F32), pltpu.VMEM((many, width), F32),
            pltpu.VMEM((chunks, many, width), BF16), pltpu.VMEM((chunks, many, width), BF16),
            pltpu.VMEM((chunks, rows, width), BF16), pltpu.VMEM((chunks, rows, width), BF16),
            pltpu.VMEM((images, padded, width), BF16), pltpu.VMEM((images, padded, width), BF16),
            pltpu.VMEM((images, padded, width), BF16), pltpu.VMEM((images, padded, width), BF16),
            pltpu.VMEM((images, HEADS * qrows, padded), BF16), pltpu.VMEM((images, qrows, width), F32),
            pltpu.VMEM((2, width, width), F32), pltpu.VMEM((qrows, width), F32),
            pltpu.VMEM((images, qrows, width), BF16),
        ],
        compiler_params=pltpu.CompilerParams(vmem_limit_bytes=VMEM_LIMIT),
        cost_estimate=cost(35),
        name="middle",
    )(me, x1, sine, norm, col, row, *pieces)


def sine_table(width, padded):
    cells = np.arange(SIDE * SIDE)
    half = width // 2
    index = np.arange(half)
    freqs = 10000.0 ** ((2 * (index // 2)) / half)
    parts = []
    for coord in (cells // SIDE + 1, cells % SIDE + 1):
        angle = (coord / (SIDE + 1e-06) * (2.0 * math.pi))[:, None] / freqs[None, :]
        parts.append(np.where(index[None, :] % 2 == 0, np.sin(angle), np.cos(angle)))
    table = np.concatenate(parts, axis=1).astype(np.float32)
    return np.concatenate([table, np.zeros((padded - table.shape[0], width), np.float32)], axis=0)


def round_up(value, unit):
    return -(-value // unit) * unit


def target_info(matches, labels, boxes, classes, qrows):
    images, queries = matches.shape
    pad = ((0, 0), (0, qrows - queries))
    matched = matches >= 0
    picker = matches[:, :, None] == jnp.arange(labels.shape[1])[None, None, :]
    label = jnp.where(matched, jnp.sum(jnp.where(picker, labels[:, None, :], 0), axis=2), classes - 1)
    weight = jnp.pad(jnp.where(matched, 1.0, NO_OBJECT), pad)
    label = jnp.pad(label, pad).astype(F32)
    col = jnp.stack([weight.reshape(-1), label.reshape(-1)], axis=1)
    mask = jnp.pad(matched.astype(F32), pad).reshape(1, -1)
    wanted = []
    for j in range(4):
        one = jnp.sum(jnp.where(picker, boxes[:, None, :, j], 0.0), axis=2)
        wanted.append(jnp.pad(jnp.where(matched, one, 0.5), pad, constant_values=0.5).reshape(1, -1))
    row = jnp.concatenate([mask] + wanted + [jnp.zeros((3, mask.shape[1]), F32)], axis=0)
    return col, row


AXES = ("dp", "fsdp")


def swap(value, bit, devices):
    return lax.ppermute(value, AXES, [(i, i ^ bit) for i in range(devices)])


def bits_of(devices):
    return [1 << j for j in range(devices.bit_length() - 1)]


def groups_of(devices):
    bits = bits_of(devices)
    return [(bits[j], bits[j + 1]) for j in range(len(bits) - 2, 0, -2)]


def place_of(far, devices):
    place = 0
    for low, _ in reversed(groups_of(devices)):
        place = place * 4 + (far // low) % 4
    return place


def gather_four(held, pair, devices):
    low, high = pair
    return [held] + [swap(held, bits, devices) for bits in (low, high, low | high)]


def gather_round(held, pair, devices):
    return jnp.concatenate(gather_four(held, pair, devices))


def natural_order(got, other, me, pieces):
    devices = 2 * got.shape[0]
    both = jnp.concatenate([got, other])
    table = jnp.asarray([(j & 1) * (devices // 2) + place_of(j, devices) for j in range(devices)])
    blocks = join(both[table[jnp.arange(devices) ^ me]], pieces)
    chips = sorted(range(0, BLOCKS, 2), key=lambda block: place_of(block, BLOCKS))
    return [jnp.stack([blocks[block + core] for block in chips]) for core in range(2)]


def join(got, pieces):
    ratio = got.shape[0] // BLOCKS
    if ratio == 1:
        return got
    got = got.reshape(BLOCKS, ratio, got.shape[1], got.shape[2])
    out, at = [], 0
    for piece in pieces:
        rows = piece // ratio
        out.append(got[:, :, at:at + rows].reshape(BLOCKS, piece, got.shape[3]))
        at += rows
    return jnp.concatenate(out, axis=1)


def launch(keep, send, pieces, devices):
    bits = bits_of(devices)
    ratio = devices // BLOCKS
    tail = keep.shape[1:]
    if ratio == 1:
        shape = (2,) * (len(bits) - 1) + tail
        return swap(send, bits[0], devices).reshape(shape), keep.reshape(shape), list(reversed(bits[1:]))
    value = jnp.stack([keep, send], axis=1).reshape((BLOCKS,) + tail)
    out, at = [], 0
    for piece in pieces:
        out.append(value[:, at:at + piece].reshape(devices, piece // ratio, tail[1]))
        at += piece
    out = jnp.concatenate(out, axis=1)
    out = out.reshape((2,) * len(bits) + out.shape[1:])
    left = list(reversed(bits))
    return advance((jnp.zeros_like(out), out, left), bits[0], devices)


def halves(flight, bit):
    came, kept, left = flight
    axis = left.index(bit)
    mine = (lax.axis_index(AXES) // bit) % 2
    pick = lambda value, at: lax.dynamic_index_in_dim(value, at, axis, keepdims=False).astype(F32)
    out = (pick(kept, 1 - mine) + pick(came, 1 - mine)).astype(BF16)
    return out, pick(kept, mine) + pick(came, mine), [one for one in left if one != bit]


def advance(flight, bit, devices):
    out, kept, left = halves(flight, bit)
    return swap(out, bit, devices), kept, left


def parts_of_four(flight, low, high, devices):
    *addends, left = flight
    axes = [left.index(bit) for bit in (low, high)]
    mine = [(lax.axis_index(AXES) // bit) % 2 for bit in (low, high)]
    out = []
    for bits in (low, high, low | high, 0):
        total = 0.0
        for value in addends:
            for axis, bit, at in sorted(zip(axes, (low, high), mine), key=lambda one: -one[0]):
                at = 1 - at if bits & bit else at
                value = lax.dynamic_index_in_dim(value, at, axis, keepdims=False)
            total = total + value.astype(F32)
        out.append(total.astype(BF16) if bits else total)
    return out


def send_four(parts, flight, low, high, devices):
    came = [swap(one, bits, devices) for one, bits in zip(parts, (low, high, low | high))]
    return (parts[3], *came, [bit for bit in flight[-1] if bit not in (low, high)])


def exact(left, right, dims=((1,), (0,))):
    return lax.dot_general(left, right, (dims, ((), ())), precision=lax.Precision.HIGHEST, preferred_element_type=F32)


def gram_kernel(mom_ref, grad_ref, x_ref, gram_ref, sums_ref):
    slot = mom_ref.shape[1]
    devices, _, width = grad_ref.shape
    sums = jnp.sum(grad_ref[:, slot:, :].astype(F32), axis=0)
    sums_ref[...] = sums
    squares = jnp.sum(sums[0:1, 0:3], axis=1, keepdims=True)
    factor = jnp.minimum(1.0, CLIP / (jnp.sqrt(squares) + 1e-06))
    x = BETA_M * mom_ref[...].astype(F32) + factor * grad_ref[:, :slot, :].astype(F32)
    x = x.reshape(devices * slot, width)
    x_ref[...] = x
    gram = exact(x, x, ((0,), (0,)))
    half = width // 2
    for at, (top, left) in enumerate(((0, 0), (0, half), (half, half))):
        gram_ref[at * half:(at + 1) * half, :] = gram[top:top + half, left:left + half]


def rough(left, right):
    left_high, right_high = left.astype(BF16), right.astype(BF16)
    left_low = (left - left_high.astype(F32)).astype(BF16)
    right_low = (right - right_high.astype(F32)).astype(BF16)
    return nn(left_high, right_high) + (nn(left_high, right_low) + nn(left_low, right_high))


def polish_kernel(x_ref, gram_ref, one_ref, two_ref, three_ref, out_ref):
    packed = (gram_ref[...] + one_ref[...]) + (two_ref[...] + three_ref[...])
    half = packed.shape[1]
    first, cross, last = [packed[at * half:(at + 1) * half] for at in range(3)]
    gram = jnp.concatenate([
        jnp.concatenate([first, cross], axis=1), jnp.concatenate([cross.T, last], axis=1)], axis=0)
    diagonal = lax.broadcasted_iota(jnp.int32, gram.shape, 0) == lax.broadcasted_iota(jnp.int32, gram.shape, 1)
    eye = jnp.where(diagonal, 1.0, 0.0)
    square = jnp.sum(jnp.sum(gram * eye, axis=1, keepdims=True), axis=0, keepdims=True)
    scale = 1.0 / (jnp.sqrt(square) + 1e-07)
    gram = gram * (scale * scale)
    total = None
    for sweep in range(5):
        product = exact if sweep < 2 else rough
        poly = NS_A * eye + NS_B * gram + NS_C * product(gram, gram)
        total = poly if sweep == 0 else rough(total, poly)
        if sweep < 4:
            gram = product(product(poly, gram), poly)
    out = rough(x_ref[...] * scale, total)
    out_ref[...] = out.reshape(out_ref.shape).astype(out_ref.dtype)


def plain_call(body, shapes, *args, near=()):
    vmem = pl.BlockSpec(memory_space=pltpu.VMEM)
    args = [pltpu.with_memory_space_constraint(arg, pltpu.VMEM) if at in near else arg for at, arg in enumerate(args)]
    return pl.pallas_call(
        body,
        in_specs=[vmem] * len(args),
        out_specs=[vmem] * len(shapes),
        out_shape=[
            pltpu.VMEM(shape, kind) if stays else jax.ShapeDtypeStruct(shape, kind)
            for shape, kind, *stays in shapes],
        compiler_params=pltpu.CompilerParams(vmem_limit_bytes=VMEM_LIMIT),
        cost_estimate=cost(2),
        name=body.__name__,
    )(*args)


def to_slots(square, feeds, devices):
    count, rows, width = square.shape
    slot = feeds.shape[1] // 4
    feed_slots = feeds.reshape(feeds.shape[0] * 4, slot, width)
    square_slots = jnp.pad(square, ((0, devices - count - feed_slots.shape[0]), (0, slot - rows), (0, 0)))
    return jnp.concatenate([feed_slots, square_slots], axis=0)


def exchange(slots):
    return lax.all_to_all(slots, AXES, split_axis=0, concat_axis=0, tiled=True)


def adam(weight, first, second, gradient, rate, decay):
    first = ADAM_B1 * first + (1.0 - ADAM_B1) * gradient
    second = ADAM_B2 * second + (1.0 - ADAM_B2) * gradient * gradient
    fixed_first = first / (1.0 - ADAM_B1**STEP)
    fixed_second = second / (1.0 - ADAM_B2**STEP)
    weight = weight * (1.0 - rate * decay) - rate * fixed_first / (jnp.sqrt(fixed_second) + 1e-08)
    return weight, first, second, weight.astype(BF16)


def muon(weight, ortho, longest):
    fresh = weight * (1.0 - LR_M * DECAY_M) - LR_M * 0.2 * math.sqrt(longest) * ortho
    return fresh, fresh.astype(BF16)


def pack_kernel(win_ref, sq_ref, ex_ref, re_ref, head_ref, query_ref, norm_ref, matches_ref, one_ref, two_ref):
    one, two = pack(win_ref[...], sq_ref[...], ex_ref[...], re_ref[...], head_ref[...], query_ref[...], norm_ref[...],
                    matches_ref[...])
    one_ref[...] = one
    two_ref[...] = two


def pack(win, sq, ex, re, head, query, norm, matches):
    width = win.shape[1]
    rows = sq.shape[1]
    wide = lambda value: jnp.concatenate([value, jnp.zeros((value.shape[0], width - value.shape[1]), F32)], axis=1)
    flat = lambda value: [value[j] for j in range(value.shape[0])]
    found = jnp.where(matches >= 0, 1.0, 0.0)
    found = jnp.sum(jnp.sum(found, axis=1, keepdims=True), axis=0, keepdims=True)
    one = [win] + flat(sq[:4]) + [wide(norm), jnp.zeros((rows, width), F32)]
    two = flat(ex) + flat(re) + flat(sq[4:]) + [wide(head), jnp.broadcast_to(found, (rows, width))]
    two = two + [wide(query[0]), wide(query[1])]
    return jnp.concatenate(one).astype(BF16), jnp.concatenate(two).astype(BF16)


def per_device(devices, features, matches, target_labels, target_boxes,
               square_weight, square_momentum, expand_weight, expand_momentum, reduce_weight, reduce_momentum,
               input_weight, input_momentum, input_second, head_weight, head_momentum, head_second,
               query_weight, query_momentum, query_second, norm_weight, norm_momentum, norm_second):
    images, tokens, channels = features.shape
    count, rs, width = square_weight.shape
    pairs, _, rf = expand_weight.shape
    ri = input_weight.shape[0]
    rh, head_lanes = head_weight.shape
    _, queries, rq = query_weight.shape
    norms, rn = norm_weight.shape
    classes = head_lanes - 4
    padded, qrows = round_up(tokens, 128), round_up(queries, 128)
    hidden = rf * devices
    aligned = devices == BLOCKS

    shards = (input_weight, square_weight, jnp.transpose(expand_weight, (0, 2, 1)), reduce_weight, head_weight,
              jnp.transpose(query_weight, (0, 2, 1)), norm_weight.T, matches)
    if aligned:
        first, second = plain_call(
            pack_kernel, [((sum(FIRST), width), BF16), ((sum(SECOND), width), BF16)], *shards)
    else:
        first, second = lax.optimization_barrier(pack(*shards))
    sine = jnp.asarray(sine_table(width, padded))
    laid = with_layout_constraint(features, Layout(major_to_minor=(0, 1, 2)))
    info = target_info(matches, target_labels, target_boxes, classes, qrows)
    expand_momentum_t = jnp.transpose(expand_momentum, (0, 2, 1))
    mom_slots = to_slots(
        square_momentum, jnp.concatenate([expand_momentum_t, reduce_momentum]), devices).astype(BF16)

    held_one, held_two = first[None], second[None]
    pairs_of_bits = groups_of(devices)
    for pair in pairs_of_bits[:-1]:
        held_one, held_two = lax.optimization_barrier((gather_round(held_one, pair, devices), held_two))
        held_one, (col, row) = lax.optimization_barrier((held_one, info))
        four = gather_four(held_two, pair, devices)
        held_two = jnp.concatenate(four) if pair != pairs_of_bits[-2] else None
    near, far = pairs_of_bits[-1]
    held_one = gather_round(held_one, pairs_of_bits[-1], devices)
    held_one, four, laid, mom_slots = lax.optimization_barrier((held_one, four, laid, mom_slots))
    mom_in = exchange(mom_slots)
    two_a, two_b = jnp.concatenate(four[:2]), jnp.concatenate(four[2:])
    other_one = swap(held_one, 1, devices)
    two_a = jnp.concatenate([two_a, swap(two_a, near, devices)])
    two_b = jnp.concatenate([two_b, swap(two_b, far, devices)])
    held_one, other_one, two_a, two_b = lax.optimization_barrier((held_one, other_one, two_a, two_b))
    far_a, far_b = swap(two_a, far, devices), swap(two_b, near, devices)
    me = lax.axis_index(AXES)
    if not aligned:
        held_one, other_one = natural_order(held_one, other_one, me, FIRST)
        me = jnp.zeros((), jnp.int32)
    me = me.reshape(1)

    inverse = 1.0 / (images * devices * queries)
    probs, keyed, lowm, q, k, v, o, s0, x1, sq_one, norm_all = encode(laid, me, held_one, other_one, sine)
    far_a, far_b, x1, mom_in = lax.optimization_barrier((far_a, far_b, x1, mom_in))
    pieces_two = [two_a, far_a, two_b, far_b]
    pieces_two = pieces_two + [swap(one, 1, devices) for one in pieces_two]
    if not aligned:
        half = two_a.shape[0] // 2
        both = []
        for a, ax, b, by in (pieces_two[:4], pieces_two[4:]):
            both.append(jnp.concatenate([
                a[:half], b[:half], a[half:], by[:half], ax[:half], b[half:], ax[half:], by[half:]]))
        both = natural_order(*both, lax.axis_index(AXES), SECOND)
        pieces_two = [jnp.stack([one[spot] for spot in spots]) for one in both for spots in PIECES]
    dx1, keep_a, send_a, keep_b, send_b, loss, box_total = middle(
        me, x1, sine, norm_all, col, row, pieces_two, tokens, queries, classes, inverse, rs)

    bits = bits_of(devices)
    near, far = bits[1], bits[2]
    turns = [(near, far), (far, near)]
    flight_a, flight_b = launch(keep_a, send_a, PART_A, devices), launch(keep_b, send_b, PART_B, devices)
    sums = ()
    for image in range(images):
        if image and turns:
            half_a, half_b = [halves(flight, bit) for flight, bit in zip((flight_a, flight_b), turns.pop(0))]
            sums, (out_a, out_b) = lax.optimization_barrier((sums, (half_a[0], half_b[0])))
            flight_a = (swap(out_a, near, devices),) + half_a[1:]
            flight_b = (swap(out_b, far, devices),) + half_b[1:]
        sums = encode_back(
            image, images, me, dx1, s0, norm_all, probs, keyed, lowm, q, k, v, o, sq_one, laid, *sums)
    sums, ready_a, ready_b = lax.optimization_barrier((sums, flight_a[:2], flight_b[:2]))
    flight_a, flight_b = (*ready_a, flight_a[2]), (*ready_b, flight_b[2])
    flight_c = launch(*sums, PART_C, devices)
    for bit_a, bit_b in turns:
        flight_a, flight_b = advance(flight_a, bit_a, devices), advance(flight_b, bit_b, devices)
    rest = [bit for bit in bits if bit not in (bits[0], near, far)]
    half_a, half_b = halves(flight_a, rest[0]), halves(flight_b, rest[0])
    out, kept = [jnp.concatenate([a, b], axis=-2) for a, b in zip(half_a[:2], half_b[:2])]
    flight = (swap(out, rest[0], devices), kept, half_a[2])
    for bit in rest[1:]:
        flight = advance(flight, bit, devices)
    for pair in reversed(pairs_of_bits):
        flight_c = send_four(parts_of_four(flight_c, *pair, devices), flight_c, *pair, devices)

    rows_ab, rows_c = sum(PART_A + PART_B) * BLOCKS // devices, sum(PART_C) * BLOCKS // devices
    slot = rf // 4
    ready, ready_c = flight[:-1], flight_c[:-1]
    shapes = [((rows_ab, width), F32, 1), ((rows_c, width), F32, 1), ((devices, slot + 8, width), BF16, 1)]
    if aligned:
        sum_ab, sum_c, grad_slots = plain_call(prepare_kernel, shapes, *ready, *ready_c, loss, near=range(len(ready) + len(ready_c)))
    else:
        sum_ab, sum_c, grad_slots = prepare(ready, ready_c, loss, devices, lambda value: lax.reduce_precision(value, 8, 7))
    grad_in = exchange(grad_slots)
    x, gram, sums = plain_call(
        gram_kernel, [((devices * slot, width), F32, 1), ((3 * width // 2, width // 2), F32, 1), ((8, width), F32, 1)],
        mom_in, grad_in, near=(1,))
    feeds = 8 * pairs
    came = [lax.ppermute(gram, AXES, [(i, i ^ bits) for i in range(feeds)]) for bits in (2, 3, 1)]
    back = exchange(plain_call(
        polish_kernel, [((devices, slot, width), BF16, 1)], x, gram, *came, near=range(5))[0])

    turn = lambda value: jnp.transpose(value, (0, 2, 1))
    states = (square_momentum, expand_momentum_t, reduce_momentum,
              input_weight, input_momentum, input_second, head_weight, head_momentum, head_second,
              turn(query_weight), turn(query_momentum), turn(query_second),
              norm_weight.T, norm_momentum.T, norm_second.T)
    weights = (square_weight, turn(expand_weight), reduce_weight)
    if aligned:
        like = lambda value, kind: (value.shape, kind)
        shapes = [like(value, F32) for value in states[:3]]
        for value in states[3::3]:
            shapes += [like(value, F32)] * 3 + [like(value, BF16)]
        new = plain_call(adapt_kernel, shapes + [((1, 1), F32)] * 2, sum_ab, sum_c, sums, *states, near=range(3))
        shapes = [like(value, kind) for value in weights for kind in (F32, BF16)]
        fresh = plain_call(apply_kernel, shapes, back, *weights, near=(0,))
    else:
        new = adapt(sum_ab, sum_c, sums, *states)
        fresh = apply(back, hidden, *weights)
    square_mom, expand_mom, reduce_mom = new[:3]
    query_out = [turn(value) for value in new[11:15]]
    norm_out = [value.T for value in new[15:19]]
    return (
        (fresh[0], square_mom, fresh[1], turn(fresh[2]), turn(expand_mom), turn(fresh[3]),
         fresh[4], reduce_mom, fresh[5]) + tuple(new[3:11]) + tuple(query_out) + tuple(norm_out)
        + (new[19].reshape(()), box_total.reshape(()), new[20].reshape(()))
    )


def row_parts(sum_ab, sum_c):
    rf = sum_c.shape[0] * PART_C[0] // sum(PART_C)
    rs = rf // 8
    cut = lambda value, start, rows: value[start:start + rows]
    half = 2 * rf + 6 * rs
    feeds = [cut(sum_ab, j * rf, rf) for j in range(2)] + [cut(sum_ab, half + j * rf, rf) for j in range(2)]
    squares = [cut(sum_c, rf + j * rs, rs) for j in range(4)]
    squares += [cut(sum_ab, 2 * rf + j * rs, rs) for j in range(6)]
    at = half + 2 * rf
    squares += [cut(sum_ab, at + j * rs, rs) for j in range(4)]
    head, norm, content, place = [cut(sum_ab, at + (4 + j) * rs, rs) for j in range(4)]
    norm = norm + cut(sum_c, rf + 4 * rs, rs)
    return feeds, squares, cut(sum_c, 0, rf), head, [content, place], norm


def prepare(parts_ab, parts_c, loss, devices, low):
    sum_ab, sum_c = [sum(value.astype(F32) for value in some) for some in (parts_ab, parts_c)]
    width = sum_ab.shape[1]
    total = sum(
        jnp.sum(jnp.sum(value * value, axis=0, keepdims=True), axis=1, keepdims=True) for value in (sum_ab, sum_c))
    spot = [lax.broadcasted_iota(jnp.int32, (8, width), axis) for axis in (0, 1)]
    numbers = jnp.zeros((8, width), F32)
    for row, value in enumerate((total, loss)):
        for lane in range(3):
            high = low(value)
            numbers = jnp.where(jnp.logical_and(spot[0] == row, spot[1] == lane), high, numbers)
            value = value - high
    feeds, squares, _, _, _, _ = row_parts(sum_ab, sum_c)
    slot = feeds[0].shape[0] // 4
    rs = squares[0].shape[0]
    none = jnp.zeros((slot - rs, width), F32)
    spare = [jnp.zeros((slot, width), F32)] * (devices - 16 - len(squares))
    slots = [feed[j * slot:(j + 1) * slot] for feed in feeds for j in range(4)]
    slots += [jnp.concatenate([square, none]) for square in squares] + spare
    slots = jnp.stack([jnp.concatenate([one, numbers]) for one in slots])
    return sum_ab, sum_c, slots.astype(BF16)


def prepare_kernel(*refs):
    *parts, loss, sum_ab, sum_c, slots = refs
    sum_ab[...], sum_c[...], slots[...] = prepare(
        [ref[...] for ref in parts[:2]], [ref[...] for ref in parts[2:]], loss[...], slots.shape[0], lambda value: value.astype(BF16).astype(F32))


def adapt(sum_ab, sum_c, sums, square_mom, expand_mom, reduce_mom, *states):
    feeds, squares, win, head, query, norm = row_parts(sum_ab, sum_c)
    lane = lax.broadcasted_iota(jnp.int32, (1, sums.shape[1]), 1)
    total, loss = [jnp.sum(jnp.where(lane < 3, sums[j:j + 1, :], 0.0), axis=1, keepdims=True) for j in range(2)]
    size = jnp.sqrt(total)
    factor = jnp.minimum(1.0, CLIP / (size + 1e-06))
    out = [BETA_M * square_mom + factor * jnp.stack(squares),
           BETA_M * expand_mom + factor * jnp.stack(feeds[:2]),
           BETA_M * reduce_mom + factor * jnp.stack(feeds[2:])]
    query = jnp.stack([one[:, :states[6].shape[2]] for one in query])
    grads = (win, head[:, :states[3].shape[1]], query, norm[:, :states[9].shape[1]])
    for j, (grad, rate, decay) in enumerate(zip(grads, (0.04, 0.1, 0.5, 0.5), (0.0001, 0.0001, 0.0, 0.0))):
        out += adam(*states[3 * j:3 * j + 3], factor * grad, rate, decay)
    return out + [loss, size]


def adapt_kernel(*refs):
    count = 18
    for ref, value in zip(refs[count:], adapt(*[ref[...] for ref in refs[:count]])):
        ref[...] = value


def apply(back, hidden, square, expand, reduce):
    slot = back.shape[1]
    rf = 4 * slot
    rs = square.shape[1]
    feed = back[:16].astype(F32).reshape(4, rf, back.shape[2])
    ortho = back[16:16 + square.shape[0]].astype(F32)[:, :rs]
    return muon(square, ortho, square.shape[2]) + muon(expand, feed[:2], hidden) + muon(reduce, feed[2:], hidden)


def apply_kernel(back, square, expand, reduce, *outs):
    hidden = back.shape[0] * expand.shape[1]
    for ref, value in zip(outs, apply(back[...], hidden, square[...], expand[...], reduce[...])):
        ref[...] = value


def solution(mesh):
    both = ("dp", "fsdp")
    first = [P(both), P(both), P(both), P(both)]
    square, expand, reduce = P(None, both), P(None, None, both), P(None, both)
    rows, query, norm = P(both), P(None, None, both), P(None, both)
    in_specs = tuple(first + [square] * 2 + [expand] * 2 + [reduce] * 2 + [rows] * 6 + [query] * 3 + [norm] * 3)
    out_specs = tuple([square] * 3 + [expand] * 3 + [reduce] * 3 + [rows] * 8 + [query] * 4 + [norm] * 4 + [P()] * 3)
    return jax.shard_map(
        functools.partial(per_device, mesh.size), mesh=mesh, in_specs=in_specs, out_specs=out_specs, check_vma=False)
```
